32 devices in a mesh: dp: 8 (over y, x, core), mp: 4 (over z).
Axes of the slice: x: 2, y: 2, z: 4, core: 2. Of those that a mesh axis runs over, the one named last changes fastest.
Arguments:
- tokens: bfloat16 [2, 12288, 768], P(None, ('dp', 'mp')), may hold values from -6 to 6
- lengths: int32 [2, 24], P(None, 'dp'), may hold values from 1 to 512, 9216 in all within a row
- cotangent: bfloat16 [2, 12288, 768], P(None, ('dp', 'mp')), may hold values from -6 to 6
- attn_in: float32 [3, 768, 768], P(None, 'dp', 'mp'), may hold values from -0.078125 to 0.078125
- attn_out: float32 [768, 768], P('mp', 'dp'), may hold values from -4 to 4
- ffn_in: float32 [2, 768, 2048], P(None, 'dp', 'mp'), may hold values from -0.21875 to 0.21875
- ffn_out: float32 [2048, 768], P('mp', 'dp'), may hold values from -0.125 to 0.125
- gains: float32 [2, 768], P(None, 'dp'), may hold values from 0.4 to 2.4
- table: float32 [32, 12], P(None, 'mp'), may hold values from -3 to 3
- attn_in_mom: float32 [3, 768, 768], P(None, 'dp', 'mp'), may hold values from -1280 to 1280
- attn_out_mom: float32 [768, 768], P('mp', 'dp'), may hold values from -28 to 28
- ffn_in_mom: float32 [2, 768, 2048], P(None, 'dp', 'mp'), may hold values from -224 to 224
- ffn_out_mom: float32 [2048, 768], P('mp', 'dp'), may hold values from -512 to 512
- gain_first: float32 [2, 768], P(None, 'dp'), may hold values from -80 to 80
- gain_second: float32 [2, 768], P(None, 'dp'), may hold values from 614 to 2457
- table_first: float32 [32, 12], P(None, 'mp'), may hold values from -160 to 160
- table_second: float32 [32, 12], P(None, 'mp'), may hold values from 3072 to 12288
Outputs:
- output: bfloat16 [2, 12288, 768], P(None, ('dp', 'mp'))
- tokens_grad: float32 [2, 12288, 768], P(None, ('dp', 'mp'))
- attn_in_next: float32 [3, 768, 768], P(None, 'dp', 'mp')
- attn_out_next: float32 [768, 768], P('mp', 'dp')
- ffn_in_next: float32 [2, 768, 2048], P(None, 'dp', 'mp')
- ffn_out_next: float32 [2048, 768], P('mp', 'dp')
- attn_in_mom_next: float32 [3, 768, 768], P(None, 'dp', 'mp')
- attn_out_mom_next: float32 [768, 768], P('mp', 'dp')
- ffn_in_mom_next: float32 [2, 768, 2048], P(None, 'dp', 'mp')
- ffn_out_mom_next: float32 [2048, 768], P('mp', 'dp')
- gain_first_next: float32 [2, 768], P(None, 'dp')
- gain_second_next: float32 [2, 768], P(None, 'dp')
- gains_next: float32 [2, 768], P(None, 'dp')
- table_first_next: float32 [32, 12], P(None, 'mp')
- table_second_next: float32 [32, 12], P(None, 'mp')
- table_next: float32 [32, 12], P(None, 'mp')
The draws below stay inside these ranges and needn't reach their ends.
Inputs may be any that keep to these rules, and one draw needn't show every extreme that they name: In each micro-batch the lengths sum to 3/4 of the 12288 positions and some document has all 512.
All inputs are finite; a program needn't handle non-finite values. No bound on the sum of `lengths` on one device may be relied on, other than what follows from the above.
Results may differ from the reference program's by a relative error of at most 0.02.
Values may be sent and summed in bfloat16 or wider, within the bound.
No kernel may reach another device: no remote copies, remote signals or barrier semaphores. Data moves between devices by JAX's collectives and lax.ppermute only.
A program may use at most 192 MiB of HBM per device.

```python
import math
import jax
import jax.numpy as jnp
import numpy as np
from jax import lax

D = 768
H = 12
DH = 64
FF = 2048
BUCKETS = 32
LEN = 512
MB = 2
NS = 2
STEP = 8
NSEQ = 24
TOK_MB = 12288
N_MP = 4


def draw_gains(key, part):
    key = jax.random.fold_in(key, 7)
    ramp = 0.6 + 1.2 * jnp.arange(D, dtype=jnp.float32) / D
    factor = jnp.clip(1.0 + 0.1 * jax.random.normal(key, (2, D), jnp.float32), 0.7, 1.3)
    return ramp[None, :] * factor


def level_of(stream_key, shape, pieces, smallest, high):
    loudness = 1.0
    for dim, shards_of in pieces:
        steps = jax.random.uniform(jax.random.fold_in(jax.random.fold_in(stream_key, 6), dim), (shards_of,), jnp.float32, smallest / len(pieces), high / len(pieces))
        loudness = loudness * jnp.repeat(jnp.exp(steps), shape[dim] // shards_of).reshape((-1,) + (1,) * (len(shape) - 1 - dim))
    return loudness


def split_up(amount, total, most, slope):
    weights = [(1 << 20) // math.isqrt(rank ** slope) + 1 for rank in range(2, amount + 1)]
    rest, given = total - most - (amount - 1), [1] * (amount - 1)
    while rest > 0:
        candidates = [i for i in range(amount - 1) if given[i] < most]
        pool, budget = sum([weights[i] for i in candidates]), rest
        for i in candidates:
            more = min(most - given[i], max(1, budget * weights[i] // pool), rest)
            given[i] = given[i] + more
            rest = rest - more
    return np.array([most] + given)


def uneven_parts(rng, count, total, bound, slope):
    if count == 2:
        one = jax.random.randint(rng, (), max(1, total - bound), min(bound, total - 1) + 1)
        return jnp.stack([one, total - one])
    sizes = jnp.asarray(split_up(count, total, bound, slope), jnp.int32)
    twos = (count - 1) // 2
    source_of, sink = sizes[1:1 + 2 * twos:2], sizes[2:2 + 2 * twos:2]
    room = jnp.minimum(source_of - 1, bound - sink)
    shifted = jax.random.randint(jax.random.fold_in(rng, 1), (twos,), 0, 1 << 20) % (room + 1)
    sizes = sizes.at[1:1 + 2 * twos:2].set(source_of - shifted).at[2:2 + 2 * twos:2].set(sink + shifted)
    return sizes[jax.random.permutation(jax.random.fold_in(rng, 2), count)]


def gaussian(key, dims, scale, reach, cuts=(), kind=jnp.bfloat16):
    values = jax.random.normal(key, dims, jnp.float32) * scale
    if len(cuts) > 0:
        values = level_of(key, dims, cuts, -0.22, 0.18) * values
    return jnp.clip(values, min=-reach, max=reach).astype(kind)


def setup_inputs(seed: int = 0) -> dict:
    key_list = jax.random.split(jax.random.key(seed), 18)
    tokens = gaussian(key_list[0], (MB, TOK_MB, D), 1.0, 6.0, ((1, 32),))
    lengths = jax.vmap(lambda own: uneven_parts(own, NSEQ, NSEQ * LEN * 3 // 4, LEN, 2))(jax.random.split(key_list[1], MB)).reshape((MB, NSEQ)).astype(jnp.int32)
    cotangent = gaussian(key_list[2], (MB, TOK_MB, D), 1.0, 6.0, ((1, 32),))
    attn_in = gaussian(key_list[3], (3, D, H * DH), (D * 8) ** -0.5, 0.078125, ((1, 8), (2, 4)), jnp.float32)
    attn_out = gaussian(key_list[4], (H * DH, D), 0.7, 4.0, ((0, 4), (1, 8)), jnp.float32)
    ffn_in = gaussian(key_list[5], (2, D, FF), D ** -0.5, 0.21875, ((1, 8), (2, 4)), jnp.float32)
    ffn_out = gaussian(key_list[6], (FF, D), FF ** -0.5, 0.125, ((0, 4), (1, 8)), jnp.float32)
    gains = draw_gains(jax.random.fold_in(key_list[17], 71), 0)
    table = gaussian(key_list[8], (BUCKETS, H), 0.5, 3.0, ((1, 4),), jnp.float32)
    attn_in_mom = gaussian(key_list[9], (3, D, H * DH), (1.5 * (MB * TOK_MB) ** 0.5), 1280.0, ((1, 8), (2, 4)), jnp.float32)
    attn_out_mom = gaussian(key_list[10], (H * DH, D), (0.03 * (MB * TOK_MB) ** 0.5), 28.0, ((0, 4), (1, 8)), jnp.float32)
    ffn_in_mom = gaussian(key_list[11], (2, D, FF), (0.25 * (MB * TOK_MB) ** 0.5), 224.0, ((1, 8), (2, 4)), jnp.float32)
    ffn_out_mom = gaussian(key_list[12], (FF, D), (0.6 * (MB * TOK_MB) ** 0.5), 512.0, ((0, 4), (1, 8)), jnp.float32)
    gain_first = gaussian(key_list[13], (2, D), (0.08 * (MB * TOK_MB) ** 0.5), 80.0, ((1, 8),), jnp.float32)
    gain_second = jnp.clip(jnp.exp(math.log(2457.0) - 1.38670144 * jax.random.uniform(key_list[14], (2, D), jnp.float32) ** level_of(key_list[14], (2, D), ((1, 8),), -0.2, 0.2)), 614.0, 2457.0)
    table_first = gaussian(key_list[15], (BUCKETS, H), (0.18 * (MB * TOK_MB) ** 0.5), 160.0, ((1, 4),), jnp.float32)
    table_second = jnp.clip(jnp.exp(math.log(12288.0) - 1.3862944 * jax.random.uniform(key_list[16], (BUCKETS, H), jnp.float32) ** level_of(key_list[16], (BUCKETS, H), ((1, 4),), -0.2, 0.2)), 3072.0, 12288.0)
    return {"tokens": tokens, "lengths": lengths, "cotangent": cotangent, "attn_in": attn_in, "attn_out": attn_out, "ffn_in": ffn_in, "ffn_out": ffn_out, "gains": gains, "table": table, "attn_in_mom": attn_in_mom, "attn_out_mom": attn_out_mom, "ffn_in_mom": ffn_in_mom, "ffn_out_mom": ffn_out_mom, "gain_first": gain_first, "gain_second": gain_second, "table_first": table_first, "table_second": table_second}


highest_precision = lax.Precision.HIGHEST
epsilon = 1e-06
negative_fill = -1e+30
momentum_decay = 0.95
decay_rate = 0.01
linear_coefficient = 3.4445
coef_second = -4.775
coef_third = 2.0315
rate_attn_in = 0.25
rate_attn_out = 12.0
rate_ffn_in = 0.6
rate_ffn_out = 0.3
beta_one = 0.9
beta_two = 0.95
adam_epsilon = 1e-08
adam_rate = 0.3
bucket_marks = (12, 16, 23, 32, 46, 64, 91)

@jax.custom_vjp
def low(v):
    return lax.optimization_barrier(v.astype(jnp.bfloat16)).astype(jnp.float32)

@jax.custom_vjp
def low_back(v):
    return v

def low_keep(v):
    return (low(v), None)

def low_pass(kept, grad):
    return (grad,)

def back_keep(v):
    return (v, None)

def back_low(kept, grad):
    return (low(grad),)
low.defvjp(low_keep, low_pass)
low_back.defvjp(back_keep, back_low)

def bucket_table(length):
    position = jnp.arange(length, dtype=jnp.int32)
    relative = position[None, :] - position[:, None]
    distance = jnp.abs(relative)
    marks = jnp.array(bucket_marks, dtype=jnp.int32)
    far_bucket = 8 + lax.optimization_barrier(jnp.sum((distance[:, :, None] >= marks[None, None, :]).astype(jnp.int32), axis=2))
    near_far = jnp.where(distance < 8, distance, far_bucket)
    return near_far + 16 * (relative > 0).astype(jnp.int32)

def norm_rows(rows, gain):
    return rows * lax.rsqrt(lax.optimization_barrier(jnp.mean(rows * rows, axis=-1, keepdims=True)) + epsilon) * gain

def forward(tokens_f, lengths, attn_in, attn_out, ffn_in, ffn_out, gains, table):
    attention_weight = low(attn_in)
    w_out = low(attn_out)
    w_fin = low(ffn_in)
    w_fout = low(ffn_out)
    gain_low = low(gains)
    bias_all = jnp.transpose(table[bucket_table(LEN)], (2, 0, 1))
    seq_count = lengths.shape[0] * lengths.shape[1]
    group = math.gcd(seq_count, 4)
    blocks_rows = tokens_f.reshape(seq_count // group, group, LEN, D)
    blocks_lens = lengths.reshape(seq_count // group, group)

    def one_group(block_rows, block_lens):
        flat = block_rows.reshape(group * LEN, D)
        normed_one = low(norm_rows(flat, gain_low[0]))
        projected = jnp.einsum('td,cdf->ctf', normed_one, attention_weight, precision=highest_precision)
        projected = low(low_back(projected)).reshape(3, group, LEN, H, DH)
        scores = jnp.einsum('gihd,gjhd->ghij', projected[0], projected[1], precision=highest_precision) + bias_all[None]
        scores = low_back(scores)
        valid = jnp.arange(LEN, dtype=jnp.int32)[None, :] < block_lens[:, None]
        scores = jnp.where(valid[:, None, None, :], scores, negative_fill)
        weights_soft = jax.nn.softmax(scores, axis=-1)
        attended = jnp.einsum('ghij,gjhd->gihd', low(weights_soft), projected[2], precision=highest_precision)
        attended = low(low_back(attended.reshape(group * LEN, H * DH)))
        branch_one = low_back(jnp.dot(attended, w_out, precision=highest_precision))
        middle = flat + branch_one
        normed_two = low(norm_rows(middle, gain_low[1]))
        gate_up = low_back(jnp.einsum('td,cdf->ctf', normed_two, w_fin, precision=highest_precision))
        hidden = low(jax.nn.gelu(gate_up[0], approximate=True) * gate_up[1])
        branch_two = low_back(jnp.dot(hidden, w_fout, precision=highest_precision))
        return (middle + branch_two).reshape(group, LEN, D)

    def scan_step(carry, inputs):
        return (carry, jax.checkpoint(one_group)(inputs[0], inputs[1]))
    _, results = lax.scan(scan_step, jnp.zeros((), jnp.float32), (blocks_rows, blocks_lens))
    return results.reshape(tokens_f.shape)

def blocks_from_cols(weight):
    count, rows_d, width = weight.shape
    split = weight.reshape(count, rows_d, N_MP, width // N_MP)
    return jnp.transpose(split, (0, 2, 1, 3)).reshape(count * N_MP, rows_d, width // N_MP)

def cols_from_blocks(weight_blocks, count):
    rows_d, width = (weight_blocks.shape[1], weight_blocks.shape[2])
    split = weight_blocks.reshape(count, N_MP, rows_d, width)
    return jnp.transpose(split, (0, 2, 1, 3)).reshape(count, rows_d, N_MP * width)

def blocks_from_rows(weight):
    width, rows_d = weight.shape
    return jnp.transpose(weight.reshape(N_MP, width // N_MP, rows_d), (0, 2, 1))

def rows_from_blocks(weight_blocks):
    return jnp.transpose(weight_blocks, (0, 2, 1)).reshape(-1, weight_blocks.shape[1])

def orthogonalize(weight_blocks):
    total = lax.optimization_barrier(jnp.sum(weight_blocks * weight_blocks, axis=(1, 2), keepdims=True))
    newton_iterate = weight_blocks * lax.rsqrt(total)
    for ns_round in range(NS):
        gram_product = jnp.einsum('ouq,ouw->oqw', newton_iterate, newton_iterate, precision=highest_precision)
        polynomial_term = coef_second * gram_product + coef_third * jnp.einsum('bij,bjk->bik', gram_product, gram_product, precision=highest_precision)
        newton_iterate = linear_coefficient * newton_iterate + jnp.einsum('rol,rlv->rov', newton_iterate, polynomial_term, precision=highest_precision)
    return newton_iterate

def adam_update(param, grad, first, second):
    first_new = beta_one * first + (1.0 - beta_one) * grad
    second_new = beta_two * second + (1.0 - beta_two) * grad * grad
    corrected_first = first_new / (1.0 - beta_one ** STEP)
    corrected_second = second_new / (1.0 - beta_two ** STEP)
    return (first_new, second_new, param - adam_rate * corrected_first / (jnp.sqrt(corrected_second) + adam_epsilon))

def reference(tokens, lengths, cotangent, attn_in, attn_out, ffn_in, ffn_out, gains, table, attn_in_mom, attn_out_mom, ffn_in_mom, ffn_out_mom, gain_first, gain_second, table_first, table_second):

    def closed(tokens_f, a_in, a_out, f_in, f_out, gain_vals, table_vals):
        return forward(tokens_f, lengths, a_in, a_out, f_in, f_out, gain_vals, table_vals)
    result, pull = jax.vjp(closed, tokens.astype(jnp.float32), attn_in, attn_out, ffn_in, ffn_out, gains, table)
    grads = pull(cotangent.astype(jnp.float32))
    mom_in = momentum_decay * attn_in_mom + grads[1]
    mom_out = momentum_decay * attn_out_mom + grads[2]
    mom_fin = momentum_decay * ffn_in_mom + grads[3]
    mom_fout = momentum_decay * ffn_out_mom + grads[4]
    orth_in = cols_from_blocks(orthogonalize(blocks_from_cols(mom_in)), 3)
    orth_out = rows_from_blocks(orthogonalize(blocks_from_rows(mom_out)))
    orth_fin = cols_from_blocks(orthogonalize(blocks_from_cols(mom_fin)), 2)
    orth_fout = rows_from_blocks(orthogonalize(blocks_from_rows(mom_fout)))
    attn_in_next = attn_in * (1.0 - rate_attn_in * decay_rate) - rate_attn_in * orth_in
    attn_out_next = attn_out * (1.0 - rate_attn_out * decay_rate) - rate_attn_out * orth_out
    ffn_in_next = ffn_in * (1.0 - rate_ffn_in * decay_rate) - rate_ffn_in * orth_fin
    ffn_out_next = ffn_out * (1.0 - rate_ffn_out * decay_rate) - rate_ffn_out * orth_fout
    gain_first_next, gain_second_next, gains_next = adam_update(gains, grads[5], gain_first, gain_second)
    table_first_next, table_second_next, table_next = adam_update(table, grads[6], table_first, table_second)
    return (result.astype(jnp.bfloat16), grads[0], attn_in_next, attn_out_next, ffn_in_next, ffn_out_next, mom_in, mom_out, mom_fin, mom_fout, gain_first_next, gain_second_next, gains_next, table_first_next, table_second_next, table_next)
```

```python
import functools

import jax
import jax.numpy as jnp
import numpy as np
from jax import lax
from jax.experimental import pallas as pl
from jax.experimental.pallas import tpu as pltpu
from jax.sharding import PartitionSpec as P

D = 768
H = 12
DH = 64
BUCKETS = 32
LEN = 512
STEP = 8
QB = 128
SKEW = 1024
PAIRS = H // 2

epsilon = 1e-06
negative_fill = -1e30
momentum_decay = 0.95
decay_rate = 0.01
linear_coefficient = 3.4445
coef_second = -4.775
coef_third = 2.0315
rate_attn_in = 0.25
rate_attn_out = 12.0
rate_ffn_in = 0.6
rate_ffn_out = 0.3
beta_one = 0.9
beta_two = 0.95
adam_epsilon = 1e-08
adam_rate = 0.3
bucket_marks = (12, 16, 23, 32, 46, 64, 91)

HIGHEST = lax.Precision.HIGHEST
HIGH = lax.Precision.HIGH
bf16 = jnp.bfloat16
f32 = jnp.float32
NN = (((1,), (0,)), ((), ()))
NT = (((1,), (1,)), ((), ()))
TN = (((0,), (0,)), ((), ()))


def dot(a, b, dims=NN):
    return lax.dot_general(a, b, dims, preferred_element_type=f32)


def skew_onehot():
    place = np.arange(SKEW)
    relative = np.where(place < SKEW - QB + 1, place, place - SKEW) - (LEN - QB)
    distance = np.abs(relative)
    far = 8 + sum((distance >= mark).astype(np.int32) for mark in bucket_marks)
    bucket = np.where(distance < 8, distance, far) + 16 * (relative > 0)
    return (bucket[:, None] == np.arange(BUCKETS)[None, :]).astype(np.float32)


def half_lanes(shape, half):
    lane = lax.broadcasted_iota(jnp.int32, shape, 1)
    return (lane < DH) if half == 0 else (lane >= DH)


def make_bias(line_ref, bias_ref):
    for half in range(2):
        line = jnp.broadcast_to(line_ref[0, half : half + 1, :], (QB, SKEW))
        bias_ref[half] = pltpu.roll(line, 0, 1, stride=1, stride_axis=0).T


def both_heads(block):
    zero = jnp.zeros_like(block)
    return jnp.concatenate(
        [
            jnp.where(half_lanes(block.shape, 0), block, zero),
            jnp.where(half_lanes(block.shape, 1), block, zero),
        ],
        axis=0,
    )


def exp_scores(meta, block, mb, keys, queries_two, bias_ref):
    start = pl.multiple_of((LEN - QB) - QB * meta[3 + block], QB)
    length = meta[6 + 2 * mb + meta[block]]
    bias = jnp.concatenate([bias_ref[0, pl.ds(start, LEN), :], bias_ref[1, pl.ds(start, LEN), :]], axis=1)
    scores = dot(keys, queries_two, NT) + bias
    row = lax.broadcasted_iota(jnp.int32, scores.shape, 0)
    scores = jnp.where(row < length, scores, negative_fill)
    top = jnp.max(scores, axis=0, keepdims=True)
    weights = jnp.exp(scores - top)
    return weights, jnp.sum(weights, axis=0, keepdims=True)


def attend_kernel(meta, q_ref, k_ref, v_ref, line_ref, o_ref, bias_ref):
    mb = pl.program_id(1)

    @pl.when(mb == 0)
    def _():
        make_bias(line_ref, bias_ref)

    for block in range(3):
        rows = pl.ds(pl.multiple_of(meta[block] * LEN, LEN), LEN)
        keys, values = k_ref[0, rows, :], v_ref[0, rows, :]
        queries_two = both_heads(q_ref[0, block * QB : (block + 1) * QB, :])
        weights, total = exp_scores(meta, block, mb, keys, queries_two, bias_ref)
        out_two = dot(values.T, weights.astype(bf16)) / total
        top = lax.broadcasted_iota(jnp.int32, (QB, QB), 0) < DH
        out = jnp.where(top, out_two[:, :QB], out_two[:, QB:])
        o_ref[0, block * QB : (block + 1) * QB, :] = out.T.astype(bf16)


def attend_back_kernel(
    meta, q_ref, k_ref, v_ref, do_ref, line_ref, dq_ref, dk_ref, dv_ref, diag_ref,
    bias_ref, acc_ref, dk_acc, dv_acc,
):
    mb = pl.program_id(1)

    @pl.when(mb == 0)
    def _():
        make_bias(line_ref, bias_ref)
        acc_ref[...] = jnp.zeros_like(acc_ref)

    dk_acc[...] = jnp.zeros_like(dk_acc)
    dv_acc[...] = jnp.zeros_like(dv_acc)
    for block in range(3):
        rows = pl.ds(pl.multiple_of(meta[block] * LEN, LEN), LEN)
        own = slice(block * QB, (block + 1) * QB)
        keys, values = k_ref[0, rows, :], v_ref[0, rows, :]
        queries_two = both_heads(q_ref[0, own, :])
        grad_two = both_heads(do_ref[0, own, :])
        weights, total = exp_scores(meta, block, mb, keys, queries_two, bias_ref)
        soft = weights * (1.0 / total)
        grad_soft = dot(values, grad_two, NT)
        inner = jnp.sum(grad_soft * soft, axis=0, keepdims=True)
        grad_scores = soft * (grad_soft - inner)
        start = pl.multiple_of((LEN - QB) - QB * meta[3 + block], QB)
        acc_ref[0, pl.ds(start, LEN), :] += grad_scores[:, :QB]
        acc_ref[1, pl.ds(start, LEN), :] += grad_scores[:, QB:]
        grad_low = grad_scores.astype(bf16)
        dk_acc[rows, :] += dot(grad_low, queries_two)
        dv_acc[rows, :] += dot(soft.astype(bf16), grad_two)
        dq_two = dot(keys.T, grad_low)
        top = lax.broadcasted_iota(jnp.int32, (QB, QB), 0) < DH
        dq_ref[0, own, :] = jnp.where(top, dq_two[:, :QB], dq_two[:, QB:]).T.astype(bf16)
    dk_ref[0] = dk_acc[...].astype(bf16)
    dv_ref[0] = dv_acc[...].astype(bf16)

    @pl.when(mb == pl.num_programs(1) - 1)
    def _():
        row = lax.broadcasted_iota(jnp.int32, (QB, QB), 0)
        lane = lax.broadcasted_iota(jnp.int32, (QB, QB), 1)
        flip = (row + lane == QB - 1).astype(f32)
        for half in range(2):
            turned = lax.dot_general(flip, acc_ref[half], NT, precision=HIGHEST, preferred_element_type=f32)
            shifted = pltpu.roll(turned, SKEW - QB + 1, 1, stride=1, stride_axis=0)
            diag_ref[0, half : half + 1, :] = jnp.sum(shifted, axis=0, keepdims=True)


def attend(meta, q, k, v, line):
    micro, rows, _ = q.shape
    window = k.shape[1]
    own = pl.BlockSpec((1, rows, QB), lambda p, m, _: (m, 0, p))
    wide = pl.BlockSpec((1, window, QB), lambda p, m, _: (m, 0, p))
    lines = pl.BlockSpec((1, 2, SKEW), lambda p, m, _: (p, 0, 0))
    return pl.pallas_call(
        attend_kernel,
        grid_spec=pltpu.PrefetchScalarGridSpec(
            num_scalar_prefetch=1,
            grid=(PAIRS, micro),
            in_specs=[own, wide, wide, lines],
            out_specs=own,
            scratch_shapes=[pltpu.VMEM((2, SKEW, QB), f32)],
        ),
        out_shape=jax.ShapeDtypeStruct(q.shape, bf16),
        compiler_params=pltpu.CompilerParams(vmem_limit_bytes=40 << 20),
        name="attend",
    )(meta, q, k, v, line)


def attend_back(meta, q, k, v, grad, line):
    micro, rows, _ = q.shape
    window = k.shape[1]
    own = pl.BlockSpec((1, rows, QB), lambda p, m, _: (m, 0, p))
    wide = pl.BlockSpec((1, window, QB), lambda p, m, _: (m, 0, p))
    lines = pl.BlockSpec((1, 2, SKEW), lambda p, m, _: (p, 0, 0))
    return pl.pallas_call(
        attend_back_kernel,
        grid_spec=pltpu.PrefetchScalarGridSpec(
            num_scalar_prefetch=1,
            grid=(PAIRS, micro),
            in_specs=[own, wide, wide, own, lines],
            out_specs=[own, wide, wide, lines],
            scratch_shapes=[
                pltpu.VMEM((2, SKEW, QB), f32),
                pltpu.VMEM((2, SKEW, QB), f32),
                pltpu.VMEM((window, QB), f32),
                pltpu.VMEM((window, QB), f32),
            ],
        ),
        out_shape=[
            jax.ShapeDtypeStruct(q.shape, bf16),
            jax.ShapeDtypeStruct(k.shape, bf16),
            jax.ShapeDtypeStruct(k.shape, bf16),
            jax.ShapeDtypeStruct(line.shape, f32),
        ],
        compiler_params=pltpu.CompilerParams(vmem_limit_bytes=40 << 20),
        name="attend_back",
    )(meta, q, k, v, grad, line)


ROWS = 256


def gelu_and_slope(gate):
    root = 0.7978845608028654
    cube = 0.044715
    square = gate * gate
    bend = jnp.tanh(root * gate * (1.0 + cube * square))
    half = 0.5 * (1.0 + bend)
    slope = half + 0.5 * gate * (1.0 - bend * bend) * (root * (1.0 + 3.0 * cube * square))
    return gate * half, slope


def ffn_kernel(
    y_ref, dy_ref, gain_ref, w_ref, out_ref, dy1_ref, dh1_ref, dgain_ref, grad_ref,
    n_ref, nt_ref, dyt_ref, acc_ref, dn_ref, hid_ref, dgate_ref, dup_ref,
):
    step = pl.program_id(0)
    tokens = y_ref.shape[0]
    width = w_ref.shape[2] // 3
    gate_cols, up_cols, down_cols = (slice(c * width, (c + 1) * width) for c in range(3))

    @pl.when(step == 0)
    def _():
        y = y_ref[...]
        rho = lax.rsqrt(jnp.mean(y * y, axis=-1, keepdims=True) + epsilon)
        normed = (y * rho * gain_ref[...]).astype(bf16)
        n_ref[...] = normed
        nt_ref[...] = normed.T
        dyt_ref[...] = dy_ref[...].T
        acc_ref[...] = y
        dn_ref[...] = jnp.zeros_like(dn_ref)

    def tile(t, _):
        rows = pl.ds(pl.multiple_of(t * ROWS, ROWS), ROWS)
        normed = n_ref[rows, :]
        gate = dot(normed, w_ref[0, :, gate_cols])
        up = dot(normed, w_ref[0, :, up_cols])
        grad_hid = dot(dy_ref[rows, :], w_ref[0, :, down_cols])
        act, slope = gelu_and_slope(gate)
        hid = (act * up).astype(bf16)
        dgate = (grad_hid * up * slope).astype(bf16)
        dup = (grad_hid * act).astype(bf16)
        hid_ref[rows, :] = hid
        dgate_ref[rows, :] = dgate
        dup_ref[rows, :] = dup
        acc_ref[rows, :] += dot(hid, w_ref[0, :, down_cols], NT)
        dn_ref[rows, :] += dot(dgate, w_ref[0, :, gate_cols], NT) + dot(dup, w_ref[0, :, up_cols], NT)
        return 0

    lax.fori_loop(0, tokens // ROWS, tile, 0)

    def grads(t, _):
        rows = pl.ds(pl.multiple_of(t * ROWS, ROWS), ROWS)
        grad_ref[0, rows, gate_cols] = dot(nt_ref[rows, :], dgate_ref[...]).astype(bf16)
        grad_ref[0, rows, up_cols] = dot(nt_ref[rows, :], dup_ref[...]).astype(bf16)
        grad_ref[0, rows, down_cols] = dot(dyt_ref[rows, :], hid_ref[...]).astype(bf16)
        return 0

    lax.fori_loop(0, D // ROWS, grads, 0)

    @pl.when(step == pl.num_programs(0) - 1)
    def _():
        out_ref[...] = acc_ref[...].astype(bf16)
        y = y_ref[...]
        rho = lax.rsqrt(jnp.mean(y * y, axis=-1, keepdims=True) + epsilon)
        scaled_y = y * rho
        dn = dn_ref[...]
        dgain_ref[...] = jnp.sum(dn * scaled_y, axis=0, keepdims=True)
        u = dn * gain_ref[...]
        inner = jnp.mean(u * scaled_y, axis=-1, keepdims=True)
        dy1 = dy_ref[...].astype(f32) + rho * (u - scaled_y * inner)
        dy1_ref[...] = dy1
        dh1_ref[...] = dy1.astype(bf16)


def ffn(y, dy, gain, weights):
    tokens = y.shape[0]
    groups, _, columns = weights.shape
    width = columns // 3
    whole = pl.BlockSpec((tokens, D), lambda m: (0, 0))
    one = pl.BlockSpec((1, D), lambda m: (0, 0))
    group = pl.BlockSpec((1, D, columns), lambda m: (m, 0, 0))
    return pl.pallas_call(
        ffn_kernel,
        grid=(groups,),
        in_specs=[whole, whole, one, group],
        out_specs=[whole, whole, whole, one, group],
        out_shape=[
            jax.ShapeDtypeStruct((tokens, D), bf16),
            jax.ShapeDtypeStruct((tokens, D), f32),
            jax.ShapeDtypeStruct((tokens, D), bf16),
            jax.ShapeDtypeStruct((1, D), f32),
            jax.ShapeDtypeStruct(weights.shape, bf16),
        ],
        scratch_shapes=[
            pltpu.VMEM((tokens, D), bf16),
            pltpu.VMEM((D, tokens), bf16),
            pltpu.VMEM((D, tokens), bf16),
            pltpu.VMEM((tokens, D), f32),
            pltpu.VMEM((tokens, D), f32),
            pltpu.VMEM((tokens, width), bf16),
            pltpu.VMEM((tokens, width), bf16),
            pltpu.VMEM((tokens, width), bf16),
        ],
        compiler_params=pltpu.CompilerParams(vmem_limit_bytes=52 << 20),
        name="ffn",
    )(y, dy, gain, weights)


def grams_of(blocks):
    return jnp.einsum("our,ouw->orw", blocks, blocks, precision=HIGHEST)


def orthogonal(blocks, gram):
    total = jnp.trace(gram, axis1=1, axis2=2)[:, None, None]
    mul = functools.partial(jnp.einsum, "oij,ojk->oik", precision=HIGH)
    first = gram / total
    start = blocks * lax.rsqrt(total)
    eye = jnp.eye(gram.shape[1], dtype=f32)[None]
    step = linear_coefficient * eye + coef_second * first + coef_third * mul(first, first)
    second = mul(mul(first, step), step)
    once = mul(start, step)
    turn = mul(once, second)
    return linear_coefficient * once + coef_second * turn + coef_third * mul(turn, second)


def adam_update(param, grad, first, second):
    first_new = beta_one * first + (1.0 - beta_one) * grad
    second_new = beta_two * second + (1.0 - beta_two) * grad * grad
    corrected_first = first_new / (1.0 - beta_one**STEP)
    corrected_second = second_new / (1.0 - beta_two**STEP)
    return (
        first_new,
        second_new,
        param - adam_rate * corrected_first / (jnp.sqrt(corrected_second) + adam_epsilon),
    )


def gather_blocks(shard):
    n_dp, n_mp = lax.axis_size("dp"), lax.axis_size("mp")
    rows, columns = shard.shape
    whole = lax.all_gather(shard, ("dp", "mp"), axis=0, tiled=False)
    return whole.reshape(n_dp, n_mp, rows, columns).transpose(1, 0, 2, 3).reshape(n_mp, n_dp * rows, columns)


def scatter_blocks(grads):
    n_dp, n_mp = lax.axis_size("dp"), lax.axis_size("mp")
    _, all_rows, columns = grads.shape
    rows = all_rows // n_dp
    parts = grads.reshape(n_mp, n_dp, rows, columns).transpose(1, 0, 2, 3).reshape(n_dp * n_mp * rows, columns)
    return lax.psum_scatter(parts, ("dp", "mp"), scatter_dimension=0, tiled=True).astype(f32)


def shards(
    tokens, lengths, cotangent, attn_in, attn_out, ffn_in, ffn_out, gains, table,
    attn_in_mom, attn_out_mom, ffn_in_mom, ffn_out_mom,
    gain_first, gain_second, table_first, table_second,
):
    micro, own_rows, _ = tokens.shape
    here = lax.axis_index("mp")
    n_mp = lax.axis_size("mp")
    width = attn_in.shape[2]
    heads_dev = table.shape[1]

    attn_low = jnp.concatenate([attn_in[0], attn_in[1], attn_in[2], attn_out.T], axis=1).astype(bf16)
    ffn_low = jnp.concatenate([ffn_in[0], ffn_in[1], ffn_out.T], axis=1).astype(bf16)
    gain_low = lax.all_gather(gains.astype(bf16), "dp", axis=1, tiled=True).astype(f32)
    table_all = lax.all_gather(table, "mp", axis=1, tiled=True)
    attn_all = gather_blocks(attn_low)
    ffn_all = gather_blocks(ffn_low)
    w_q, w_k, w_v, w_o = (
        attn_all.reshape(n_mp, D, 4, width).transpose(2, 1, 0, 3).reshape(4, D, n_mp * width)
    )

    onehot = skew_onehot()
    line = lax.dot_general(
        table_all, onehot, (((0,), (1,)), ((), ())), precision=HIGHEST, preferred_element_type=f32
    ).reshape(PAIRS, 2, SKEW)

    first_row = own_rows * here
    first_doc = first_row // LEN
    inset = first_row - first_doc * LEN
    before = lax.ppermute(tokens, "mp", [(j, j + 1) for j in range(n_mp - 1)])
    after = lax.ppermute(tokens, "mp", [(j + 1, j) for j in range(n_mp - 1)])
    side = jnp.concatenate([before, tokens, after, jnp.zeros((micro, 2 * LEN - own_rows - own_rows + QB, D), bf16)], axis=1)
    window = lax.dynamic_slice_in_dim(side, own_rows - inset, 2 * LEN, axis=1)
    block_place = first_row // QB + jnp.arange(own_rows // QB, dtype=jnp.int32)
    slot = block_place // (LEN // QB) - first_doc
    lens_window = lax.dynamic_slice_in_dim(
        jnp.concatenate([lengths, jnp.ones((micro, 1), lengths.dtype)], axis=1), first_doc, 2, axis=1
    )
    meta = jnp.concatenate([slot, block_place % (LEN // QB), lens_window.reshape(-1)]).astype(jnp.int32)

    def unit(rows):
        return rows * lax.rsqrt(jnp.mean(rows * rows, axis=-1, keepdims=True) + epsilon)

    rows = tokens.reshape(micro * own_rows, D).astype(f32)
    normed_own = (unit(rows) * gain_low[0]).astype(bf16)
    window_rows = window.reshape(micro * 2 * LEN, D).astype(f32)
    normed_window = (unit(window_rows) * gain_low[0]).astype(bf16)
    q = dot(normed_own, w_q).astype(bf16).reshape(micro, own_rows, D)
    k = dot(normed_window, w_k).astype(bf16).reshape(micro, 2 * LEN, D)
    v = dot(normed_window, w_v).astype(bf16).reshape(micro, 2 * LEN, D)
    attended = attend(meta, q, k, v, line).reshape(micro * own_rows, D)
    middle = rows + dot(attended, w_o, NT)

    dy = cotangent.reshape(micro * own_rows, D)
    output, grad_middle, grad_mid_low, grad_gain_two, grad_ffn = ffn(middle, dy, gain_low[1:2], ffn_all)
    shard_ffn = scatter_blocks(grad_ffn)

    grad_w_o = dot(grad_mid_low, attended, TN)
    grad_att = dot(grad_mid_low, w_o).astype(bf16).reshape(micro, own_rows, D)
    grad_q, grad_k, grad_v, diag = attend_back(meta, q, k, v, grad_att, line)
    grad_q = grad_q.reshape(micro * own_rows, D)
    grad_k = grad_k.reshape(micro * 2 * LEN, D)
    grad_v = grad_v.reshape(micro * 2 * LEN, D)
    grad_w_q = dot(normed_own, grad_q, TN)
    grad_w_k = dot(normed_window, grad_k, TN)
    grad_w_v = dot(normed_window, grad_v, TN)
    grad_attn = (
        jnp.stack([grad_w_q, grad_w_k, grad_w_v, grad_w_o])
        .astype(bf16)
        .reshape(4, D, n_mp, width)
        .transpose(2, 1, 0, 3)
        .reshape(n_mp, D, 4 * width)
    )
    shard_attn = scatter_blocks(grad_attn)

    grad_normed_own = dot(grad_q, w_q, NT)
    grad_normed_window = (dot(grad_k, w_k, NT) + dot(grad_v, w_v, NT)).reshape(micro, 2 * LEN, D)
    grad_side = lax.dynamic_update_slice_in_dim(
        jnp.zeros(side.shape, f32), grad_normed_window, own_rows - inset, axis=1
    )
    own_part = grad_side[:, own_rows : 2 * own_rows].reshape(micro * own_rows, D) + grad_normed_own
    back = lax.ppermute(grad_side[:, :own_rows].astype(bf16), "mp", [(j + 1, j) for j in range(n_mp - 1)])
    forth = lax.ppermute(
        grad_side[:, 2 * own_rows : 3 * own_rows].astype(bf16), "mp", [(j, j + 1) for j in range(n_mp - 1)]
    )
    grad_normed = own_part + (back.astype(f32) + forth.astype(f32)).reshape(micro * own_rows, D)
    rho = lax.rsqrt(jnp.mean(rows * rows, axis=-1, keepdims=True) + epsilon)
    grad_gain_one = jnp.sum(grad_normed * rows * rho, axis=0, keepdims=True)
    u = grad_normed * gain_low[0]
    tokens_grad = grad_middle + rho * (u - rows * rho * rho * jnp.mean(u * rows, axis=-1, keepdims=True))

    table_sum = lax.dot_general(
        onehot, diag.reshape(H, SKEW), (((0,), (1,)), ((), ())), precision=HIGHEST, preferred_element_type=f32
    )
    gain_sum = jnp.concatenate([grad_gain_one, grad_gain_two])
    gain_sum, table_sum = lax.psum((gain_sum, table_sum), ("dp", "mp"))
    gain_grad = lax.dynamic_slice_in_dim(gain_sum, lax.axis_index("dp") * gains.shape[1], gains.shape[1], axis=1)
    table_grad = lax.dynamic_slice_in_dim(table_sum, here * heads_dev, heads_dev, axis=1)

    rows_dev = attn_in.shape[1]
    width_ffn = ffn_in.shape[2]
    parts_attn = shard_attn.reshape(rows_dev, 4, width).transpose(1, 0, 2)
    parts_ffn = shard_ffn.reshape(rows_dev, 3, width_ffn).transpose(1, 0, 2)
    mom_in = momentum_decay * attn_in_mom + parts_attn[:3]
    mom_out_t = momentum_decay * attn_out_mom.T + parts_attn[3]
    mom_fin = momentum_decay * ffn_in_mom + parts_ffn[:2]
    mom_fout_t = momentum_decay * ffn_out_mom.T + parts_ffn[2]
    blocks_attn = jnp.concatenate([mom_in, mom_out_t[None]])
    blocks_ffn = jnp.concatenate([mom_fin, mom_fout_t[None]])
    gram_ffn = lax.psum(grams_of(blocks_ffn), "dp")
    gram_attn = lax.psum(grams_of(blocks_attn), "dp")
    orth_ffn = orthogonal(blocks_ffn, gram_ffn)
    orth_attn = orthogonal(blocks_attn, gram_attn)
    attn_in_next = attn_in * (1.0 - rate_attn_in * decay_rate) - rate_attn_in * orth_attn[:3]
    attn_out_next = attn_out * (1.0 - rate_attn_out * decay_rate) - rate_attn_out * orth_attn[3].T
    ffn_in_next = ffn_in * (1.0 - rate_ffn_in * decay_rate) - rate_ffn_in * orth_ffn[:2]
    ffn_out_next = ffn_out * (1.0 - rate_ffn_out * decay_rate) - rate_ffn_out * orth_ffn[2].T
    gain_first_next, gain_second_next, gains_next = adam_update(gains, gain_grad, gain_first, gain_second)
    table_first_next, table_second_next, table_next = adam_update(table, table_grad, table_first, table_second)
    return (
        output.reshape(tokens.shape),
        tokens_grad.reshape(tokens.shape),
        attn_in_next,
        attn_out_next,
        ffn_in_next,
        ffn_out_next,
        mom_in,
        mom_out_t.T,
        mom_fin,
        mom_fout_t.T,
        gain_first_next,
        gain_second_next,
        gains_next,
        table_first_next,
        table_second_next,
        table_next,
    )


def solution(mesh):
    token = P(None, ("dp", "mp"), None)
    columns = P(None, "dp", "mp")
    flipped = P("mp", "dp")
    gain = P(None, "dp")
    head = P(None, "mp")
    return jax.shard_map(
        shards,
        mesh=mesh,
        in_specs=(
            token, P(None, "dp"), token, columns, flipped, columns, flipped, gain, head,
            columns, flipped, columns, flipped, gain, gain, head, head,
        ),
        out_specs=(
            token, token, columns, flipped, columns, flipped, columns, flipped, columns, flipped,
            gain, gain, gain, head, head, head,
        ),
        check_vma=False,
    )
```

```python
import functools

import jax
import jax.numpy as jnp
import numpy as np
from jax import lax
from jax.experimental import pallas as pl
from jax.experimental.pallas import tpu as pltpu
from jax.sharding import PartitionSpec as P

D = 768
H = 12
DH = 64
BUCKETS = 32
LEN = 512
STEP = 8
QB = 128
SKEW = 1024
PAIRS = H // 2
TILE = 128
HEAD_ORDER = (0, 1, 3, 4, 6, 7, 9, 10, 2, 5, 8, 11)

epsilon = 1e-06
negative_fill = -1e30
momentum_decay = 0.95
decay_rate = 0.01
linear_coefficient = 3.4445
coef_second = -4.775
coef_third = 2.0315
rate_attn_in = 0.25
rate_attn_out = 12.0
rate_ffn_in = 0.6
rate_ffn_out = 0.3
beta_one = 0.9
beta_two = 0.95
adam_epsilon = 1e-08
adam_rate = 0.3
bucket_marks = (12, 16, 23, 32, 46, 64, 91)

HIGHEST = lax.Precision.HIGHEST
HIGH = lax.Precision.HIGH
bf16 = jnp.bfloat16
f32 = jnp.float32
NN = (((1,), (0,)), ((), ()))
NT = (((1,), (1,)), ((), ()))
TN = (((0,), (0,)), ((), ()))


VMEM_GRANT = 60 << 20
ANY = pl.BlockSpec(memory_space=pltpu.HBM)
SMEM = pl.BlockSpec(memory_space=pltpu.SMEM)
VMEM = pl.BlockSpec(memory_space=pltpu.VMEM)


def dot(a, b, dims=NN):
    return lax.dot_general(a, b, dims, preferred_element_type=f32)


def skew_onehot():
    place = np.arange(SKEW)
    relative = np.where(place < SKEW - QB + 1, place, place - SKEW) - (LEN - QB)
    distance = np.abs(relative)
    far = 8 + sum((distance >= mark).astype(np.int32) for mark in bucket_marks)
    bucket = np.where(distance < 8, distance, far) + 16 * (relative > 0)
    return (bucket[:, None] == np.arange(BUCKETS)[None, :]).astype(np.float32)


def cost(micros):
    return pl.CostEstimate(flops=int(micros * 3e8), bytes_accessed=0, transcendentals=0)


def half_lanes(shape, half):
    lane = lax.broadcasted_iota(jnp.int32, shape, 1)
    return (lane < DH) if half == 0 else (lane >= DH)


def bias_kernel(line_ref, bias_ref):
    for half in range(2):
        line = jnp.broadcast_to(line_ref[0, half : half + 1, :], (QB, SKEW))
        bias_ref[0, half] = pltpu.roll(line, 0, 1, stride=1, stride_axis=0).T


def make_bias(line):
    return pl.pallas_call(
        bias_kernel,
        grid=(PAIRS,),
        compiler_params=pltpu.CompilerParams(vmem_limit_bytes=VMEM_GRANT),
        in_specs=[pl.BlockSpec((1, 2, SKEW), lambda p: (p, 0, 0))],
        out_specs=pl.BlockSpec((1, 2, SKEW, QB), lambda p: (p, 0, 0, 0)),
        out_shape=jax.ShapeDtypeStruct((PAIRS, 2, SKEW, QB), f32),
        cost_estimate=cost(8),
        name="make_bias",
    )(line)


def diag_kernel(acc_ref, diag_ref):
    row = lax.broadcasted_iota(jnp.int32, (QB, QB), 0)
    lane = lax.broadcasted_iota(jnp.int32, (QB, QB), 1)
    flip = (row + lane == QB - 1).astype(f32)
    for half in range(2):
        turned = lax.dot_general(flip, acc_ref[0, half], NT, precision=HIGHEST, preferred_element_type=f32)
        shifted = pltpu.roll(turned, SKEW - QB + 1, 1, stride=1, stride_axis=0)
        diag_ref[0, half : half + 1, :] = jnp.sum(shifted, axis=0, keepdims=True)


def diagonals(acc):
    return pl.pallas_call(
        diag_kernel,
        grid=(PAIRS,),
        compiler_params=pltpu.CompilerParams(vmem_limit_bytes=VMEM_GRANT),
        in_specs=[pl.BlockSpec((1, 2, SKEW, QB), lambda p: (p, 0, 0, 0))],
        out_specs=pl.BlockSpec((1, 2, SKEW), lambda p: (p, 0, 0)),
        out_shape=jax.ShapeDtypeStruct((PAIRS, 2, SKEW), f32),
        cost_estimate=cost(1),
        name="diagonals",
    )(acc)


def both_heads(block):
    zero = jnp.zeros_like(block)
    return jnp.concatenate(
        [
            jnp.where(half_lanes(block.shape, 0), block, zero),
            jnp.where(half_lanes(block.shape, 1), block, zero),
        ],
        axis=0,
    )


def exp_scores(meta, block, mb, keys, queries_two, bias_ref):
    start = pl.multiple_of((LEN - QB) - QB * meta[3 + block], QB)
    length = meta[6 + 2 * mb + meta[block]]
    bias = jnp.concatenate([bias_ref[0, 0, pl.ds(start, LEN), :], bias_ref[0, 1, pl.ds(start, LEN), :]], axis=1)
    scores = dot(keys, queries_two, NT) + bias
    row = lax.broadcasted_iota(jnp.int32, scores.shape, 0)
    scores = jnp.where(row < length, scores, negative_fill)
    top = jnp.max(scores, axis=0, keepdims=True)
    weights = jnp.exp(scores - top)
    return weights, jnp.sum(weights, axis=0, keepdims=True)


def attend_kernel(mb, meta, q_ref, k_ref, v_ref, bias_ref, *refs):
    o_ref = refs[-1]
    for block in range(3):
        rows = pl.ds(pl.multiple_of(meta[block] * LEN, LEN), LEN)
        keys, values = k_ref[0, rows, :], v_ref[0, rows, :]
        queries_two = both_heads(q_ref[0, block * QB : (block + 1) * QB, :])
        weights, total = exp_scores(meta, block, mb, keys, queries_two, bias_ref)
        out_two = dot(values.T, weights.astype(bf16)) / total
        top = lax.broadcasted_iota(jnp.int32, (QB, QB), 0) < DH
        out = jnp.where(top, out_two[:, :QB], out_two[:, QB:])
        o_ref[0, block * QB : (block + 1) * QB, :] = out.T.astype(bf16)


def attend_back_kernel(kept, meta, q_ref, k_ref, v_ref, do_ref, bias_ref, *refs):
    dq_ref, dk_ref, dv_ref, acc_ref, dk_acc, dv_acc = refs[kept:]
    mb = pl.program_id(1)

    @pl.when(mb == 0)
    def _():
        acc_ref[...] = jnp.zeros_like(acc_ref)

    dk_acc[...] = jnp.zeros_like(dk_acc)
    dv_acc[...] = jnp.zeros_like(dv_acc)
    for block in range(3):
        rows = pl.ds(pl.multiple_of(meta[block] * LEN, LEN), LEN)
        own = slice(block * QB, (block + 1) * QB)
        keys, values = k_ref[0, rows, :], v_ref[0, rows, :]
        queries_two = both_heads(q_ref[0, own, :])
        grad_two = both_heads(do_ref[0, own, :])
        weights, total = exp_scores(meta, block, mb, keys, queries_two, bias_ref)
        soft = weights * (1.0 / total)
        grad_soft = dot(values, grad_two, NT)
        inner = jnp.sum(grad_soft * soft, axis=0, keepdims=True)
        grad_scores = soft * (grad_soft - inner)
        start = pl.multiple_of((LEN - QB) - QB * meta[3 + block], QB)
        acc_ref[0, 0, pl.ds(start, LEN), :] += grad_scores[:, :QB]
        acc_ref[0, 1, pl.ds(start, LEN), :] += grad_scores[:, QB:]
        grad_low = grad_scores.astype(bf16)
        dk_acc[rows, :] += dot(grad_low, queries_two)
        dv_acc[rows, :] += dot(soft.astype(bf16), grad_two)
        dq_two = dot(keys.T, grad_low)
        top = lax.broadcasted_iota(jnp.int32, (QB, QB), 0) < DH
        dq_ref[0, own, :] = jnp.where(top, dq_two[:, :QB], dq_two[:, QB:]).T.astype(bf16)
    dk_ref[0] = dk_acc[...].astype(bf16)
    dv_ref[0] = dv_acc[...].astype(bf16)


def attend(meta, q, k, v, bias, mb, earlier=()):
    rows, window = q.shape[1], k.shape[1]
    own = pl.BlockSpec((1, rows, QB), lambda p, _: (mb, 0, p))
    wide = pl.BlockSpec((1, window, QB), lambda p, _: (mb, 0, p))
    lines = pl.BlockSpec((1, 2, SKEW, QB), lambda p, _: (p, 0, 0, 0))
    return pl.pallas_call(
        functools.partial(attend_kernel, mb),
        grid_spec=pltpu.PrefetchScalarGridSpec(
            num_scalar_prefetch=1,
            grid=(PAIRS,),
            in_specs=[own, wide, wide, lines] + [ANY] * len(earlier),
            out_specs=own,
        ),
        out_shape=jax.ShapeDtypeStruct(q.shape, bf16),
        input_output_aliases={5 + j: j for j in range(len(earlier))},
        compiler_params=pltpu.CompilerParams(vmem_limit_bytes=VMEM_GRANT),
        cost_estimate=cost(11),
        name="attend",
    )(meta, q, k, v, bias, *earlier)


def attend_back(meta, q, k, v, grad, bias, pairs, earlier=(), after=()):
    micro, rows, _ = q.shape
    window = k.shape[1]
    first, count = pairs
    own = pl.BlockSpec((1, rows, QB), lambda p, m, _: (m, 0, p + first))
    wide = pl.BlockSpec((1, window, QB), lambda p, m, _: (m, 0, p + first))
    lines = pl.BlockSpec((1, 2, SKEW, QB), lambda p, m, _: (p + first, 0, 0, 0))
    kept = len(earlier) + len(after)
    return pl.pallas_call(
        functools.partial(attend_back_kernel, kept),
        grid_spec=pltpu.PrefetchScalarGridSpec(
            num_scalar_prefetch=1,
            grid=(count, micro),
            in_specs=[own, wide, wide, own, lines] + [ANY] * kept,
            out_specs=[own, wide, wide, lines],
            scratch_shapes=[pltpu.VMEM((window, QB), f32), pltpu.VMEM((window, QB), f32)],
        ),
        out_shape=[
            jax.ShapeDtypeStruct(q.shape, bf16),
            jax.ShapeDtypeStruct(k.shape, bf16),
            jax.ShapeDtypeStruct(k.shape, bf16),
            jax.ShapeDtypeStruct(bias.shape, f32),
        ],
        input_output_aliases={6 + j: j for j in range(len(earlier))},
        compiler_params=pltpu.CompilerParams(vmem_limit_bytes=VMEM_GRANT),
        cost_estimate=cost(7 * count),
        name="attend_back",
    )(meta, q, k, v, grad, bias, *earlier, *after)


PARTS = 8
PART = D // PARTS


def part_rows(place, k):
    return pl.ds(pl.multiple_of((place[0] ^ k) * PART, PART), PART)


def entry_of(place, group):
    return lax.rem(group - place[1] + 4, 4)


def wait_for(ref, sem):
    pltpu.make_async_copy(ref, ref, sem).wait()


def lower_lanes(shape):
    return lax.broadcasted_iota(jnp.int32, shape, 1) < DH


def join_kernel(place, *refs):
    pieces, (w_ref, rest_ref, sems) = refs[:PARTS], refs[-3:]
    for group in range(4):
        entry = entry_of(place, group)
        for k, piece in enumerate(pieces):
            rows = part_rows(place, k)
            lanes = pl.ds(group * TILE, TILE)
            pltpu.make_async_copy(piece.at[entry, pl.ds(0, 4)], w_ref.at[:, rows, lanes], sems.at[0]).start()
            pltpu.make_async_copy(piece.at[entry, pl.ds(4, 2)], rest_ref.at[group, :, rows], sems.at[1]).start()
    wait_for(rest_ref, sems.at[1])
    lower = lower_lanes((D, TILE))
    for two in range(2):
        lanes = slice((4 + two) * TILE, (5 + two) * TILE)
        for both in range(2):
            even, odd = rest_ref[2 * two, both], rest_ref[2 * two + 1, both]
            w_ref[2 * both, :, lanes] = jnp.where(lower, even, odd)
            w_ref[2 * both + 1, :, lanes] = pltpu.roll(jnp.where(lower, odd, even).astype(f32), DH, 1).astype(bf16)
    wait_for(w_ref.at[:, :, pl.ds(0, 4 * TILE)], sems.at[0])


def join(place, pieces, later=()):
    return pl.pallas_call(
        join_kernel,
        in_specs=[SMEM] + [ANY] * (PARTS + len(later)),
        out_specs=VMEM,
        out_shape=jax.ShapeDtypeStruct((4, D, D), bf16),
        scratch_shapes=[pltpu.VMEM((4, 2, D, TILE), bf16), pltpu.SemaphoreType.DMA((2,))],
        compiler_params=pltpu.CompilerParams(vmem_limit_bytes=VMEM_GRANT),
        cost_estimate=cost(5),
        name="join",
    )(place, *pieces, *later)


def project_kernel(x_ref, own_ref, gain_ref, w_ref, *refs):
    q_ref, k_ref, v_ref, n_ref, n_own_ref = refs[-5:]

    def norm(rows):
        rows = rows.astype(f32)
        rho = lax.rsqrt(jnp.mean(rows * rows, axis=-1, keepdims=True) + epsilon)
        return (rows * rho * gain_ref[...]).astype(bf16)

    normed = norm(x_ref[...])
    n_ref[0] = normed
    k_ref[0] = dot(normed, w_ref[1]).astype(bf16)
    v_ref[0] = dot(normed, w_ref[2]).astype(bf16)
    normed = norm(own_ref[0])
    n_own_ref[0] = normed
    q_ref[0] = dot(normed, w_ref[0]).astype(bf16)


PROJECT_STEPS = 4


def project(window, own, gain, weights, mb, earlier=(), later=()):
    micro, own_rows, _ = own.shape
    rows, few = window.shape[0] // PROJECT_STEPS, own_rows // PROJECT_STEPS
    wide = pl.BlockSpec((1, rows, D), lambda t: (mb, t, 0))
    small = pl.BlockSpec((1, few, D), lambda t: (mb, t, 0))
    many_shape = jax.ShapeDtypeStruct((micro, window.shape[0], D), bf16)
    few_shape = jax.ShapeDtypeStruct(own.shape, bf16)
    return pl.pallas_call(
        project_kernel,
        grid=(PROJECT_STEPS,),
        in_specs=[
            pl.BlockSpec((rows, D), lambda t: (t, 0)),
            small,
            pl.BlockSpec((1, D), lambda t: (0, 0)),
            pl.BlockSpec((3, D, D), lambda t: (0, 0, 0)),
        ]
        + [ANY] * (len(earlier) + len(later)),
        out_specs=[small, wide, wide, wide, small],
        out_shape=[few_shape, many_shape, many_shape, many_shape, few_shape],
        input_output_aliases={4 + j: j for j in range(len(earlier))},
        compiler_params=pltpu.CompilerParams(vmem_limit_bytes=VMEM_GRANT),
        cost_estimate=cost(7),
        name="project",
    )(window, own, gain, weights, *earlier, *later)


GRAD_STEPS = 8


def attn_grads_kernel(place, n_ref, dk_ref, dv_ref, own_ref, dq_ref, dh_ref, o_ref, even_ref, odd_ref, *scratch):
    acc_ref, main_ref, rest_ref, sems = scratch
    step = pl.program_id(0)

    @pl.when(step == 0)
    def _():
        acc_ref[...] = jnp.zeros_like(acc_ref)

    turned = n_ref[...].T
    acc_ref[1] += dot(turned, dk_ref[...])
    acc_ref[2] += dot(turned, dv_ref[...])

    @pl.when(step % 2 == 1)
    def _():
        acc_ref[0] += dot(own_ref[...].T, dq_ref[...])
        acc_ref[3] += dot(dh_ref[...].T, o_ref[...])

    @pl.when(step == GRAD_STEPS - 1)
    def _():
        lower = lower_lanes((D, TILE))
        for c in range(4):
            main_ref[c] = acc_ref[c, :, : 4 * TILE].astype(bf16)
        for group in range(4):
            entry = entry_of(place, group)
            for k in range(PARTS):
                part = (odd_ref if k % 2 else even_ref).at[k // 2, entry, pl.ds(0, 4)]
                source = main_ref.at[:, part_rows(place, k), pl.ds(group * TILE, TILE)]
                pltpu.make_async_copy(source, part, sems.at[0]).start()
        for two in range(2):
            lanes = slice((4 + two) * TILE, (5 + two) * TILE)
            for both in range(2):
                one = acc_ref[2 * both, :, lanes]
                other = pltpu.roll(acc_ref[2 * both + 1, :, lanes], DH, 1)
                rest_ref[2 * two, both] = jnp.where(lower, one, other).astype(bf16)
                rest_ref[2 * two + 1, both] = jnp.where(lower, other, one).astype(bf16)
        for group in range(4):
            entry = entry_of(place, group)
            for k in range(PARTS):
                part = (odd_ref if k % 2 else even_ref).at[k // 2, entry, pl.ds(4, 2)]
                source = rest_ref.at[group, :, part_rows(place, k)]
                pltpu.make_async_copy(source, part, sems.at[0]).start()
        wait_for(even_ref, sems.at[0])
        wait_for(odd_ref, sems.at[0])


def attn_grads(place, normed_window, dk, dv, normed_own, dq, dh, o):
    rows, few = dk.shape[0] // GRAD_STEPS, dq.shape[0] // (GRAD_STEPS // 2)
    wide = pl.BlockSpec((rows, D), lambda t: (t, 0))
    small = pl.BlockSpec((few, D), lambda t: (t // 2, 0))
    parts = jax.ShapeDtypeStruct((PARTS // 2, 4, 6, PART, TILE), bf16)
    return pl.pallas_call(
        attn_grads_kernel,
        grid=(GRAD_STEPS,),
        in_specs=[SMEM, wide, wide, wide, small, small, small, small],
        out_specs=[ANY] * 2,
        out_shape=[parts] * 2,
        scratch_shapes=[
            pltpu.VMEM((4, D, D), f32),
            pltpu.VMEM((4, D, 4 * TILE), bf16),
            pltpu.VMEM((4, 2, D, TILE), bf16),
            pltpu.SemaphoreType.DMA((1,)),
        ],
        compiler_params=pltpu.CompilerParams(vmem_limit_bytes=VMEM_GRANT),
        cost_estimate=cost(10),
        name="attn_grads",
    )(place, normed_window, dk, dv, normed_own, dq, dh, o)


ROWS = 256


def gelu_and_slope(gate):
    root = 0.7978845608028654
    cube = 0.044715
    square = gate * gate
    bend = jnp.tanh(root * gate * (1.0 + cube * square))
    half = 0.5 * (1.0 + bend)
    slope = half + 0.5 * gate * (1.0 - bend * bend) * (root * (1.0 + 3.0 * cube * square))
    return gate * half, slope


def ffn_kernel(first, last, entries, place, *refs):
    refs = list(refs)
    take = lambda count: [refs.pop(0) for _ in range(count)]
    y_ref, dy_ref, gain_ref = take(3)
    acc_in, dn_in = (None, None) if first else take(2)
    (all_w,) = take(1)
    outs = take(3 if last else 2)
    even_ref, odd_ref = take(2)
    w_ref, g_ref, n_ref, nt_ref, dyt_ref, acc_ref, dn_ref, hid_ref, dgate_ref, dup_ref, w_sems, g_sems = refs
    tokens = y_ref.shape[0]
    width = w_ref.shape[2] // 3
    gate_cols, up_cols, down_cols = (slice(c * width, (c + 1) * width) for c in range(3))

    for at, entry in enumerate(entries):
        group = lax.rem(entry + place[1], 4)
        for k in range(PARTS):
            pltpu.make_async_copy(all_w.at[k, group], w_ref.at[at, pl.ds(k * PART, PART)], w_sems.at[at]).start()
    y = y_ref[...]
    rho = lax.rsqrt(jnp.mean(y * y, axis=-1, keepdims=True) + epsilon)
    normed = (y * rho * gain_ref[...]).astype(bf16)
    n_ref[...] = normed
    nt_ref[...] = normed.T
    dyt_ref[...] = dy_ref[...].T
    acc_ref[...] = y if first else acc_in[...]
    dn_ref[...] = jnp.zeros_like(dn_ref) if first else dn_in[...]

    def one_group(at, _):
        wait_for(w_ref.at[at], w_sems.at[at])
        w = w_ref.at[at]

        def tile(t, _):
            rows = pl.ds(pl.multiple_of(t * ROWS, ROWS), ROWS)
            normed = n_ref[rows, :]
            gate = dot(normed, w[:, gate_cols])
            up = dot(normed, w[:, up_cols])
            grad_hid = dot(dy_ref[rows, :], w[:, down_cols])
            act, slope = gelu_and_slope(gate)
            hid = (act * up).astype(bf16)
            dgate = (grad_hid * up * slope).astype(bf16)
            dup = (grad_hid * act).astype(bf16)
            hid_ref[rows, :] = hid
            dgate_ref[rows, :] = dgate
            dup_ref[rows, :] = dup
            acc_ref[rows, :] += dot(hid, w[:, down_cols], NT)
            dn_ref[rows, :] += dot(dgate, w[:, gate_cols], NT) + dot(dup, w[:, up_cols], NT)
            return 0

        lax.fori_loop(0, tokens // ROWS, tile, 0)

        def grads(t, _):
            rows = pl.ds(pl.multiple_of(t * ROWS, ROWS), ROWS)
            g_ref[at, rows, gate_cols] = dot(nt_ref[rows, :], dgate_ref[...]).astype(bf16)
            g_ref[at, rows, up_cols] = dot(nt_ref[rows, :], dup_ref[...]).astype(bf16)
            g_ref[at, rows, down_cols] = dot(dyt_ref[rows, :], hid_ref[...]).astype(bf16)
            return 0

        lax.fori_loop(0, D // ROWS, grads, 0)
        for k in range(PARTS):
            part = (odd_ref if k % 2 else even_ref).at[k // 2, at]
            pltpu.make_async_copy(g_ref.at[at, part_rows(place, k)], part, g_sems.at[0]).start()
        return 0

    lax.fori_loop(0, len(entries), one_group, 0)

    if last:
        out_ref, dy1_ref, dh1_ref = outs
        out_ref[...] = acc_ref[...].astype(bf16)
        y = y_ref[...]
        rho = lax.rsqrt(jnp.mean(y * y, axis=-1, keepdims=True) + epsilon)
        scaled_y = y * rho
        u = dn_ref[...] * gain_ref[...]
        inner = jnp.mean(u * scaled_y, axis=-1, keepdims=True)
        dy1 = dy_ref[...].astype(f32) + rho * (u - scaled_y * inner)
        dy1_ref[...] = dy1
        dh1_ref[...] = dy1.astype(bf16)
    else:
        outs[0][...] = acc_ref[...]
        outs[1][...] = dn_ref[...]
    wait_for(even_ref, g_sems.at[0])
    wait_for(odd_ref, g_sems.at[0])


def ffn(place, y, dy, gain, weights, entries, sums=None, last=False):
    tokens = y.shape[0]
    columns = weights.shape[3]
    wide = lambda dtype: jax.ShapeDtypeStruct((tokens, D), dtype)
    outs = [wide(bf16), wide(f32), wide(bf16)] if last else [wide(f32), wide(f32)]
    operands = [y, dy, gain] + list(sums or [])
    parts = jax.ShapeDtypeStruct((PARTS // 2, len(entries), PART, columns), bf16)
    results = pl.pallas_call(
        functools.partial(ffn_kernel, sums is None, last, entries),
        in_specs=[SMEM] + [VMEM] * len(operands) + [ANY],
        out_specs=[VMEM] * len(outs) + [ANY] * 2,
        out_shape=outs + [parts] * 2,
        scratch_shapes=[
            pltpu.VMEM((len(entries), D, columns), bf16),
            pltpu.VMEM((len(entries), D, columns), bf16),
            pltpu.VMEM((tokens, D), bf16),
            pltpu.VMEM((D, tokens), bf16),
            pltpu.VMEM((D, tokens), bf16),
            pltpu.VMEM((tokens, D), f32),
            pltpu.VMEM((tokens, D), f32),
            pltpu.VMEM((tokens, columns // 3), bf16),
            pltpu.VMEM((tokens, columns // 3), bf16),
            pltpu.VMEM((tokens, columns // 3), bf16),
            pltpu.SemaphoreType.DMA((len(entries),)),
            pltpu.SemaphoreType.DMA((1,)),
        ],
        compiler_params=pltpu.CompilerParams(vmem_limit_bytes=VMEM_GRANT),
        cost_estimate=cost(20),
        name="ffn",
    )(place, *operands, weights)
    return results[: len(outs)], results[len(outs) :]


def grams_of(blocks):
    return jnp.einsum("our,ouw->orw", blocks, blocks, precision=HIGHEST)


def orthogonal(blocks, gram):
    total = jnp.trace(gram, axis1=1, axis2=2)[:, None, None]
    mul = functools.partial(jnp.einsum, "oij,ojk->oik", precision=HIGH)
    first = gram / total
    start = blocks * lax.rsqrt(total)
    eye = jnp.eye(gram.shape[1], dtype=f32)[None]
    step = linear_coefficient * eye + coef_second * first + coef_third * mul(first, first)
    second = mul(mul(first, step), step)
    once = mul(start, step)
    turn = mul(once, second)
    return linear_coefficient * once + coef_second * turn + coef_third * mul(turn, second)


def adam_update(param, grad, first, second):
    first_new = beta_one * first + (1.0 - beta_one) * grad
    second_new = beta_two * second + (1.0 - beta_two) * grad * grad
    corrected_first = first_new / (1.0 - beta_one**STEP)
    corrected_second = second_new / (1.0 - beta_two**STEP)
    return (
        first_new,
        second_new,
        param - adam_rate * corrected_first / (jnp.sqrt(corrected_second) + adam_epsilon),
    )


def direct():
    return lax.axis_size("dp") == PARTS and lax.axis_size("mp") == 4


def swap(x, bit):
    return lax.ppermute(x, "dp", [(j, j ^ bit) for j in range(lax.axis_size("dp"))])


def from_above(x, k):
    return lax.ppermute(x, "mp", [((j + k) % 4, j) for j in range(4)])


def to_above(x, k):
    return lax.ppermute(x, "mp", [(j, (j + k) % 4) for j in range(4)])


def behind(x, *others):
    return lax.optimization_barrier((x, others))[0]


def total(*terms):
    return sum(term.astype(f32) for term in terms)


def gather_all(shard):
    rows, columns = shard.shape
    whole = lax.all_gather(shard, ("dp", "mp"), axis=0, tiled=False)
    if rows == PART:
        return whole.reshape(PARTS, 4, PART, columns)
    whole = whole.reshape(-1, 4, rows, columns).transpose(1, 0, 2, 3).reshape(4, PARTS, PART, columns)
    return whole.transpose(1, 0, 2, 3)


def gather_pieces(shard):
    tiles, rows, _ = shard.shape
    if not direct():
        whole = lax.all_gather(shard, ("dp", "mp"), axis=0, tiled=False)
        whole = whole.reshape(PARTS, -1, 4, tiles, rows, TILE).transpose(0, 2, 3, 1, 4, 5)
        return list(whole.reshape(PARTS, 4, tiles, PART, TILE))
    own = jnp.stack([shard] + [from_above(shard, k) for k in (1, 2, 3)])
    return own


def spread_pieces(own, meanwhile):
    if not direct():
        return own
    along, across = behind((swap(own, 2), swap(own, 4)), meanwhile)
    far = jnp.concatenate([swap(along[:2], 4), swap(across[2:], 2)])
    even = [own, along, across, far]
    return [piece for here in even for piece in (here, swap(here, 1))]


def scatter_core(even, odd):
    return total(even, swap(odd, 1)).astype(bf16)


def scatter_plane(mine, meanwhile=()):
    others = behind((swap(mine[1], 2), swap(mine[2], 4), swap(mine[3], 6)), meanwhile)
    return total(mine[0], *others).astype(bf16)


def scatter_plain(even, odd, rows):
    whole = jnp.stack([even, odd], axis=1)
    whole = whole.reshape(PARTS, 4, -1, PART // rows, rows, whole.shape[-1])
    parts = whole.transpose(0, 3, 1, 2, 4, 5)
    parts = parts.reshape((-1,) + parts.shape[3:])
    return lax.psum_scatter(parts, ("dp", "mp"), scatter_dimension=0, tiled=False).astype(f32)


def gather_small(x, axis_name, axis):
    if not direct():
        return lax.all_gather(x, axis_name, axis=axis, tiled=True)
    here = lax.axis_index(axis_name)
    size = lax.axis_size(axis_name)
    bit = 1
    while bit < size:
        other = lax.ppermute(x, axis_name, [(j, j ^ bit) for j in range(size)])
        upper = (here & bit) != 0
        x = jnp.concatenate([jnp.where(upper, other, x), jnp.where(upper, x, other)], axis=axis)
        bit *= 2
    return x


def sum_line(x):
    if not direct():
        return lax.psum(x, "mp")
    return x + from_above(x, 1) + from_above(x, 2) + from_above(x, 3)


def sum_planes(x, meanwhile=()):
    if not direct():
        return lax.psum(x, "dp")
    odd = (lax.axis_index("dp") & 1) != 0
    low = lambda v: v.astype(bf16)
    mine = total(jnp.where(odd, x[2:], x[:2]), swap(low(jnp.where(odd, x[:2], x[2:])), 1))
    one, two = mine[0], mine[1]
    one, two = behind((total(one, swap(low(one), 2)), total(two, swap(low(two), 4))), meanwhile)
    one, two = total(one, swap(low(one), 4)), total(two, swap(low(two), 2))
    mine = low(jnp.stack([one, two]))
    other = swap(mine, 1)
    return jnp.concatenate([jnp.where(odd, other, mine), jnp.where(odd, mine, other)]).astype(f32)


def shards(
    tokens, lengths, cotangent, attn_in, attn_out, ffn_in, ffn_out, gains, table,
    attn_in_mom, attn_out_mom, ffn_in_mom, ffn_out_mom,
    gain_first, gain_second, table_first, table_second,
):
    micro, own_rows, _ = tokens.shape
    here = lax.axis_index("mp")
    n_mp = lax.axis_size("mp")
    width = attn_in.shape[2]
    heads_dev = table.shape[1]

    rows_dev = attn_in.shape[1]
    width_ffn = ffn_in.shape[2]
    index = jnp.stack([lax.axis_index("dp"), here]).astype(jnp.int32)
    place = index if direct() else jnp.zeros_like(index)
    odd_group = (here & 1) != 0

    ffn_low = jnp.concatenate([ffn_in[0], ffn_in[1], ffn_out.T], axis=1).astype(bf16)
    attn_low = [part.astype(bf16) for part in (attn_in[0], attn_in[1], attn_in[2], attn_out.T)]
    tails = [part[:, TILE:] for part in attn_low]
    beside = lambda one, two: jnp.where(
        odd_group, jnp.concatenate([two, one], axis=1), jnp.concatenate([one, two], axis=1)
    )
    attn_tiles = jnp.stack([part[:, :TILE] for part in attn_low] + [beside(*tails[:2]), beside(*tails[2:])])
    gain_low = gather_small(gains.astype(bf16), "dp", 1).astype(f32)
    table_all = gather_small(table, "mp", 1)[:, np.array(HEAD_ORDER)]
    onehot = skew_onehot()
    line = lax.dot_general(
        table_all, onehot, (((0,), (1,)), ((), ())), precision=HIGHEST, preferred_element_type=f32
    ).reshape(PAIRS, 2, SKEW)
    attn_own = behind(gather_pieces(attn_tiles), gain_low, line)
    halo, ffn_low = behind((tokens, ffn_low), attn_own)
    up, down = [(j, j + 1) for j in range(n_mp - 1)], [(j + 1, j) for j in range(n_mp - 1)]
    sides = []
    for mb in range(micro):
        part = behind(halo[mb], sides)
        sides.append((lax.ppermute(part, "mp", up), lax.ppermute(part, "mp", down)))
    ffn_all = gather_all(ffn_low)
    bias = make_bias(behind(line, attn_own))
    attn_pieces = spread_pieces(attn_own, (bias, sides[0]))
    weights = join(place, behind(attn_pieces, sides))
    w_q, w_k, w_v, w_o = weights

    first_row = own_rows * here
    first_doc = first_row // LEN
    inset = first_row - first_doc * LEN
    gap = jnp.zeros((2 * LEN - 2 * own_rows + QB, D), bf16)
    block_place = first_row // QB + jnp.arange(own_rows // QB, dtype=jnp.int32)
    slot = block_place // (LEN // QB) - first_doc
    lens_window = lax.dynamic_slice_in_dim(
        jnp.concatenate([lengths, jnp.ones((micro, 1), lengths.dtype)], axis=1), first_doc, 2, axis=1
    )
    meta = jnp.concatenate([slot, block_place % (LEN // QB), lens_window.reshape(-1)]).astype(jnp.int32)

    projected, attended = (), ()
    for mb in range(micro):
        above, below = behind(sides[mb], weights, attended)
        window = jnp.concatenate([above, tokens[mb], below, gap])
        window = lax.dynamic_slice_in_dim(window, own_rows - inset, 2 * LEN, axis=0)
        projected = project(window, tokens, gain_low[0:1], weights, mb, projected, attended)
        q, k, v, normed_window, normed_own = projected
        attended = (attend(meta, q, k, v, bias, mb, attended),)
    attended = attended[0].reshape(micro * own_rows, D)
    normed_window = normed_window.reshape(micro * 2 * LEN, D)
    normed_own = normed_own.reshape(micro * own_rows, D)
    rows = tokens.reshape(micro * own_rows, D).astype(f32)
    middle = rows + dot(attended, w_o, NT)

    dy = cotangent.reshape(micro * own_rows, D)
    ffn_args = (place, middle, dy, gain_low[1:2], ffn_all)
    sums, (even_one, odd_one) = ffn(*ffn_args, (0, 1))
    (output, grad_middle, grad_mid_low), (even_two, odd_two) = ffn(*ffn_args, (2, 3), sums, last=True)
    if direct():
        mine_one, mine_two = scatter_core(even_one, odd_one), scatter_core(even_two, odd_two)
    else:
        shard_ffn = scatter_plain(
            jnp.concatenate([even_one, even_two], axis=1), jnp.concatenate([odd_one, odd_two], axis=1), rows_dev
        )[0]
        mine_one = mine_two = ()

    grad_att = dot(grad_mid_low, w_o).astype(bf16).reshape(micro, own_rows, D)
    back_args = (meta, q, k, v, grad_att, bias)
    grads = attend_back(*back_args, (0, 2), (), [mine_one] if direct() else ())
    grads = attend_back(*back_args, (2, 2), grads, [mine_two] if direct() else ())
    line_one, line_two = (), ()
    if direct():
        line_one = scatter_plane(mine_one, grads)
        line_two = scatter_plane(behind(mine_two, line_one))
        sent_one = to_above(line_one[1], 1)
    grad_q, grad_k, grad_v, grad_bias = attend_back(*back_args, (4, 2), grads, [line_one] if direct() else ())
    grad_q = grad_q.reshape(micro * own_rows, D)
    grad_k = grad_k.reshape(micro * 2 * LEN, D)
    grad_v = grad_v.reshape(micro * 2 * LEN, D)
    even, odd = attn_grads(
        place, normed_window, grad_k, grad_v, normed_own, grad_q, grad_mid_low, attended
    )
    grad_q, grad_k, grad_v = behind((grad_q, grad_k, grad_v), even)
    grad_normed_own = dot(grad_q, w_q, NT)
    grad_normed_window = (dot(grad_k, w_k, NT) + dot(grad_v, w_v, NT)).reshape(micro, 2 * LEN, D)
    edge = ((0, 0), (own_rows, own_rows), (0, 0))
    sent = jnp.pad(grad_normed_window.astype(bf16), edge)
    back = lax.dynamic_slice_in_dim(sent, inset, own_rows, axis=1)
    forth = lax.dynamic_slice_in_dim(sent, inset + 2 * own_rows, own_rows, axis=1)
    own_part = lax.dynamic_slice_in_dim(grad_normed_window, inset, own_rows, axis=1)
    own_part = own_part.reshape(micro * own_rows, D) + grad_normed_own
    if direct():
        shard_ffn = total(line_one[0], sent_one, to_above(line_two[0], 2), to_above(line_two[1], 3))
        mine_attn = behind(scatter_core(even, odd), back, forth, shard_ffn)
        back, forth = behind((back, forth), mine_attn)
    else:
        mine_attn = even
    back, forth = lax.ppermute(back, "mp", down), lax.ppermute(forth, "mp", up)
    if direct():
        line_attn = scatter_plane(mine_attn, (back, forth))
        shard_attn = total(line_attn[0], *[to_above(line_attn[k], k) for k in (1, 2, 3)])
    else:
        line_attn = even
        shard_attn = scatter_plain(even, odd, rows_dev)
    grad_bias = behind(grad_bias, mine_attn)
    back, forth = behind((back, forth), shard_attn)
    grad_normed = own_part + (back.astype(f32) + forth.astype(f32)).reshape(micro * own_rows, D)
    rho = lax.rsqrt(jnp.mean(rows * rows, axis=-1, keepdims=True) + epsilon)
    u = grad_normed * gain_low[0]
    tokens_grad = grad_middle + rho * (u - rows * rho * rho * jnp.mean(u * rows, axis=-1, keepdims=True))

    pick = lambda tile, second: jnp.where(odd_group ^ second, tile[:, DH:], tile[:, :DH])
    parts_attn = jnp.stack(
        [
            jnp.concatenate([shard_attn[c], pick(shard_attn[4 + c // 2], c % 2 == 1)], axis=1)
            for c in range(4)
        ]
    )
    parts_ffn = shard_ffn.reshape(rows_dev, 3, width_ffn).transpose(1, 0, 2)
    low = lambda v: v.astype(bf16).astype(f32)
    gain_terms = jnp.stack(
        [jnp.sum(low(attn_in) * parts_attn[:3], axis=(0, 2)), jnp.sum(low(ffn_in) * parts_ffn[:2], axis=(0, 2))]
    )
    mom_in = momentum_decay * attn_in_mom + parts_attn[:3]
    mom_out_t = momentum_decay * attn_out_mom.T + parts_attn[3]
    mom_fin = momentum_decay * ffn_in_mom + parts_ffn[:2]
    mom_fout_t = momentum_decay * ffn_out_mom.T + parts_ffn[2]
    blocks_attn = jnp.concatenate([mom_in, mom_out_t[None]])
    blocks_ffn = jnp.concatenate([mom_fin, mom_fout_t[None]])
    gram_ffn = behind(grams_of(blocks_ffn), line_attn)
    gram_ffn = sum_planes(gram_ffn.reshape(4, -1, width_ffn)).reshape(gram_ffn.shape)
    table_sum = lax.dot_general(
        onehot,
        diagonals(grad_bias).reshape(H, SKEW),
        (((0,), (1,)), ((), ())),
        precision=HIGHEST,
        preferred_element_type=f32,
    )
    gram_attn = grams_of(blocks_attn)
    gram_ffn = behind(gram_ffn, gram_attn)
    orth_ffn = orthogonal(blocks_ffn, gram_ffn)
    extra = jnp.pad(table_sum.reshape(4, 1, -1), ((0, 0), (0, 15), (0, width - BUCKETS * H // 4)))
    summed = sum_planes(jnp.concatenate([gram_attn, extra], axis=1), orth_ffn)
    table_sum = summed[:, width, : BUCKETS * H // 4]
    orth_attn = orthogonal(blocks_attn, summed[:, :width])
    small = jnp.concatenate([gain_terms.reshape(-1), table_sum.reshape(-1)])
    small = sum_line(jnp.pad(small, (0, -small.size % 1024)).reshape(-1, 128)).reshape(-1)
    gain_grad = small[: gain_terms.size].reshape(gain_terms.shape) / low(gains)
    table_sum = small[gain_terms.size : gain_terms.size + BUCKETS * H].reshape(BUCKETS, H)
    table_sum = table_sum[:, np.argsort(np.array(HEAD_ORDER))]
    table_grad = lax.dynamic_slice_in_dim(table_sum, here * heads_dev, heads_dev, axis=1)
    attn_in_next = attn_in * (1.0 - rate_attn_in * decay_rate) - rate_attn_in * orth_attn[:3]
    attn_out_next = attn_out * (1.0 - rate_attn_out * decay_rate) - rate_attn_out * orth_attn[3].T
    ffn_in_next = ffn_in * (1.0 - rate_ffn_in * decay_rate) - rate_ffn_in * orth_ffn[:2]
    ffn_out_next = ffn_out * (1.0 - rate_ffn_out * decay_rate) - rate_ffn_out * orth_ffn[2].T
    gain_first_next, gain_second_next, gains_next = adam_update(gains, gain_grad, gain_first, gain_second)
    table_first_next, table_second_next, table_next = adam_update(table, table_grad, table_first, table_second)
    return (
        output.reshape(tokens.shape),
        tokens_grad.reshape(tokens.shape),
        attn_in_next,
        attn_out_next,
        ffn_in_next,
        ffn_out_next,
        mom_in,
        mom_out_t.T,
        mom_fin,
        mom_fout_t.T,
        gain_first_next,
        gain_second_next,
        gains_next,
        table_first_next,
        table_second_next,
        table_next,
    )


def solution(mesh):
    token = P(None, ("dp", "mp"), None)
    columns = P(None, "dp", "mp")
    flipped = P("mp", "dp")
    gain = P(None, "dp")
    head = P(None, "mp")
    return jax.shard_map(
        shards,
        mesh=mesh,
        in_specs=(
            token, P(None, "dp"), token, columns, flipped, columns, flipped, gain, head,
            columns, flipped, columns, flipped, gain, gain, head, head,
        ),
        out_specs=(
            token, token, columns, flipped, columns, flipped, columns, flipped, columns, flipped,
            gain, gain, gain, head, head, head,
        ),
        check_vma=False,
    )
```

```python
import functools

import jax
import jax.numpy as jnp
import numpy as np
from jax import lax
from jax.experimental import pallas as pl
from jax.experimental.pallas import tpu as pltpu
from jax.sharding import PartitionSpec as P

D = 768
H = 12
DH = 64
BUCKETS = 32
LEN = 512
STEP = 8
QB = 128
SKEW = 1024
PAIRS = H // 2
TILE = 128
HEAD_ORDER = (0, 1, 3, 4, 6, 7, 9, 10, 2, 5, 8, 11)

epsilon = 1e-06
negative_fill = -1e30
momentum_decay = 0.95
decay_rate = 0.01
linear_coefficient = 3.4445
coef_second = -4.775
coef_third = 2.0315
rate_attn_in = 0.25
rate_attn_out = 12.0
rate_ffn_in = 0.6
rate_ffn_out = 0.3
beta_one = 0.9
beta_two = 0.95
adam_epsilon = 1e-08
adam_rate = 0.3
bucket_marks = (12, 16, 23, 32, 46, 64, 91)

HIGHEST = lax.Precision.HIGHEST
HIGH = lax.Precision.HIGH
bf16 = jnp.bfloat16
f32 = jnp.float32
NN = (((1,), (0,)), ((), ()))
NT = (((1,), (1,)), ((), ()))
TN = (((0,), (0,)), ((), ()))


VMEM_GRANT = 60 << 20
ANY = pl.BlockSpec(memory_space=pltpu.HBM)
SMEM = pl.BlockSpec(memory_space=pltpu.SMEM)
VMEM = pl.BlockSpec(memory_space=pltpu.VMEM)


def dot(a, b, dims=NN):
    return lax.dot_general(a, b, dims, preferred_element_type=f32)


def skew_onehot():
    place = np.arange(SKEW)
    relative = np.where(place < SKEW - QB + 1, place, place - SKEW) - (LEN - QB)
    distance = np.abs(relative)
    far = 8 + sum((distance >= mark).astype(np.int32) for mark in bucket_marks)
    bucket = np.where(distance < 8, distance, far) + 16 * (relative > 0)
    return (bucket[:, None] == np.arange(BUCKETS)[None, :]).astype(np.float32)


def cost(micros):
    return pl.CostEstimate(flops=int(micros * 3e8), bytes_accessed=0, transcendentals=0)


def half_lanes(shape, half):
    lane = lax.broadcasted_iota(jnp.int32, shape, 1)
    return (lane < DH) if half == 0 else (lane >= DH)


def bias_kernel(line_ref, bias_ref):
    for half in range(2):
        line = jnp.broadcast_to(line_ref[0, half : half + 1, :], (QB, SKEW))
        bias_ref[0, half] = pltpu.roll(line, 0, 1, stride=1, stride_axis=0).T


def make_bias(line):
    return pl.pallas_call(
        bias_kernel,
        grid=(PAIRS,),
        compiler_params=pltpu.CompilerParams(vmem_limit_bytes=VMEM_GRANT),
        in_specs=[pl.BlockSpec((1, 2, SKEW), lambda p: (p, 0, 0))],
        out_specs=pl.BlockSpec((1, 2, SKEW, QB), lambda p: (p, 0, 0, 0)),
        out_shape=jax.ShapeDtypeStruct((PAIRS, 2, SKEW, QB), f32),
        cost_estimate=cost(8),
        name="make_bias",
    )(line)


def diag_kernel(acc_ref, diag_ref):
    row = lax.broadcasted_iota(jnp.int32, (QB, QB), 0)
    lane = lax.broadcasted_iota(jnp.int32, (QB, QB), 1)
    flip = (row + lane == QB - 1).astype(f32)
    for half in range(2):
        turned = lax.dot_general(flip, acc_ref[0, half], NT, precision=HIGHEST, preferred_element_type=f32)
        shifted = pltpu.roll(turned, SKEW - QB + 1, 1, stride=1, stride_axis=0)
        diag_ref[0, half : half + 1, :] = jnp.sum(shifted, axis=0, keepdims=True)


def diagonals(acc):
    return pl.pallas_call(
        diag_kernel,
        grid=(PAIRS,),
        compiler_params=pltpu.CompilerParams(vmem_limit_bytes=VMEM_GRANT),
        in_specs=[pl.BlockSpec((1, 2, SKEW, QB), lambda p: (p, 0, 0, 0))],
        out_specs=pl.BlockSpec((1, 2, SKEW), lambda p: (p, 0, 0)),
        out_shape=jax.ShapeDtypeStruct((PAIRS, 2, SKEW), f32),
        cost_estimate=cost(1),
        name="diagonals",
    )(acc)


def both_heads(block):
    zero = jnp.zeros_like(block)
    return jnp.concatenate(
        [
            jnp.where(half_lanes(block.shape, 0), block, zero),
            jnp.where(half_lanes(block.shape, 1), block, zero),
        ],
        axis=0,
    )


def block_scores(meta, block, mb, keys, queries_two, bias_ref):
    start = pl.multiple_of((LEN - QB) - QB * meta[3 + block], QB)
    length = meta[6 + 2 * mb + meta[block]]
    bias = jnp.concatenate([bias_ref[0, 0, pl.ds(start, LEN), :], bias_ref[0, 1, pl.ds(start, LEN), :]], axis=1)
    scores = dot(keys, queries_two, NT) + bias
    row = lax.broadcasted_iota(jnp.int32, scores.shape, 0)
    return jnp.where(row < length, scores, negative_fill)


def block_rows(meta, block):
    return pl.ds(pl.multiple_of(meta[block] * LEN, LEN), LEN)


def one_of_two(pair):
    top = lax.broadcasted_iota(jnp.int32, (QB, QB), 0) < DH
    return jnp.where(top, pair[:, :QB], pair[:, QB:]).T


def attend_kernel(meta, q_ref, k_ref, v_ref, bias_ref, o_ref, lse_ref):
    mb = pl.program_id(1)
    blocks = range(q_ref.shape[1] // QB)
    scores, values = [], []
    for block in blocks:
        rows = block_rows(meta, block)
        values.append(v_ref[0, rows, :].T)
        queries_two = both_heads(q_ref[0, block * QB : (block + 1) * QB, :])
        scores.append(block_scores(meta, block, mb, k_ref[0, rows, :], queries_two, bias_ref))
    for block in blocks:
        top = jnp.max(scores[block], axis=0, keepdims=True)
        weights = jnp.exp(scores[block] - top)
        total = jnp.sum(weights, axis=0, keepdims=True)
        lse_ref[0, 0, block : block + 1, :] = top + jnp.log(total)
        out = one_of_two(dot(values[block], weights.astype(bf16)) / total)
        o_ref[0, block * QB : (block + 1) * QB, :] = out.astype(bf16)


def attend_back_kernel(
    meta, q_ref, k_ref, v_ref, do_ref, o_ref, lse_ref, bias_ref, dq_ref, dk_ref, dv_ref, acc_ref, dk_acc, dv_acc
):
    mb = pl.program_id(1)

    @pl.when(mb == 0)
    def _():
        acc_ref[...] = jnp.zeros_like(acc_ref)

    dk_acc[...] = jnp.zeros_like(dk_acc)
    dv_acc[...] = jnp.zeros_like(dv_acc)
    parts = []
    for block in range(q_ref.shape[1] // QB):
        rows = block_rows(meta, block)
        own = slice(block * QB, (block + 1) * QB)
        keys = k_ref[0, rows, :]
        grad = do_ref[0, own, :]
        queries_two, grad_two = both_heads(q_ref[0, own, :]), both_heads(grad)
        scores = block_scores(meta, block, mb, keys, queries_two, bias_ref)
        grad_soft = dot(v_ref[0, rows, :], grad_two, NT)
        inner = (grad.astype(f32) * o_ref[0, own, :].astype(f32)).T
        inner = jnp.concatenate(
            [jnp.sum(inner[:DH], axis=0, keepdims=True), jnp.sum(inner[DH:], axis=0, keepdims=True)], axis=1
        )
        parts.append((rows, own, keys, queries_two, grad_two, scores, grad_soft, inner))
    lows = []
    for block, (_, _, _, _, _, scores, grad_soft, inner) in enumerate(parts):
        soft = jnp.exp(scores - lse_ref[0, 0, block : block + 1, :])
        grad_scores = soft * (grad_soft - inner)
        start = pl.multiple_of((LEN - QB) - QB * meta[3 + block], QB)
        acc_ref[0, 0, pl.ds(start, LEN), :] += grad_scores[:, :QB]
        acc_ref[0, 1, pl.ds(start, LEN), :] += grad_scores[:, QB:]
        lows.append((soft.astype(bf16), grad_scores.astype(bf16)))
    for (rows, own, keys, queries_two, grad_two, _, _, _), (soft, grad_low) in zip(parts, lows):
        both = dot(jnp.concatenate([grad_low, soft], axis=0), jnp.concatenate([queries_two, grad_two], axis=1))
        dk_acc[rows, :] += both[:LEN, :QB]
        dv_acc[rows, :] += both[LEN:, QB:]
        dq_ref[0, own, :] = one_of_two(dot(keys.T, grad_low)).astype(bf16)
    dk_ref[0] = dk_acc[...].astype(bf16)
    dv_ref[0] = dv_acc[...].astype(bf16)


def attention_specs(rows, window):
    own = pl.BlockSpec((1, rows, QB), lambda p, m, _: (m, 0, p))
    wide = pl.BlockSpec((1, window, QB), lambda p, m, _: (m, 0, p))
    lines = pl.BlockSpec((1, 2, SKEW, QB), lambda p, m, _: (p, 0, 0, 0))
    stats = pl.BlockSpec((1, 1, 8, 2 * QB), lambda p, m, _: (m, p, 0, 0))
    return own, wide, lines, stats


def attend(meta, q, k, v, bias):
    micro, rows, _ = q.shape
    own, wide, lines, stats = attention_specs(rows, k.shape[1])
    return pl.pallas_call(
        attend_kernel,
        grid_spec=pltpu.PrefetchScalarGridSpec(
            num_scalar_prefetch=1,
            grid=(PAIRS, micro),
            in_specs=[own, wide, wide, lines],
            out_specs=[own, stats],
        ),
        out_shape=[
            jax.ShapeDtypeStruct(q.shape, bf16),
            jax.ShapeDtypeStruct((micro, PAIRS, 8, 2 * QB), f32),
        ],
        compiler_params=pltpu.CompilerParams(vmem_limit_bytes=VMEM_GRANT),
        cost_estimate=cost(17),
        name="attend",
    )(meta, q, k, v, bias)


def attend_back(meta, q, k, v, grad, out, stats, bias, after=()):
    micro, rows, _ = q.shape
    window = k.shape[1]
    own, wide, lines, lse = attention_specs(rows, window)
    kernel = lambda *refs: attend_back_kernel(*refs[:8], *refs[8 + len(after) :])
    return pl.pallas_call(
        kernel,
        grid_spec=pltpu.PrefetchScalarGridSpec(
            num_scalar_prefetch=1,
            grid=(PAIRS, micro),
            in_specs=[own, wide, wide, own, own, lse, lines] + [ANY] * len(after),
            out_specs=[own, wide, wide, lines],
            scratch_shapes=[pltpu.VMEM((window, QB), f32), pltpu.VMEM((window, QB), f32)],
        ),
        out_shape=[
            jax.ShapeDtypeStruct(q.shape, bf16),
            jax.ShapeDtypeStruct(k.shape, bf16),
            jax.ShapeDtypeStruct(k.shape, bf16),
            jax.ShapeDtypeStruct(bias.shape, f32),
        ],
        compiler_params=pltpu.CompilerParams(vmem_limit_bytes=VMEM_GRANT),
        cost_estimate=cost(24),
        name="attend_back",
    )(meta, q, k, v, grad, out, stats, bias, *after)


PARTS = 8
PART = D // PARTS


def part_rows(place, k):
    return pl.ds(pl.multiple_of((place[0] ^ k) * PART, PART), PART)


def entry_of(place, group):
    return lax.rem(group - place[1] + 4, 4)


def wait_for(ref, sem):
    pltpu.make_async_copy(ref, ref, sem).wait()


def lower_lanes(shape):
    return lax.broadcasted_iota(jnp.int32, shape, 1) < DH


def join_kernel(place, *refs):
    pieces, (w_ref, rest_ref, sems) = refs[:PARTS], refs[-3:]
    for group in range(4):
        entry = entry_of(place, group)
        for k, piece in enumerate(pieces):
            rows = part_rows(place, k)
            lanes = pl.ds(group * TILE, TILE)
            pltpu.make_async_copy(piece.at[entry, pl.ds(0, 4)], w_ref.at[:, rows, lanes], sems.at[0]).start()
            pltpu.make_async_copy(piece.at[entry, pl.ds(4, 2)], rest_ref.at[group, :, rows], sems.at[1]).start()
    wait_for(rest_ref, sems.at[1])
    lower = lower_lanes((D, TILE))
    for two in range(2):
        lanes = slice((4 + two) * TILE, (5 + two) * TILE)
        for both in range(2):
            even, odd = rest_ref[2 * two, both], rest_ref[2 * two + 1, both]
            w_ref[2 * both, :, lanes] = jnp.where(lower, even, odd)
            w_ref[2 * both + 1, :, lanes] = pltpu.roll(jnp.where(lower, odd, even).astype(f32), DH, 1).astype(bf16)
    wait_for(w_ref.at[:, :, pl.ds(0, 4 * TILE)], sems.at[0])


def join(place, pieces, later=()):
    return pl.pallas_call(
        join_kernel,
        in_specs=[SMEM] + [ANY] * (PARTS + len(later)),
        out_specs=VMEM,
        out_shape=jax.ShapeDtypeStruct((4, D, D), bf16),
        scratch_shapes=[pltpu.VMEM((4, 2, D, TILE), bf16), pltpu.SemaphoreType.DMA((2,))],
        compiler_params=pltpu.CompilerParams(vmem_limit_bytes=VMEM_GRANT),
        cost_estimate=cost(5),
        name="join",
    )(place, *pieces, *later)


PROJECT_STEPS = 2


def project_kernel(place, above, own_all, below, own_ref, gain_ref, w_ref, *refs):
    q_ref, k_ref, v_ref, n_ref, n_own_ref, x_ref, sems = refs
    mb, step = pl.program_id(0), pl.program_id(1)
    own_rows = own_all.shape[1]

    @pl.when((mb == 0) & (step == 0))
    def _():
        for m in range(own_all.shape[0]):
            for block in range(2 * LEN // QB):
                row = block * QB - place[2]
                for source, first, here in (
                    (above, row + own_rows, row < 0),
                    (own_all, row, (row >= 0) & (row < own_rows)),
                    (below, jnp.minimum(row - own_rows, own_rows - QB), row >= own_rows),
                ):

                    @pl.when(here)
                    def _():
                        rows = pl.ds(pl.multiple_of(first, QB), QB)
                        into = x_ref.at[m, pl.ds(block * QB, QB)]
                        pltpu.make_async_copy(source.at[m, rows], into, sems.at[m]).start()

    @pl.when(step == 0)
    def _():
        wait_for(x_ref.at[mb], sems.at[mb])

    def norm(rows):
        rows = rows.astype(f32)
        rho = lax.rsqrt(jnp.mean(rows * rows, axis=-1, keepdims=True) + epsilon)
        return (rows * rho * gain_ref[...]).astype(bf16)

    size = k_ref.shape[1]
    normed = norm(x_ref[mb, pl.ds(pl.multiple_of(step * size, size), size), :])
    n_ref[0] = normed
    k_ref[0] = dot(normed, w_ref[1]).astype(bf16)
    v_ref[0] = dot(normed, w_ref[2]).astype(bf16)
    normed = norm(own_ref[0])
    n_own_ref[0] = normed
    q_ref[0] = dot(normed, w_ref[0]).astype(bf16)


def project(place, sides, own, gain, weights):
    micro, own_rows, _ = own.shape
    rows, few = 2 * LEN // PROJECT_STEPS, own_rows // PROJECT_STEPS
    wide = pl.BlockSpec((1, rows, D), lambda m, t: (m, t, 0))
    small = pl.BlockSpec((1, few, D), lambda m, t: (m, t, 0))
    many_shape = jax.ShapeDtypeStruct((micro, 2 * LEN, D), bf16)
    few_shape = jax.ShapeDtypeStruct(own.shape, bf16)
    return pl.pallas_call(
        project_kernel,
        grid=(micro, PROJECT_STEPS),
        in_specs=[
            SMEM,
            ANY,
            ANY,
            ANY,
            small,
            pl.BlockSpec((1, D), lambda m, t: (0, 0)),
            pl.BlockSpec((3, D, D), lambda m, t: (0, 0, 0)),
        ],
        out_specs=[small, wide, wide, wide, small],
        out_shape=[few_shape, many_shape, many_shape, many_shape, few_shape],
        scratch_shapes=[pltpu.VMEM((micro, 2 * LEN, D), bf16), pltpu.SemaphoreType.DMA((micro,))],
        compiler_params=pltpu.CompilerParams(vmem_limit_bytes=VMEM_GRANT),
        cost_estimate=cost(12),
        name="project",
    )(place, sides[0], own, sides[1], own, gain, weights)


GRAD_STEPS = 4


def attn_grads_kernel(place, n_ref, dk_ref, dv_ref, own_ref, dq_ref, dh_ref, o_ref, even_ref, odd_ref, *scratch):
    acc_ref, main_ref, rest_ref, sems = scratch
    step = pl.program_id(0)

    @pl.when(step == 0)
    def _():
        acc_ref[...] = jnp.zeros_like(acc_ref)

    turned = n_ref[...].T
    acc_ref[1] += dot(turned, dk_ref[...])
    acc_ref[2] += dot(turned, dv_ref[...])

    @pl.when(step % 2 == 1)
    def _():
        acc_ref[0] += dot(own_ref[...].T, dq_ref[...])
        acc_ref[3] += dot(dh_ref[...].T, o_ref[...])

    @pl.when(step == GRAD_STEPS - 1)
    def _():
        lower = lower_lanes((D, TILE))
        for c in range(4):
            main_ref[c] = acc_ref[c, :, : 4 * TILE].astype(bf16)
        for group in range(4):
            entry = entry_of(place, group)
            for k in range(PARTS):
                part = (odd_ref if k % 2 else even_ref).at[k // 2, entry, pl.ds(0, 4)]
                source = main_ref.at[:, part_rows(place, k), pl.ds(group * TILE, TILE)]
                pltpu.make_async_copy(source, part, sems.at[0]).start()
        for two in range(2):
            lanes = slice((4 + two) * TILE, (5 + two) * TILE)
            for both in range(2):
                one = acc_ref[2 * both, :, lanes]
                other = pltpu.roll(acc_ref[2 * both + 1, :, lanes], DH, 1)
                rest_ref[2 * two, both] = jnp.where(lower, one, other).astype(bf16)
                rest_ref[2 * two + 1, both] = jnp.where(lower, other, one).astype(bf16)
        for group in range(4):
            entry = entry_of(place, group)
            for k in range(PARTS):
                part = (odd_ref if k % 2 else even_ref).at[k // 2, entry, pl.ds(4, 2)]
                source = rest_ref.at[group, :, part_rows(place, k)]
                pltpu.make_async_copy(source, part, sems.at[0]).start()
        wait_for(even_ref, sems.at[0])
        wait_for(odd_ref, sems.at[0])


def attn_grads(place, normed_window, dk, dv, normed_own, dq, dh, o):
    rows, few = dk.shape[0] // GRAD_STEPS, dq.shape[0] // (GRAD_STEPS // 2)
    wide = pl.BlockSpec((rows, D), lambda t: (t, 0))
    small = pl.BlockSpec((few, D), lambda t: (t // 2, 0))
    parts = jax.ShapeDtypeStruct((PARTS // 2, 4, 6, PART, TILE), bf16)
    return pl.pallas_call(
        attn_grads_kernel,
        grid=(GRAD_STEPS,),
        in_specs=[SMEM, wide, wide, wide, small, small, small, small],
        out_specs=[ANY] * 2,
        out_shape=[parts] * 2,
        scratch_shapes=[
            pltpu.VMEM((4, D, D), f32),
            pltpu.VMEM((4, D, 4 * TILE), bf16),
            pltpu.VMEM((4, 2, D, TILE), bf16),
            pltpu.SemaphoreType.DMA((1,)),
        ],
        compiler_params=pltpu.CompilerParams(vmem_limit_bytes=VMEM_GRANT),
        cost_estimate=cost(10),
        name="attn_grads",
    )(place, normed_window, dk, dv, normed_own, dq, dh, o)


def gelu_and_slope(gate):
    root = 0.7978845608028654
    cube = 0.044715
    square = gate * gate
    bend = jnp.tanh(root * gate * (1.0 + cube * square))
    half = 0.5 * (1.0 + bend)
    slope = half + 0.5 * gate * (1.0 - bend * bend) * (root * (1.0 + 3.0 * cube * square))
    return gate * half, slope


def ffn_kernel(place, o_ref, x_ref, dy_ref, wo_ref, gain_ref, all_w, *refs):
    out_ref, dy1_ref, dh1_ref = refs[:3]
    parts = (refs[3:5], refs[5:7])
    (w_ref, g_ref, y_ref, n_ref, nt_ref, dyt_ref, acc_ref, dn_ref, hid_ref, dgate_ref, dup_ref,
     out_held, dy1_held, dh1_held, w_sems, g_sems, out_sems) = refs[7:]
    width = w_ref.shape[2] // 3
    gate_cols, up_cols, down_cols = (slice(c * width, (c + 1) * width) for c in range(3))

    def load(entry):
        group = lax.rem(entry + place[1], 4)
        for k in range(PARTS):
            rows = pl.ds(k * PART, PART)
            pltpu.make_async_copy(all_w.at[k, group], w_ref.at[entry, rows], w_sems.at[entry]).start()

    load(0)
    y = x_ref[...].astype(f32) + dot(o_ref[...], wo_ref[...], NT)
    y_ref[...] = y
    rho = lax.rsqrt(jnp.mean(y * y, axis=-1, keepdims=True) + epsilon)
    normed = (y * rho * gain_ref[...]).astype(bf16)
    n_ref[...] = normed
    nt_ref[...] = normed.T
    dyt_ref[...] = dy_ref[...].T
    acc_ref[...] = y
    dn_ref[...] = jnp.zeros_like(dn_ref)
    for entry in range(1, 4):
        load(entry)

    def through(entry):
        wait_for(w_ref.at[entry], w_sems.at[entry])
        w = w_ref.at[entry]
        normed = n_ref[...]
        gate = dot(normed, w[:, gate_cols])
        up = dot(normed, w[:, up_cols])
        grad_hid = dot(dy_ref[...], w[:, down_cols])
        act, slope = gelu_and_slope(gate)
        hid = (act * up).astype(bf16)
        dgate = (grad_hid * up * slope).astype(bf16)
        dup = (grad_hid * act).astype(bf16)
        hid_ref[...] = hid
        dgate_ref[...] = dgate
        dup_ref[...] = dup
        acc_ref[...] += dot(hid, w[:, down_cols], NT)
        dn_ref[...] += dot(dgate, w[:, gate_cols], NT) + dot(dup, w[:, up_cols], NT)

    def grads(entry, slot, pair):
        g_ref[slot, :, gate_cols] = dot(nt_ref[...], dgate_ref[...]).astype(bf16)
        g_ref[slot, :, up_cols] = dot(nt_ref[...], dup_ref[...]).astype(bf16)
        g_ref[slot, :, down_cols] = dot(dyt_ref[...], hid_ref[...]).astype(bf16)
        for k in range(PARTS):
            part = parts[pair][k % 2].at[k // 2, slot]
            pltpu.make_async_copy(g_ref.at[slot, part_rows(place, k)], part, g_sems.at[slot]).start()

    def one_group(entry, _):
        through(entry)
        grads(entry, entry, 0)
        return 0

    lax.fori_loop(0, 2, one_group, 0)
    through(2)
    wait_for(g_ref.at[0], g_sems.at[0])
    grads(2, 0, 1)
    through(3)
    outs = [(out_held, out_ref), (dy1_held, dy1_ref), (dh1_held, dh1_ref)]
    out_held[...] = acc_ref[...].astype(bf16)
    scaled_y = y_ref[...]
    rho = lax.rsqrt(jnp.mean(scaled_y * scaled_y, axis=-1, keepdims=True) + epsilon)
    scaled_y = scaled_y * rho
    u = dn_ref[...] * gain_ref[...]
    inner = jnp.mean(u * scaled_y, axis=-1, keepdims=True)
    dy1 = dy_ref[...].astype(f32) + rho * (u - scaled_y * inner)
    dy1_held[...] = dy1
    dh1_held[...] = dy1.astype(bf16)
    copies = [pltpu.make_async_copy(held, ref, out_sems.at[j]) for j, (held, ref) in enumerate(outs)]
    for copy in copies:
        copy.start()
    wait_for(g_ref.at[1], g_sems.at[1])
    grads(3, 1, 1)
    for copy in copies:
        copy.wait()
    for slot in range(2):
        wait_for(g_ref.at[slot], g_sems.at[slot])


def ffn(place, attended, x, dy, w_o, gain, weights):
    tokens = x.shape[0]
    columns = weights.shape[3]
    wide = lambda dtype: jax.ShapeDtypeStruct((tokens, D), dtype)
    parts = jax.ShapeDtypeStruct((PARTS // 2, 2, PART, columns), bf16)
    scratch = lambda rows, width, dtype: pltpu.VMEM((rows, width), dtype)
    return pl.pallas_call(
        ffn_kernel,
        in_specs=[SMEM] + [VMEM] * 5 + [ANY],
        out_specs=[ANY] * 7,
        out_shape=[wide(bf16), wide(f32), wide(bf16)] + [parts] * 4,
        scratch_shapes=[
            pltpu.VMEM((4, D, columns), bf16),
            pltpu.VMEM((2, D, columns), bf16),
            scratch(tokens, D, f32),
            scratch(tokens, D, bf16),
            scratch(D, tokens, bf16),
            scratch(D, tokens, bf16),
            scratch(tokens, D, f32),
            scratch(tokens, D, f32),
            scratch(tokens, columns // 3, bf16),
            scratch(tokens, columns // 3, bf16),
            scratch(tokens, columns // 3, bf16),
            scratch(tokens, D, bf16),
            scratch(tokens, D, f32),
            scratch(tokens, D, bf16),
            pltpu.SemaphoreType.DMA((4,)),
            pltpu.SemaphoreType.DMA((2,)),
            pltpu.SemaphoreType.DMA((3,)),
        ],
        compiler_params=pltpu.CompilerParams(vmem_limit_bytes=VMEM_GRANT),
        cost_estimate=cost(32),
        name="ffn",
    )(place, attended, x, dy, w_o, gain, weights)


def grams_of(blocks):
    return jnp.einsum("our,ouw->orw", blocks, blocks, precision=HIGHEST)


def orthogonal(blocks, gram):
    total = jnp.trace(gram, axis1=1, axis2=2)[:, None, None]
    mul = functools.partial(jnp.einsum, "oij,ojk->oik", precision=HIGH)
    first = gram / total
    start = blocks * lax.rsqrt(total)
    eye = jnp.eye(gram.shape[1], dtype=f32)[None]
    step = linear_coefficient * eye + coef_second * first + coef_third * mul(first, first)
    second = mul(mul(first, step), step)
    once = mul(start, step)
    turn = mul(once, second)
    return linear_coefficient * once + coef_second * turn + coef_third * mul(turn, second)


def adam_update(param, grad, first, second):
    first_new = beta_one * first + (1.0 - beta_one) * grad
    second_new = beta_two * second + (1.0 - beta_two) * grad * grad
    corrected_first = first_new / (1.0 - beta_one**STEP)
    corrected_second = second_new / (1.0 - beta_two**STEP)
    return (
        first_new,
        second_new,
        param - adam_rate * corrected_first / (jnp.sqrt(corrected_second) + adam_epsilon),
    )


def direct():
    return lax.axis_size("dp") == PARTS and lax.axis_size("mp") == 4


def swap(x, bit):
    return lax.ppermute(x, "dp", [(j, j ^ bit) for j in range(lax.axis_size("dp"))])


def from_above(x, k):
    return lax.ppermute(x, "mp", [((j + k) % 4, j) for j in range(4)])


def to_above(x, k):
    return lax.ppermute(x, "mp", [(j, (j + k) % 4) for j in range(4)])


def behind(x, *others):
    return lax.optimization_barrier((x, others))[0]


def total(*terms):
    return sum(term.astype(f32) for term in terms)


def gather_all(shard):
    rows, columns = shard.shape
    whole = lax.all_gather(shard, ("dp", "mp"), axis=0, tiled=False)
    if rows == PART:
        return whole.reshape(PARTS, 4, PART, columns)
    whole = whole.reshape(-1, 4, rows, columns).transpose(1, 0, 2, 3).reshape(4, PARTS, PART, columns)
    return whole.transpose(1, 0, 2, 3)


def gather_pieces(shard):
    tiles, rows, _ = shard.shape
    if not direct():
        whole = lax.all_gather(shard, ("dp", "mp"), axis=0, tiled=False)
        whole = whole.reshape(PARTS, -1, 4, tiles, rows, TILE).transpose(0, 2, 3, 1, 4, 5)
        return list(whole.reshape(PARTS, 4, tiles, PART, TILE))
    own = jnp.stack([shard] + [from_above(shard, k) for k in (1, 2, 3)])
    return own


def spread_pieces(own, meanwhile):
    if not direct():
        return own
    along, across = behind((swap(own, 2), swap(own, 4)), meanwhile)
    far = jnp.concatenate([swap(along[:2], 4), swap(across[2:], 2)])
    even = [own, along, across, far]
    return [piece for here in even for piece in (here, swap(here, 1))]


def scatter_core(even, odd):
    return total(even, swap(odd, 1)).astype(bf16)


def scatter_plane(mine, meanwhile=()):
    others = behind((swap(mine[1], 2), swap(mine[2], 4), swap(mine[3], 6)), meanwhile)
    return total(mine[0], *others).astype(bf16)


def scatter_plain(even, odd, rows):
    whole = jnp.stack([even, odd], axis=1)
    whole = whole.reshape(PARTS, 4, -1, PART // rows, rows, whole.shape[-1])
    parts = whole.transpose(0, 3, 1, 2, 4, 5)
    parts = parts.reshape((-1,) + parts.shape[3:])
    return lax.psum_scatter(parts, ("dp", "mp"), scatter_dimension=0, tiled=False).astype(f32)


def gather_small(x, axis_name, axis):
    if not direct():
        return lax.all_gather(x, axis_name, axis=axis, tiled=True)
    here = lax.axis_index(axis_name)
    size = lax.axis_size(axis_name)
    bit = 1
    while bit < size:
        other = lax.ppermute(x, axis_name, [(j, j ^ bit) for j in range(size)])
        upper = (here & bit) != 0
        x = jnp.concatenate([jnp.where(upper, other, x), jnp.where(upper, x, other)], axis=axis)
        bit *= 2
    return x


def sum_line(x):
    if not direct():
        return lax.psum(x, "mp")
    return x + from_above(x, 1) + from_above(x, 2) + from_above(x, 3)


def sum_planes(x, meanwhile=()):
    if not direct():
        return lax.psum(x, "dp")
    odd = (lax.axis_index("dp") & 1) != 0
    low = lambda v: v.astype(bf16)
    mine = total(jnp.where(odd, x[2:], x[:2]), swap(low(jnp.where(odd, x[:2], x[2:])), 1))
    one, two = mine[0], mine[1]
    one, two = behind((total(one, swap(low(one), 2)), total(two, swap(low(two), 4))), meanwhile)
    one, two = total(one, swap(low(one), 4)), total(two, swap(low(two), 2))
    mine = low(jnp.stack([one, two]))
    other = swap(mine, 1)
    return jnp.concatenate([jnp.where(odd, other, mine), jnp.where(odd, mine, other)]).astype(f32)


def shards(
    tokens, lengths, cotangent, attn_in, attn_out, ffn_in, ffn_out, gains, table,
    attn_in_mom, attn_out_mom, ffn_in_mom, ffn_out_mom,
    gain_first, gain_second, table_first, table_second,
):
    micro, own_rows, _ = tokens.shape
    here = lax.axis_index("mp")
    n_mp = lax.axis_size("mp")
    width = attn_in.shape[2]
    heads_dev = table.shape[1]

    rows_dev = attn_in.shape[1]
    width_ffn = ffn_in.shape[2]
    index = jnp.stack([lax.axis_index("dp"), here]).astype(jnp.int32)
    place = index if direct() else jnp.zeros_like(index)
    odd_group = (here & 1) != 0

    ffn_low = jnp.concatenate([ffn_in[0], ffn_in[1], ffn_out.T], axis=1).astype(bf16)
    attn_low = [part.astype(bf16) for part in (attn_in[0], attn_in[1], attn_in[2], attn_out.T)]
    tails = [part[:, TILE:] for part in attn_low]
    beside = lambda one, two: jnp.where(
        odd_group, jnp.concatenate([two, one], axis=1), jnp.concatenate([one, two], axis=1)
    )
    attn_tiles = jnp.stack([part[:, :TILE] for part in attn_low] + [beside(*tails[:2]), beside(*tails[2:])])
    gain_low = gather_small(gains.astype(bf16), "dp", 1).astype(f32)
    table_all = gather_small(table, "mp", 1)[:, np.array(HEAD_ORDER)]
    onehot = skew_onehot()
    line = lax.dot_general(
        table_all, onehot, (((0,), (1,)), ((), ())), precision=HIGHEST, preferred_element_type=f32
    ).reshape(PAIRS, 2, SKEW)
    attn_own = behind(gather_pieces(attn_tiles), gain_low, line)
    halo, ffn_low = behind((tokens, ffn_low), attn_own)
    up, down = [(j, j + 1) for j in range(n_mp - 1)], [(j + 1, j) for j in range(n_mp - 1)]
    sides = (lax.ppermute(halo, "mp", up), lax.ppermute(halo, "mp", down))
    ffn_all = gather_all(ffn_low)
    bias = make_bias(behind(line, attn_own))
    attn_pieces = spread_pieces(attn_own, bias)
    weights = join(place, behind(attn_pieces, sides))
    w_q, w_k, w_v, w_o = weights

    first_row = own_rows * here
    first_doc = first_row // LEN
    inset = first_row - first_doc * LEN
    block_place = first_row // QB + jnp.arange(own_rows // QB, dtype=jnp.int32)
    slot = block_place // (LEN // QB) - first_doc
    lens_window = lax.dynamic_slice_in_dim(
        jnp.concatenate([lengths, jnp.ones((micro, 1), lengths.dtype)], axis=1), first_doc, 2, axis=1
    )
    meta = jnp.concatenate([slot, block_place % (LEN // QB), lens_window.reshape(-1)]).astype(jnp.int32)

    there = jnp.concatenate([place, inset[None].astype(jnp.int32)])
    q, k, v, normed_window, normed_own = project(there, sides, tokens, gain_low[0:1], weights)
    attended, stats = attend(meta, q, k, v, bias)
    out_seq = attended
    attended = attended.reshape(micro * own_rows, D)
    normed_window = normed_window.reshape(micro * 2 * LEN, D)
    normed_own = normed_own.reshape(micro * own_rows, D)

    dy = cotangent.reshape(micro * own_rows, D)
    output, grad_middle, grad_mid_low, even_one, odd_one, even_two, odd_two = ffn(
        place, attended, tokens.reshape(micro * own_rows, D), dy, w_o, gain_low[1:2], ffn_all
    )
    grad_att = dot(grad_mid_low, w_o).astype(bf16).reshape(micro, own_rows, D)
    back_args = (meta, q, k, v, grad_att, out_seq, stats, bias)
    if direct():
        mine_one, mine_two = scatter_core(even_one, odd_one), scatter_core(even_two, odd_two)
        grads = attend_back(*back_args, [mine_one, mine_two])
        line_one = scatter_plane(mine_one, grads)
        line_two = scatter_plane(behind(mine_two, line_one))
        sent_one = to_above(line_one[1], 1)
        grads = behind(grads, line_one)
    else:
        shard_ffn = scatter_plain(
            jnp.concatenate([even_one, even_two], axis=1), jnp.concatenate([odd_one, odd_two], axis=1), rows_dev
        )[0]
        grads = attend_back(*back_args)
    grad_q, grad_k, grad_v, grad_bias = grads
    grad_q = grad_q.reshape(micro * own_rows, D)
    grad_k = grad_k.reshape(micro * 2 * LEN, D)
    grad_v = grad_v.reshape(micro * 2 * LEN, D)
    even, odd = attn_grads(
        place, normed_window, grad_k, grad_v, normed_own, grad_q, grad_mid_low, attended
    )
    grad_q, grad_k, grad_v = behind((grad_q, grad_k, grad_v), even)
    grad_normed_own = dot(grad_q, w_q, NT)
    grad_normed_window = (dot(grad_k, w_k, NT) + dot(grad_v, w_v, NT)).reshape(micro, 2 * LEN, D)
    edge = ((0, 0), (own_rows, own_rows), (0, 0))
    sent = jnp.pad(grad_normed_window.astype(bf16), edge)
    back = lax.dynamic_slice_in_dim(sent, inset, own_rows, axis=1)
    forth = lax.dynamic_slice_in_dim(sent, inset + 2 * own_rows, own_rows, axis=1)
    own_part = lax.dynamic_slice_in_dim(grad_normed_window, inset, own_rows, axis=1)
    own_part = own_part.reshape(micro * own_rows, D) + grad_normed_own
    if direct():
        shard_ffn = total(line_one[0], sent_one, to_above(line_two[0], 2), to_above(line_two[1], 3))
        mine_attn = behind(scatter_core(even, odd), back, forth, shard_ffn)
        back, forth = behind((back, forth), mine_attn)
    else:
        mine_attn = even
    back, forth = lax.ppermute(back, "mp", down), lax.ppermute(forth, "mp", up)
    if direct():
        line_attn = scatter_plane(mine_attn, (back, forth))
        shard_attn = total(line_attn[0], *[to_above(line_attn[k], k) for k in (1, 2, 3)])
    else:
        line_attn = even
        shard_attn = scatter_plain(even, odd, rows_dev)
    grad_bias = behind(grad_bias, mine_attn)
    back, forth = behind((back, forth), shard_attn)
    grad_normed = own_part + (back.astype(f32) + forth.astype(f32)).reshape(micro * own_rows, D)
    rows = tokens.reshape(micro * own_rows, D).astype(f32)
    rho = lax.rsqrt(jnp.mean(rows * rows, axis=-1, keepdims=True) + epsilon)
    u = grad_normed * gain_low[0]
    tokens_grad = grad_middle + rho * (u - rows * rho * rho * jnp.mean(u * rows, axis=-1, keepdims=True))

    pick = lambda tile, second: jnp.where(odd_group ^ second, tile[:, DH:], tile[:, :DH])
    parts_attn = jnp.stack(
        [
            jnp.concatenate([shard_attn[c], pick(shard_attn[4 + c // 2], c % 2 == 1)], axis=1)
            for c in range(4)
        ]
    )
    parts_ffn = shard_ffn.reshape(rows_dev, 3, width_ffn).transpose(1, 0, 2)
    low = lambda v: v.astype(bf16).astype(f32)
    gain_terms = jnp.stack(
        [jnp.sum(low(attn_in) * parts_attn[:3], axis=(0, 2)), jnp.sum(low(ffn_in) * parts_ffn[:2], axis=(0, 2))]
    )
    mom_in = momentum_decay * attn_in_mom + parts_attn[:3]
    mom_out_t = momentum_decay * attn_out_mom.T + parts_attn[3]
    mom_fin = momentum_decay * ffn_in_mom + parts_ffn[:2]
    mom_fout_t = momentum_decay * ffn_out_mom.T + parts_ffn[2]
    blocks_attn = jnp.concatenate([mom_in, mom_out_t[None]])
    blocks_ffn = jnp.concatenate([mom_fin, mom_fout_t[None]])
    gram_ffn = behind(grams_of(blocks_ffn), line_attn)
    gram_ffn = sum_planes(gram_ffn.reshape(4, -1, width_ffn)).reshape(gram_ffn.shape)
    table_sum = lax.dot_general(
        onehot,
        diagonals(grad_bias).reshape(H, SKEW),
        (((0,), (1,)), ((), ())),
        precision=HIGHEST,
        preferred_element_type=f32,
    )
    gram_attn = grams_of(blocks_attn)
    gram_ffn = behind(gram_ffn, gram_attn)
    orth_ffn = orthogonal(blocks_ffn, gram_ffn)
    extra = jnp.pad(table_sum.reshape(4, 1, -1), ((0, 0), (0, 15), (0, width - BUCKETS * H // 4)))
    summed = sum_planes(jnp.concatenate([gram_attn, extra], axis=1), orth_ffn)
    table_sum = summed[:, width, : BUCKETS * H // 4]
    orth_attn = orthogonal(blocks_attn, summed[:, :width])
    small = jnp.concatenate([gain_terms.reshape(-1), table_sum.reshape(-1)])
    small = sum_line(jnp.pad(small, (0, -small.size % 1024)).reshape(-1, 128)).reshape(-1)
    gain_grad = small[: gain_terms.size].reshape(gain_terms.shape) / low(gains)
    table_sum = small[gain_terms.size : gain_terms.size + BUCKETS * H].reshape(BUCKETS, H)
    table_sum = table_sum[:, np.argsort(np.array(HEAD_ORDER))]
    table_grad = lax.dynamic_slice_in_dim(table_sum, here * heads_dev, heads_dev, axis=1)
    attn_in_next = attn_in * (1.0 - rate_attn_in * decay_rate) - rate_attn_in * orth_attn[:3]
    attn_out_next = attn_out * (1.0 - rate_attn_out * decay_rate) - rate_attn_out * orth_attn[3].T
    ffn_in_next = ffn_in * (1.0 - rate_ffn_in * decay_rate) - rate_ffn_in * orth_ffn[:2]
    ffn_out_next = ffn_out * (1.0 - rate_ffn_out * decay_rate) - rate_ffn_out * orth_ffn[2].T
    gain_first_next, gain_second_next, gains_next = adam_update(gains, gain_grad, gain_first, gain_second)
    table_first_next, table_second_next, table_next = adam_update(table, table_grad, table_first, table_second)
    return (
        output.reshape(tokens.shape),
        tokens_grad.reshape(tokens.shape),
        attn_in_next,
        attn_out_next,
        ffn_in_next,
        ffn_out_next,
        mom_in,
        mom_out_t.T,
        mom_fin,
        mom_fout_t.T,
        gain_first_next,
        gain_second_next,
        gains_next,
        table_first_next,
        table_second_next,
        table_next,
    )


def solution(mesh):
    token = P(None, ("dp", "mp"), None)
    columns = P(None, "dp", "mp")
    flipped = P("mp", "dp")
    gain = P(None, "dp")
    head = P(None, "mp")
    return jax.shard_map(
        shards,
        mesh=mesh,
        in_specs=(
            token, P(None, "dp"), token, columns, flipped, columns, flipped, gain, head,
            columns, flipped, columns, flipped, gain, gain, head, head,
        ),
        out_specs=(
            token, token, columns, flipped, columns, flipped, columns, flipped, columns, flipped,
            gain, gain, gain, head, head, head,
        ),
        check_vma=False,
    )
```

```python
import functools

import jax
import jax.numpy as jnp
import numpy as np
from jax import lax
from jax.experimental import pallas as pl
from jax.experimental.pallas import tpu as pltpu
from jax.sharding import PartitionSpec as P

D = 768
H = 12
DH = 64
BUCKETS = 32
LEN = 512
STEP = 8
QB = 128
SKEW = 1024
PAIRS = H // 2
TILE = 128
HEAD_ORDER = (0, 1, 3, 4, 6, 7, 9, 10, 2, 5, 8, 11)

epsilon = 1e-06
negative_fill = -1e30
momentum_decay = 0.95
decay_rate = 0.01
linear_coefficient = 3.4445
coef_second = -4.775
coef_third = 2.0315
rate_attn_in = 0.25
rate_attn_out = 12.0
rate_ffn_in = 0.6
rate_ffn_out = 0.3
beta_one = 0.9
beta_two = 0.95
adam_epsilon = 1e-08
adam_rate = 0.3
bucket_marks = (12, 16, 23, 32, 46, 64, 91)

HIGHEST = lax.Precision.HIGHEST
HIGH = lax.Precision.HIGH
bf16 = jnp.bfloat16
f32 = jnp.float32
NN = (((1,), (0,)), ((), ()))
NT = (((1,), (1,)), ((), ()))
TN = (((0,), (0,)), ((), ()))


VMEM_GRANT = 60 << 20
ANY = pl.BlockSpec(memory_space=pltpu.HBM)
SMEM = pl.BlockSpec(memory_space=pltpu.SMEM)
VMEM = pl.BlockSpec(memory_space=pltpu.VMEM)


def dot(a, b, dims=NN):
    return lax.dot_general(a, b, dims, preferred_element_type=f32)


def skew_onehot():
    place = np.arange(SKEW)
    relative = np.where(place < SKEW - QB + 1, place, place - SKEW) - (LEN - QB)
    distance = np.abs(relative)
    far = 8 + sum((distance >= mark).astype(np.int32) for mark in bucket_marks)
    bucket = np.where(distance < 8, distance, far) + 16 * (relative > 0)
    return (bucket[:, None] == np.arange(BUCKETS)[None, :]).astype(np.float32)


def cost(micros):
    return pl.CostEstimate(flops=int(micros * 1e7), bytes_accessed=0, transcendentals=0)


def half_lanes(shape, half):
    lane = lax.broadcasted_iota(jnp.int32, shape, 1)
    return (lane < DH) if half == 0 else (lane >= DH)


def bias_kernel(line_ref, bias_ref):
    for half in range(2):
        line = jnp.broadcast_to(line_ref[0, half : half + 1, :], (QB, SKEW))
        bias_ref[0, half] = pltpu.roll(line, 0, 1, stride=1, stride_axis=0).T


def make_bias(line):
    return pl.pallas_call(
        bias_kernel,
        grid=(PAIRS,),
        compiler_params=pltpu.CompilerParams(vmem_limit_bytes=VMEM_GRANT),
        in_specs=[pl.BlockSpec((1, 2, SKEW), lambda p: (p, 0, 0))],
        out_specs=pl.BlockSpec((1, 2, SKEW, QB), lambda p: (p, 0, 0, 0)),
        out_shape=jax.ShapeDtypeStruct((PAIRS, 2, SKEW, QB), f32),
        cost_estimate=cost(8),
        name="make_bias",
    )(line)


def diag_kernel(acc_ref, diag_ref):
    row = lax.broadcasted_iota(jnp.int32, (QB, QB), 0)
    lane = lax.broadcasted_iota(jnp.int32, (QB, QB), 1)
    flip = (row + lane == QB - 1).astype(f32)
    for half in range(2):
        turned = lax.dot_general(flip, acc_ref[0, half], NT, precision=HIGHEST, preferred_element_type=f32)
        shifted = pltpu.roll(turned, SKEW - QB + 1, 1, stride=1, stride_axis=0)
        diag_ref[0, half : half + 1, :] = jnp.sum(shifted, axis=0, keepdims=True)


def diagonals(acc):
    return pl.pallas_call(
        diag_kernel,
        grid=(PAIRS,),
        compiler_params=pltpu.CompilerParams(vmem_limit_bytes=VMEM_GRANT),
        in_specs=[pl.BlockSpec((1, 2, SKEW, QB), lambda p: (p, 0, 0, 0))],
        out_specs=pl.BlockSpec((1, 2, SKEW), lambda p: (p, 0, 0)),
        out_shape=jax.ShapeDtypeStruct((PAIRS, 2, SKEW), f32),
        cost_estimate=cost(1),
        name="diagonals",
    )(acc)


def both_heads(block):
    zero = jnp.zeros_like(block)
    return jnp.concatenate(
        [
            jnp.where(half_lanes(block.shape, 0), block, zero),
            jnp.where(half_lanes(block.shape, 1), block, zero),
        ],
        axis=0,
    )


def block_scores(meta, block, mb, keys, queries_two, bias_ref):
    start = pl.multiple_of((LEN - QB) - QB * meta[3 + block], QB)
    length = meta[6 + 2 * mb + meta[block]]
    bias = jnp.concatenate([bias_ref[0, 0, pl.ds(start, LEN), :], bias_ref[0, 1, pl.ds(start, LEN), :]], axis=1)
    scores = dot(keys, queries_two, NT) + bias
    row = lax.broadcasted_iota(jnp.int32, scores.shape, 0)
    return jnp.where(row < length, scores, negative_fill)


def block_rows(meta, block):
    return pl.ds(pl.multiple_of(meta[block] * LEN, LEN), LEN)


def one_of_two(pair):
    top = lax.broadcasted_iota(jnp.int32, (QB, QB), 0) < DH
    return jnp.where(top, pair[:, :QB], pair[:, QB:]).T


def attend_kernel(meta, q_ref, k_ref, v_ref, bias_ref, o_ref, lse_ref):
    mb = pl.program_id(1)
    blocks = range(q_ref.shape[1] // QB)
    scores, values = [], []
    for block in blocks:
        rows = block_rows(meta, block)
        values.append(v_ref[0, rows, :].T)
        queries_two = both_heads(q_ref[0, block * QB : (block + 1) * QB, :])
        scores.append(block_scores(meta, block, mb, k_ref[0, rows, :], queries_two, bias_ref))
    for block in blocks:
        top = jnp.max(scores[block], axis=0, keepdims=True)
        weights = jnp.exp(scores[block] - top)
        total = jnp.sum(weights, axis=0, keepdims=True)
        lse_ref[0, 0, block : block + 1, :] = top + jnp.log(total)
        out = one_of_two(dot(values[block], weights.astype(bf16)) / total)
        o_ref[0, block * QB : (block + 1) * QB, :] = out.astype(bf16)


def attend_back_kernel(
    meta, q_ref, k_ref, v_ref, do_ref, o_ref, lse_ref, bias_ref, dq_ref, dk_ref, dv_ref, acc_ref, dk_acc, dv_acc
):
    mb = pl.program_id(1)

    @pl.when(mb == 0)
    def _():
        acc_ref[...] = jnp.zeros_like(acc_ref)

    dk_acc[...] = jnp.zeros_like(dk_acc)
    dv_acc[...] = jnp.zeros_like(dv_acc)
    parts = []
    for block in range(q_ref.shape[1] // QB):
        rows = block_rows(meta, block)
        own = slice(block * QB, (block + 1) * QB)
        keys = k_ref[0, rows, :]
        grad = do_ref[0, own, :]
        queries_two, grad_two = both_heads(q_ref[0, own, :]), both_heads(grad)
        scores = block_scores(meta, block, mb, keys, queries_two, bias_ref)
        grad_soft = dot(v_ref[0, rows, :], grad_two, NT)
        inner = (grad.astype(f32) * o_ref[0, own, :].astype(f32)).T
        inner = jnp.concatenate(
            [jnp.sum(inner[:DH], axis=0, keepdims=True), jnp.sum(inner[DH:], axis=0, keepdims=True)], axis=1
        )
        parts.append((rows, own, keys, queries_two, grad_two, scores, grad_soft, inner))
    lows = []
    for block, (_, _, _, _, _, scores, grad_soft, inner) in enumerate(parts):
        soft = jnp.exp(scores - lse_ref[0, 0, block : block + 1, :])
        grad_scores = soft * (grad_soft - inner)
        start = pl.multiple_of((LEN - QB) - QB * meta[3 + block], QB)
        acc_ref[0, 0, pl.ds(start, LEN), :] += grad_scores[:, :QB]
        acc_ref[0, 1, pl.ds(start, LEN), :] += grad_scores[:, QB:]
        lows.append((soft.astype(bf16), grad_scores.astype(bf16)))
    for (rows, own, keys, queries_two, grad_two, _, _, _), (soft, grad_low) in zip(parts, lows):
        both = dot(jnp.concatenate([grad_low, soft], axis=0), jnp.concatenate([queries_two, grad_two], axis=1))
        dk_acc[rows, :] += both[:LEN, :QB]
        dv_acc[rows, :] += both[LEN:, QB:]
        dq_ref[0, own, :] = one_of_two(dot(keys.T, grad_low)).astype(bf16)
    dk_ref[0] = dk_acc[...].astype(bf16)
    dv_ref[0] = dv_acc[...].astype(bf16)


def attention_specs(rows, window):
    own = pl.BlockSpec((1, rows, QB), lambda p, m, _: (m, 0, p))
    wide = pl.BlockSpec((1, window, QB), lambda p, m, _: (m, 0, p))
    lines = pl.BlockSpec((1, 2, SKEW, QB), lambda p, m, _: (p, 0, 0, 0))
    stats = pl.BlockSpec((1, 1, 8, 2 * QB), lambda p, m, _: (m, p, 0, 0))
    return own, wide, lines, stats


def attend(meta, q, k, v, bias):
    micro, rows, _ = q.shape
    own, wide, lines, stats = attention_specs(rows, k.shape[1])
    return pl.pallas_call(
        attend_kernel,
        grid_spec=pltpu.PrefetchScalarGridSpec(
            num_scalar_prefetch=1,
            grid=(PAIRS, micro),
            in_specs=[own, wide, wide, lines],
            out_specs=[own, stats],
        ),
        out_shape=[
            jax.ShapeDtypeStruct(q.shape, bf16),
            jax.ShapeDtypeStruct((micro, PAIRS, 8, 2 * QB), f32),
        ],
        compiler_params=pltpu.CompilerParams(vmem_limit_bytes=VMEM_GRANT),
        cost_estimate=cost(17),
        name="attend",
    )(meta, q, k, v, bias)


def attend_back(meta, q, k, v, grad, out, stats, bias, after=()):
    micro, rows, _ = q.shape
    window = k.shape[1]
    own, wide, lines, lse = attention_specs(rows, window)
    kernel = lambda *refs: attend_back_kernel(*refs[:8], *refs[8 + len(after) :])
    return pl.pallas_call(
        kernel,
        grid_spec=pltpu.PrefetchScalarGridSpec(
            num_scalar_prefetch=1,
            grid=(PAIRS, micro),
            in_specs=[own, wide, wide, own, own, lse, lines] + [ANY] * len(after),
            out_specs=[own, wide, wide, lines],
            scratch_shapes=[pltpu.VMEM((window, QB), f32), pltpu.VMEM((window, QB), f32)],
        ),
        out_shape=[
            jax.ShapeDtypeStruct(q.shape, bf16),
            jax.ShapeDtypeStruct(k.shape, bf16),
            jax.ShapeDtypeStruct(k.shape, bf16),
            jax.ShapeDtypeStruct(bias.shape, f32),
        ],
        compiler_params=pltpu.CompilerParams(vmem_limit_bytes=VMEM_GRANT),
        cost_estimate=cost(24),
        name="attend_back",
    )(meta, q, k, v, grad, out, stats, bias, *after)


PARTS = 8
PART = D // PARTS


def part_rows(place, k):
    return pl.ds(pl.multiple_of((place[0] ^ k) * PART, PART), PART)


def entry_of(place, group):
    return lax.rem(group - place[1] + 4, 4)


def wait_for(ref, sem):
    pltpu.make_async_copy(ref, ref, sem).wait()


def lower_lanes(shape):
    return lax.broadcasted_iota(jnp.int32, shape, 1) < DH


PROJECT_STEPS = 2


def project_kernel(place, above, own_all, below, own_ref, gain_ref, *refs):
    pieces = refs[:PARTS]
    q_ref, k_ref, v_ref, n_ref, n_own_ref = refs[PARTS : PARTS + 5]
    w_refs = refs[PARTS + 5 : PARTS + 9]
    x_ref, rest_ref, sems, w_sems = refs[PARTS + 9 :]
    mb, step = pl.program_id(0), pl.program_id(1)
    own_rows = own_all.shape[1]

    @pl.when((mb == 0) & (step == 0))
    def _():
        for group in range(4):
            entry = entry_of(place, group)
            lanes = pl.ds(group * TILE, TILE)
            for k, piece in enumerate(pieces):
                rows = part_rows(place, k)
                pltpu.make_async_copy(piece.at[entry, pl.ds(4, 2)], rest_ref.at[group, :, rows], w_sems.at[4]).start()
                for c in range(4):
                    pltpu.make_async_copy(piece.at[entry, c], w_refs[c].at[rows, lanes], w_sems.at[c]).start()
        for m in range(own_all.shape[0]):
            for block in range(2 * LEN // QB):
                row = block * QB - place[2]
                for source, first, here in (
                    (above, row + own_rows, row < 0),
                    (own_all, row, (row >= 0) & (row < own_rows)),
                    (below, jnp.minimum(row - own_rows, own_rows - QB), row >= own_rows),
                ):

                    @pl.when(here)
                    def _():
                        rows = pl.ds(pl.multiple_of(first, QB), QB)
                        into = x_ref.at[m, pl.ds(block * QB, QB)]
                        pltpu.make_async_copy(source.at[m, rows], into, sems.at[m]).start()

        wait_for(rest_ref, w_sems.at[4])
        lower = lower_lanes((D, TILE))
        for two in range(2):
            lanes = slice((4 + two) * TILE, (5 + two) * TILE)
            for both in range(2):
                even, odd = rest_ref[2 * two, both], rest_ref[2 * two + 1, both]
                w_refs[2 * both][:, lanes] = jnp.where(lower, even, odd)
                turned = pltpu.roll(jnp.where(lower, odd, even).astype(f32), DH, 1)
                w_refs[2 * both + 1][:, lanes] = turned.astype(bf16)
        for c in range(4):
            wait_for(w_refs[c].at[:, pl.ds(0, 4 * TILE)], w_sems.at[c])

    @pl.when(step == 0)
    def _():
        wait_for(x_ref.at[mb], sems.at[mb])

    def norm(rows):
        rows = rows.astype(f32)
        rho = lax.rsqrt(jnp.mean(rows * rows, axis=-1, keepdims=True) + epsilon)
        return (rows * rho * gain_ref[...]).astype(bf16)

    size = k_ref.shape[1]
    normed = norm(x_ref[mb, pl.ds(pl.multiple_of(step * size, size), size), :])
    n_ref[0] = normed
    k_ref[0] = dot(normed, w_refs[1][...]).astype(bf16)
    v_ref[0] = dot(normed, w_refs[2][...]).astype(bf16)
    normed = norm(own_ref[0])
    n_own_ref[0] = normed
    q_ref[0] = dot(normed, w_refs[0][...]).astype(bf16)


def project(place, sides, own, gain, pieces):
    micro, own_rows, _ = own.shape
    rows, few = 2 * LEN // PROJECT_STEPS, own_rows // PROJECT_STEPS
    wide = pl.BlockSpec((1, rows, D), lambda m, t: (m, t, 0))
    small = pl.BlockSpec((1, few, D), lambda m, t: (m, t, 0))
    whole = pl.BlockSpec((D, D), lambda m, t: (0, 0))
    many_shape = jax.ShapeDtypeStruct((micro, 2 * LEN, D), bf16)
    few_shape = jax.ShapeDtypeStruct(own.shape, bf16)
    results = pl.pallas_call(
        project_kernel,
        grid=(micro, PROJECT_STEPS),
        in_specs=[SMEM, ANY, ANY, ANY, small, pl.BlockSpec((1, D), lambda m, t: (0, 0))] + [ANY] * PARTS,
        out_specs=[small, wide, wide, wide, small] + [whole] * 4,
        out_shape=[few_shape, many_shape, many_shape, many_shape, few_shape]
        + [jax.ShapeDtypeStruct((D, D), bf16)] * 4,
        scratch_shapes=[
            pltpu.VMEM((micro, 2 * LEN, D), bf16),
            pltpu.VMEM((4, 2, D, TILE), bf16),
            pltpu.SemaphoreType.DMA((micro,)),
            pltpu.SemaphoreType.DMA((5,)),
        ],
        compiler_params=pltpu.CompilerParams(vmem_limit_bytes=VMEM_GRANT),
        cost_estimate=cost(14),
        name="project",
    )(place, sides[0], own, sides[1], own, gain, *pieces)
    return results[:5], results[5:]


GRAD_STEPS = 4


def attn_grads_kernel(place, n_ref, dk_ref, dv_ref, own_ref, dq_ref, dh_ref, o_ref, even_ref, odd_ref, *scratch):
    acc_ref, main_ref, rest_ref, sems = scratch
    step = pl.program_id(0)

    @pl.when(step == 0)
    def _():
        acc_ref[...] = jnp.zeros_like(acc_ref)

    turned = n_ref[...].T
    acc_ref[1] += dot(turned, dk_ref[...])
    acc_ref[2] += dot(turned, dv_ref[...])

    @pl.when(step % 2 == 1)
    def _():
        acc_ref[0] += dot(own_ref[...].T, dq_ref[...])
        acc_ref[3] += dot(dh_ref[...].T, o_ref[...])

    @pl.when(step == GRAD_STEPS - 1)
    def _():
        lower = lower_lanes((D, TILE))
        for c in range(4):
            main_ref[c] = acc_ref[c, :, : 4 * TILE].astype(bf16)
        for group in range(4):
            entry = entry_of(place, group)
            for k in range(PARTS):
                part = (odd_ref if k % 2 else even_ref).at[k // 2, entry, pl.ds(0, 4)]
                source = main_ref.at[:, part_rows(place, k), pl.ds(group * TILE, TILE)]
                pltpu.make_async_copy(source, part, sems.at[0]).start()
        for two in range(2):
            lanes = slice((4 + two) * TILE, (5 + two) * TILE)
            for both in range(2):
                one = acc_ref[2 * both, :, lanes]
                other = pltpu.roll(acc_ref[2 * both + 1, :, lanes], DH, 1)
                rest_ref[2 * two, both] = jnp.where(lower, one, other).astype(bf16)
                rest_ref[2 * two + 1, both] = jnp.where(lower, other, one).astype(bf16)
        for group in range(4):
            entry = entry_of(place, group)
            for k in range(PARTS):
                part = (odd_ref if k % 2 else even_ref).at[k // 2, entry, pl.ds(4, 2)]
                source = rest_ref.at[group, :, part_rows(place, k)]
                pltpu.make_async_copy(source, part, sems.at[0]).start()
        wait_for(even_ref, sems.at[0])
        wait_for(odd_ref, sems.at[0])


def attn_grads(place, normed_window, dk, dv, normed_own, dq, dh, o):
    rows, few = dk.shape[0] // GRAD_STEPS, dq.shape[0] // (GRAD_STEPS // 2)
    wide = pl.BlockSpec((rows, D), lambda t: (t, 0))
    small = pl.BlockSpec((few, D), lambda t: (t // 2, 0))
    parts = jax.ShapeDtypeStruct((PARTS // 2, 4, 6, PART, TILE), bf16)
    return pl.pallas_call(
        attn_grads_kernel,
        grid=(GRAD_STEPS,),
        in_specs=[SMEM, wide, wide, wide, small, small, small, small],
        out_specs=[ANY] * 2,
        out_shape=[parts] * 2,
        scratch_shapes=[
            pltpu.VMEM((4, D, D), f32),
            pltpu.VMEM((4, D, 4 * TILE), bf16),
            pltpu.VMEM((4, 2, D, TILE), bf16),
            pltpu.SemaphoreType.DMA((1,)),
        ],
        compiler_params=pltpu.CompilerParams(vmem_limit_bytes=VMEM_GRANT),
        cost_estimate=cost(10),
        name="attn_grads",
    )(place, normed_window, dk, dv, normed_own, dq, dh, o)


def norm_grads_kernel(place, dk_ref, dv_ref, dq_ref, wk_ref, wv_ref, wq_ref, back_ref, own_ref, forth_ref, held_ref):
    own_rows = dq_ref.shape[1]
    held_ref[...] = dot(dk_ref[0], wk_ref[...], NT) + dot(dv_ref[0], wv_ref[...], NT)
    own_ref[0] = dot(dq_ref[0], wq_ref[...], NT)
    back_ref[...] = jnp.zeros_like(back_ref)
    forth_ref[...] = jnp.zeros_like(forth_ref)
    for block in range(2 * LEN // QB):
        row = block * QB - place[2]
        part = slice(block * QB, (block + 1) * QB)

        @pl.when(row < 0)
        def _():
            back_ref[0, pl.ds(pl.multiple_of(row + own_rows, QB), QB), :] = held_ref[part, :].astype(bf16)

        @pl.when((row >= 0) & (row < own_rows))
        def _():
            own_ref[0, pl.ds(pl.multiple_of(row, QB), QB), :] += held_ref[part, :]

        @pl.when((row >= own_rows) & (row < 2 * own_rows))
        def _():
            forth_ref[0, pl.ds(pl.multiple_of(row - own_rows, QB), QB), :] = held_ref[part, :].astype(bf16)


def norm_grads(place, dk, dv, dq, w_k, w_v, w_q):
    micro, own_rows, _ = dq.shape
    wide = pl.BlockSpec((1, 2 * LEN, D), lambda m: (m, 0, 0))
    small = pl.BlockSpec((1, own_rows, D), lambda m: (m, 0, 0))
    whole = pl.BlockSpec((D, D), lambda m: (0, 0))
    return pl.pallas_call(
        norm_grads_kernel,
        grid=(micro,),
        in_specs=[SMEM, wide, wide, small, whole, whole, whole],
        out_specs=[small] * 3,
        out_shape=[
            jax.ShapeDtypeStruct(dq.shape, bf16),
            jax.ShapeDtypeStruct(dq.shape, f32),
            jax.ShapeDtypeStruct(dq.shape, bf16),
        ],
        scratch_shapes=[pltpu.VMEM((2 * LEN, D), f32)],
        compiler_params=pltpu.CompilerParams(vmem_limit_bytes=VMEM_GRANT),
        cost_estimate=cost(10),
        name="norm_grads",
    )(place, dk, dv, dq, w_k, w_v, w_q)


def gelu_and_slope(gate):
    root = 0.7978845608028654
    cube = 0.044715
    square = gate * gate
    bend = jnp.tanh(root * gate * (1.0 + cube * square))
    half = 0.5 * (1.0 + bend)
    slope = half + 0.5 * gate * (1.0 - bend * bend) * (root * (1.0 + 3.0 * cube * square))
    return gate * half, slope


def ffn_kernel(place, o_ref, x_ref, dy_ref, wo_ref, gain_ref, all_w, *refs):
    out_ref, dy1_ref, dh1_ref = refs[:3]
    parts = (refs[3:5], refs[5:7])
    (w_ref, g_ref, y_ref, n_ref, nt_ref, dyt_ref, acc_ref, dn_ref, hid_ref, dgate_ref, dup_ref,
     out_held, dy1_held, dh1_held, w_sems, g_sems, out_sems) = refs[7:]
    width = w_ref.shape[2] // 3
    gate_cols, up_cols, down_cols = (slice(c * width, (c + 1) * width) for c in range(3))

    def load(entry):
        group = lax.rem(entry + place[1], 4)
        for k in range(PARTS):
            rows = pl.ds(k * PART, PART)
            pltpu.make_async_copy(all_w.at[k, group], w_ref.at[entry, rows], w_sems.at[entry]).start()

    load(0)
    y = x_ref[...].astype(f32) + dot(o_ref[...], wo_ref[...], NT)
    y_ref[...] = y
    rho = lax.rsqrt(jnp.mean(y * y, axis=-1, keepdims=True) + epsilon)
    normed = (y * rho * gain_ref[...]).astype(bf16)
    n_ref[...] = normed
    nt_ref[...] = normed.T
    dyt_ref[...] = dy_ref[...].T
    acc_ref[...] = y
    dn_ref[...] = jnp.zeros_like(dn_ref)
    for entry in range(1, 4):
        load(entry)

    def through(entry):
        wait_for(w_ref.at[entry], w_sems.at[entry])
        w = w_ref.at[entry]
        normed = n_ref[...]
        gate = dot(normed, w[:, gate_cols])
        up = dot(normed, w[:, up_cols])
        grad_hid = dot(dy_ref[...], w[:, down_cols])
        act, slope = gelu_and_slope(gate)
        hid = (act * up).astype(bf16)
        dgate = (grad_hid * up * slope).astype(bf16)
        dup = (grad_hid * act).astype(bf16)
        hid_ref[...] = hid
        dgate_ref[...] = dgate
        dup_ref[...] = dup
        acc_ref[...] += dot(hid, w[:, down_cols], NT)
        dn_ref[...] += dot(dgate, w[:, gate_cols], NT) + dot(dup, w[:, up_cols], NT)

    def grads(entry, slot, pair):
        g_ref[slot, :, gate_cols] = dot(nt_ref[...], dgate_ref[...]).astype(bf16)
        g_ref[slot, :, up_cols] = dot(nt_ref[...], dup_ref[...]).astype(bf16)
        g_ref[slot, :, down_cols] = dot(dyt_ref[...], hid_ref[...]).astype(bf16)
        for k in range(PARTS):
            part = parts[pair][k % 2].at[k // 2, slot]
            pltpu.make_async_copy(g_ref.at[slot, part_rows(place, k)], part, g_sems.at[slot]).start()

    def one_group(entry, _):
        through(entry)
        grads(entry, entry, 0)
        return 0

    lax.fori_loop(0, 2, one_group, 0)
    through(2)
    wait_for(g_ref.at[0], g_sems.at[0])
    grads(2, 0, 1)
    through(3)
    outs = [(out_held, out_ref), (dy1_held, dy1_ref), (dh1_held, dh1_ref)]
    out_held[...] = acc_ref[...].astype(bf16)
    scaled_y = y_ref[...]
    rho = lax.rsqrt(jnp.mean(scaled_y * scaled_y, axis=-1, keepdims=True) + epsilon)
    scaled_y = scaled_y * rho
    u = dn_ref[...] * gain_ref[...]
    inner = jnp.mean(u * scaled_y, axis=-1, keepdims=True)
    dy1 = dy_ref[...].astype(f32) + rho * (u - scaled_y * inner)
    dy1_held[...] = dy1
    dh1_held[...] = dy1.astype(bf16)
    copies = [pltpu.make_async_copy(held, ref, out_sems.at[j]) for j, (held, ref) in enumerate(outs)]
    for copy in copies:
        copy.start()
    wait_for(g_ref.at[1], g_sems.at[1])
    grads(3, 1, 1)
    for copy in copies:
        copy.wait()
    for slot in range(2):
        wait_for(g_ref.at[slot], g_sems.at[slot])


def ffn(place, attended, x, dy, w_o, gain, weights):
    tokens = x.shape[0]
    columns = weights.shape[3]
    wide = lambda dtype: jax.ShapeDtypeStruct((tokens, D), dtype)
    parts = jax.ShapeDtypeStruct((PARTS // 2, 2, PART, columns), bf16)
    scratch = lambda rows, width, dtype: pltpu.VMEM((rows, width), dtype)
    return pl.pallas_call(
        ffn_kernel,
        in_specs=[SMEM] + [VMEM] * 5 + [ANY],
        out_specs=[ANY] * 7,
        out_shape=[wide(bf16), wide(f32), wide(bf16)] + [parts] * 4,
        scratch_shapes=[
            pltpu.VMEM((4, D, columns), bf16),
            pltpu.VMEM((2, D, columns), bf16),
            scratch(tokens, D, f32),
            scratch(tokens, D, bf16),
            scratch(D, tokens, bf16),
            scratch(D, tokens, bf16),
            scratch(tokens, D, f32),
            scratch(tokens, D, f32),
            scratch(tokens, columns // 3, bf16),
            scratch(tokens, columns // 3, bf16),
            scratch(tokens, columns // 3, bf16),
            scratch(tokens, D, bf16),
            scratch(tokens, D, f32),
            scratch(tokens, D, bf16),
            pltpu.SemaphoreType.DMA((4,)),
            pltpu.SemaphoreType.DMA((2,)),
            pltpu.SemaphoreType.DMA((3,)),
        ],
        compiler_params=pltpu.CompilerParams(vmem_limit_bytes=VMEM_GRANT),
        cost_estimate=cost(32),
        name="ffn",
    )(place, attended, x, dy, w_o, gain, weights)


def grams_of(blocks):
    return jnp.einsum("our,ouw->orw", blocks, blocks, precision=HIGHEST)


def dot_three(a, b):
    parts = []
    for v in (a, b):
        high = v.astype(bf16)
        parts.append((high, (v - high.astype(f32)).astype(bf16)))
    (a_high, a_low), (b_high, b_low) = parts
    return dot(a_high, b_high) + (dot(a_high, b_low) + dot(a_low, b_high))


def muon_kernel(rates, gram_ref, mom_ref, in_ref, out_ref, in_next, out_next):
    width = mom_ref.shape[2]
    for c, rate in enumerate(rates):
        gram = gram_ref[c, :width]
        row = lax.broadcasted_iota(jnp.int32, gram.shape, 0)
        eye = (row == lax.broadcasted_iota(jnp.int32, gram.shape, 1)).astype(f32)
        whole = jnp.sum(jnp.sum(gram * eye, axis=0, keepdims=True), axis=1, keepdims=True)
        first = gram / whole
        start = mom_ref[c] * lax.rsqrt(whole)
        step = linear_coefficient * eye + coef_second * first + coef_third * dot_three(first, first)
        second = dot_three(dot_three(first, step), step)
        once = dot_three(start, step)
        turn = dot_three(once, second)
        both = rate * (linear_coefficient * once + coef_second * turn + coef_third * dot_three(turn, second))
        if c < len(rates) - 1:
            in_next[c] = in_ref[c] * (1.0 - rate * decay_rate) - both
        else:
            out_next[...] = out_ref[...] * (1.0 - rate * decay_rate) - both.T


def muon(rates, gram, moms, in_param, out_param):
    return pl.pallas_call(
        functools.partial(muon_kernel, rates),
        in_specs=[VMEM] * 4,
        out_specs=[VMEM] * 2,
        out_shape=[jax.ShapeDtypeStruct(in_param.shape, f32), jax.ShapeDtypeStruct(out_param.shape, f32)],
        compiler_params=pltpu.CompilerParams(vmem_limit_bytes=VMEM_GRANT),
        cost_estimate=cost(8),
        name="muon",
    )(gram, moms, in_param, out_param)


def attn_momentum_kernel(place, *refs):
    count = len(refs) - 9
    terms, (in_mom, out_mom, in_ref, extra_ref) = refs[:count], refs[count : count + 4]
    mom_in_ref, mom_out_ref, gram_ref, gain_ref, flat_ref = refs[count + 4 :]
    tiles = [sum(term[c].astype(f32) for term in terms) for c in range(6)]
    gain = 0.0
    for c in range(4):
        tail = tiles[4 + c // 2]
        other = pltpu.roll(tail, DH, 1)
        swapped = (place[1] + c) % 2 == 1
        tail = jnp.where(swapped, other, tail)[:, :DH]
        grad = jnp.concatenate([tiles[c], tail], axis=1)
        if c < 3:
            gain += jnp.sum(in_ref[c].astype(bf16).astype(f32) * grad, axis=1, keepdims=True)
            mom = momentum_decay * in_mom[c] + grad
            mom_in_ref[c] = mom
        else:
            mom = momentum_decay * out_mom[...].T + grad
            mom_out_ref[...] = mom.T
        flat_ref[c] = mom
        gram_ref[c, : mom.shape[1]] = lax.dot_general(mom, mom, TN, precision=HIGHEST, preferred_element_type=f32)
        gram_ref[c, mom.shape[1] :] = extra_ref[c]
    gain_ref[...] = gain


def attn_momentum(place, terms, in_mom, out_mom, attn_in, extra):
    _, rows, width = in_mom.shape
    operands = [*terms, in_mom, out_mom, attn_in, extra]
    shape = lambda *dims: jax.ShapeDtypeStruct(dims, f32)
    return pl.pallas_call(
        attn_momentum_kernel,
        in_specs=[SMEM] + [VMEM] * len(operands),
        out_specs=[VMEM] * 5,
        out_shape=[
            shape(3, rows, width),
            shape(width, rows),
            shape(4, width + extra.shape[1], width),
            shape(rows, 1),
            shape(4, rows, width),
        ],
        compiler_params=pltpu.CompilerParams(vmem_limit_bytes=VMEM_GRANT),
        cost_estimate=cost(4),
        name="attn_momentum",
    )(place, *operands)


def ffn_momentum_kernel(*refs):
    count = len(refs) - 8
    terms, (in_mom, out_mom, in_ref) = refs[:count], refs[count : count + 3]
    mom_in_ref, mom_out_ref, gram_ref, gain_ref, flat_ref = refs[count + 3 :]
    width = in_mom.shape[2]
    gain = 0.0
    for c in range(3):
        grad = sum(term[:, c * width : (c + 1) * width].astype(f32) for term in terms)
        if c < 2:
            gain += jnp.sum(in_ref[c].astype(bf16).astype(f32) * grad, axis=1, keepdims=True)
            mom = momentum_decay * in_mom[c] + grad
            mom_in_ref[c] = mom
        else:
            mom = momentum_decay * out_mom[...].T + grad
            mom_out_ref[...] = mom.T
        flat_ref[c] = mom
        gram_ref[c] = lax.dot_general(mom, mom, TN, precision=HIGHEST, preferred_element_type=f32)
    gain_ref[...] = gain


def ffn_momentum(terms, in_mom, out_mom, ffn_in):
    _, rows, width = in_mom.shape
    operands = [*terms, in_mom, out_mom, ffn_in]
    shape = lambda *dims: jax.ShapeDtypeStruct(dims, f32)
    return pl.pallas_call(
        ffn_momentum_kernel,
        in_specs=[VMEM] * len(operands),
        out_specs=[VMEM] * 5,
        out_shape=[
            shape(2, rows, width),
            shape(width, rows),
            shape(3, width, width),
            shape(rows, 1),
            shape(3, rows, width),
        ],
        compiler_params=pltpu.CompilerParams(vmem_limit_bytes=VMEM_GRANT),
        cost_estimate=cost(5),
        name="ffn_momentum",
    )(*operands)


def adam_update(param, grad, first, second):
    first_new = beta_one * first + (1.0 - beta_one) * grad
    second_new = beta_two * second + (1.0 - beta_two) * grad * grad
    corrected_first = first_new / (1.0 - beta_one**STEP)
    corrected_second = second_new / (1.0 - beta_two**STEP)
    return (
        first_new,
        second_new,
        param - adam_rate * corrected_first / (jnp.sqrt(corrected_second) + adam_epsilon),
    )


def direct():
    return lax.axis_size("dp") == PARTS and lax.axis_size("mp") == 4


def swap(x, bit):
    return lax.ppermute(x, "dp", [(j, j ^ bit) for j in range(lax.axis_size("dp"))])


def from_above(x, k):
    return lax.ppermute(x, "mp", [((j + k) % 4, j) for j in range(4)])


def to_above(x, k):
    return lax.ppermute(x, "mp", [(j, (j + k) % 4) for j in range(4)])


def behind(x, *others):
    return lax.optimization_barrier((x, others))[0]


def total(*terms):
    return sum(term.astype(f32) for term in terms)


def gather_all(shard):
    rows, columns = shard.shape
    whole = lax.all_gather(shard, ("dp", "mp"), axis=0, tiled=False)
    if rows == PART:
        return whole.reshape(PARTS, 4, PART, columns)
    whole = whole.reshape(-1, 4, rows, columns).transpose(1, 0, 2, 3).reshape(4, PARTS, PART, columns)
    return whole.transpose(1, 0, 2, 3)


def gather_pieces(shard):
    tiles, rows, _ = shard.shape
    if not direct():
        whole = lax.all_gather(shard, ("dp", "mp"), axis=0, tiled=False)
        whole = whole.reshape(PARTS, -1, 4, tiles, rows, TILE).transpose(0, 2, 3, 1, 4, 5)
        return list(whole.reshape(PARTS, 4, tiles, PART, TILE))
    own = jnp.stack([shard] + [from_above(shard, k) for k in (1, 2, 3)])
    return own


def spread_pieces(own, meanwhile):
    if not direct():
        return own
    others = behind([swap(own, bit) for bit in (2, 4, 6)], meanwhile)
    return [piece for here in (own, *others) for piece in (here, swap(here, 1))]


def scatter_core(even, odd):
    return total(even, swap(odd, 1)).astype(bf16)


def send_plane(mine):
    return [swap(mine[1], 2), swap(mine[2], 4), swap(mine[3], 6)]


def send_line(line):
    return [to_above(line[k], k) for k in (1, 2, 3)]


def plain_order(even, odd):
    return jnp.stack([even, odd], axis=1).reshape((PARTS,) + even.shape[1:])


def scatter_plain(parts, rows):
    groups, columns = parts.shape[2], parts.shape[-1]
    parts = parts.reshape(PARTS, 4, groups, PART // rows, rows, columns).transpose(0, 3, 1, 2, 4, 5)
    parts = parts.reshape((-1,) + parts.shape[3:])
    return lax.psum_scatter(parts, ("dp", "mp"), scatter_dimension=0, tiled=False)


def gather_small(x, axis_name, axis):
    if not direct():
        return lax.all_gather(x, axis_name, axis=axis, tiled=True)
    here = lax.axis_index(axis_name)
    size = lax.axis_size(axis_name)
    bit = 1
    while bit < size:
        other = lax.ppermute(x, axis_name, [(j, j ^ bit) for j in range(size)])
        upper = (here & bit) != 0
        x = jnp.concatenate([jnp.where(upper, other, x), jnp.where(upper, x, other)], axis=axis)
        bit *= 2
    return x


def sum_line(x):
    if not direct():
        return lax.psum(x, "mp")
    return x + from_above(x, 1) + from_above(x, 2) + from_above(x, 3)


def to_low(x):
    return x.astype(bf16)


def split_core(x):
    odd = (lax.axis_index("dp") & 1) != 0
    return jnp.where(odd, x[2:], x[:2]), to_low(jnp.where(odd, x[:2], x[2:]))


def sum_core(mine, other, meanwhile):
    return total(mine, behind(swap(other, 1), meanwhile))


def sum_first(pair, meanwhile):
    others = behind((swap(to_low(pair[0]), 2), swap(to_low(pair[1]), 4)), meanwhile)
    return total(pair[0], others[0]), total(pair[1], others[1])


def sum_second(pair, meanwhile):
    others = behind((swap(to_low(pair[0]), 4), swap(to_low(pair[1]), 2)), meanwhile)
    return total(pair[0], others[0]), total(pair[1], others[1])


def sum_last(pair, meanwhile):
    odd = (lax.axis_index("dp") & 1) != 0
    mine = to_low(jnp.stack(pair))
    other = behind(swap(mine, 1), meanwhile)
    return jnp.concatenate([jnp.where(odd, other, mine), jnp.where(odd, mine, other)]).astype(f32)


def shards(
    tokens, lengths, cotangent, attn_in, attn_out, ffn_in, ffn_out, gains, table,
    attn_in_mom, attn_out_mom, ffn_in_mom, ffn_out_mom,
    gain_first, gain_second, table_first, table_second,
):
    micro, own_rows, _ = tokens.shape
    here = lax.axis_index("mp")
    n_mp = lax.axis_size("mp")
    width = attn_in.shape[2]
    heads_dev = table.shape[1]

    rows_dev = attn_in.shape[1]
    width_ffn = ffn_in.shape[2]
    index = jnp.stack([lax.axis_index("dp"), here]).astype(jnp.int32)
    place = index if direct() else jnp.zeros_like(index)
    odd_group = (here & 1) != 0

    ffn_low = jnp.concatenate([ffn_in[0], ffn_in[1], ffn_out.T], axis=1).astype(bf16)
    attn_low = [part.astype(bf16) for part in (attn_in[0], attn_in[1], attn_in[2], attn_out.T)]
    tails = [part[:, TILE:] for part in attn_low]
    beside = lambda one, two: jnp.where(
        odd_group, jnp.concatenate([two, one], axis=1), jnp.concatenate([one, two], axis=1)
    )
    attn_tiles = jnp.stack([part[:, :TILE] for part in attn_low] + [beside(*tails[:2]), beside(*tails[2:])])
    gain_low = gather_small(gains.astype(bf16), "dp", 1).astype(f32)
    table_all = gather_small(table, "mp", 1)[:, np.array(HEAD_ORDER)]
    onehot = skew_onehot()
    line = lax.dot_general(
        table_all, onehot, (((0,), (1,)), ((), ())), precision=HIGHEST, preferred_element_type=f32
    ).reshape(PAIRS, 2, SKEW)
    ffn_all = gather_all(ffn_low)
    attn_own = gather_pieces(attn_tiles)
    halo = behind(tokens, attn_own)
    up, down = [(j, j + 1) for j in range(n_mp - 1)], [(j + 1, j) for j in range(n_mp - 1)]
    sides = (lax.ppermute(halo, "mp", up), lax.ppermute(halo, "mp", down))
    bias = make_bias(behind(line, attn_own))
    attn_pieces = spread_pieces(attn_own, (bias, gain_low, sides))

    first_row = own_rows * here
    first_doc = first_row // LEN
    inset = first_row - first_doc * LEN
    block_place = first_row // QB + jnp.arange(own_rows // QB, dtype=jnp.int32)
    slot = block_place // (LEN // QB) - first_doc
    lens_window = lax.dynamic_slice_in_dim(
        jnp.concatenate([lengths, jnp.ones((micro, 1), lengths.dtype)], axis=1), first_doc, 2, axis=1
    )
    meta = jnp.concatenate([slot, block_place % (LEN // QB), lens_window.reshape(-1)]).astype(jnp.int32)

    there = jnp.concatenate([place, inset[None].astype(jnp.int32)])
    projected, (w_q, w_k, w_v, w_o) = project(there, sides, tokens, gain_low[0:1], attn_pieces)
    q, k, v, normed_window, normed_own = projected
    attended, stats = attend(meta, q, k, v, bias)
    out_seq = attended
    attended = attended.reshape(micro * own_rows, D)
    normed_window = normed_window.reshape(micro * 2 * LEN, D)
    normed_own = normed_own.reshape(micro * own_rows, D)

    dy = cotangent.reshape(micro * own_rows, D)
    output, grad_middle, grad_mid_low, even_one, odd_one, even_two, odd_two = ffn(
        place, attended, tokens.reshape(micro * own_rows, D), dy, w_o, gain_low[1:2], ffn_all
    )
    grad_att = dot(grad_mid_low, w_o).astype(bf16).reshape(micro, own_rows, D)
    back_args = (meta, q, k, v, grad_att, out_seq, stats, bias)
    if direct():
        mine_one, mine_two = scatter_core(even_one, odd_one), scatter_core(even_two, odd_two)
        plane_one = send_plane(mine_one)
        grads = attend_back(*back_args, [mine_one, mine_two])
        line_one = total(mine_one[0], *behind(plane_one, grads)).astype(bf16)
        plane_two = send_plane(behind(mine_two, line_one))
        grads = behind(grads, line_one)
    else:
        even_ffn = jnp.concatenate([even_one, even_two], axis=1)
        odd_ffn = jnp.concatenate([odd_one, odd_two], axis=1)
        shard_ffn = scatter_plain(plain_order(even_ffn, odd_ffn)[:, :, None], rows_dev)[0].astype(f32)
        grads = attend_back(*back_args)
    grad_q, grad_k, grad_v, grad_bias = grads
    grad_q = grad_q.reshape(micro * own_rows, D)
    grad_k = grad_k.reshape(micro * 2 * LEN, D)
    grad_v = grad_v.reshape(micro * 2 * LEN, D)
    even, odd = attn_grads(
        place, normed_window, grad_k, grad_v, normed_own, grad_q, grad_mid_low, attended
    )
    if direct():
        diag = diagonals(behind(grad_bias, even))
        line_two = total(mine_two[0], *behind(plane_two, diag)).astype(bf16)
        mine_attn = scatter_core(even, behind(odd, line_two))
        plane_attn = send_plane(mine_attn)
        sent_ffn = [to_above(line_one[1], 1), to_above(line_two[0], 2), to_above(line_two[1], 3)]
        grad_q, grad_k, grad_v = behind((grad_q, grad_k, grad_v), mine_attn)
    else:
        diag = diagonals(grad_bias)
    back, own_part, forth = norm_grads(
        there,
        grad_k.reshape(micro, 2 * LEN, D),
        grad_v.reshape(micro, 2 * LEN, D),
        grad_q.reshape(micro, own_rows, D),
        w_k,
        w_v,
        w_q,
    )
    own_part = own_part.reshape(micro * own_rows, D)
    table_sum = lax.dot_general(
        onehot,
        diag.reshape(H, SKEW),
        (((0,), (1,)), ((), ())),
        precision=HIGHEST,
        preferred_element_type=f32,
    )
    low = lambda v: v.astype(bf16).astype(f32)
    extra = jnp.pad(table_sum.reshape(4, 1, -1), ((0, 0), (0, 15), (0, width - BUCKETS * H // 4)))
    if direct():
        line_attn = total(mine_attn[0], *behind(plane_attn, (extra, back, forth, own_part))).astype(bf16)
        sent_ffn = behind(sent_ffn, line_attn)
        line_attn = behind(line_attn, sent_ffn)
        terms = [line_one[0], *sent_ffn]
    else:
        terms = [shard_ffn]
    mom_fin, mom_fout, gram_ffn, gain_ffn, blocks_ffn = ffn_momentum(terms, ffn_in_mom, ffn_out_mom, ffn_in)
    flat_ffn = gram_ffn.reshape(4, -1, width_ffn)
    if direct():
        split_ffn = split_core(flat_ffn)
        core_ffn = sum_core(*split_ffn, ())
        terms = [line_attn[0], *behind(send_line(line_attn), gram_ffn)]
    else:
        terms = [scatter_plain(plain_order(even, odd), rows_dev)]
    mom_in, mom_out, gram_attn, gain_attn, blocks_attn = attn_momentum(
        index, terms, attn_in_mom, attn_out_mom, attn_in, extra
    )
    fin_blocks = lambda gram: muon(
        [rate_ffn_in] * 2 + [rate_ffn_out],
        gram.reshape(3, width_ffn, width_ffn),
        blocks_ffn,
        ffn_in,
        ffn_out,
    )
    if direct():
        mine, other = split_core(gram_attn)
        first_ffn = sum_first(core_ffn, mine)
        second_ffn = sum_second(first_ffn, ())
        core_attn = sum_core(mine, other, second_ffn)
        ffn_in_next, ffn_out_next = fin_blocks(sum_last(second_ffn, core_attn))
        back, forth = behind((back, forth), core_attn)
        back, forth = lax.ppermute(back, "mp", down), lax.ppermute(forth, "mp", up)
        first_attn = sum_first(core_attn, (ffn_in_next, back, forth))
        second_attn = sum_second(first_attn, ())
    else:
        second_attn = ()
        back, forth = lax.ppermute(back, "mp", down), lax.ppermute(forth, "mp", up)
        ffn_in_next, ffn_out_next = fin_blocks(lax.psum(flat_ffn, "dp"))
        summed = lax.psum(gram_attn, "dp")
    own_part, back, forth = behind((own_part, back, forth), second_attn)
    grad_normed = own_part + (back.astype(f32) + forth.astype(f32)).reshape(micro * own_rows, D)
    rows = tokens.reshape(micro * own_rows, D).astype(f32)
    rho = lax.rsqrt(jnp.mean(rows * rows, axis=-1, keepdims=True) + epsilon)
    u = grad_normed * gain_low[0]
    tokens_grad = grad_middle + rho * (u - rows * rho * rho * jnp.mean(u * rows, axis=-1, keepdims=True))
    if direct():
        summed = sum_last(second_attn, tokens_grad)
    table_sum = summed[:, width, : BUCKETS * H // 4]
    gain_terms = jnp.stack([gain_attn[:, 0], gain_ffn[:, 0]])
    small = jnp.concatenate([gain_terms.reshape(-1), table_sum.reshape(-1)])
    small = sum_line(jnp.pad(small, (0, -small.size % 1024)).reshape(-1, 128)).reshape(-1)
    gain_grad = small[: gain_terms.size].reshape(gain_terms.shape) / low(gains)
    table_sum = small[gain_terms.size : gain_terms.size + BUCKETS * H].reshape(BUCKETS, H)
    table_sum = table_sum[:, np.argsort(np.array(HEAD_ORDER))]
    table_grad = lax.dynamic_slice_in_dim(table_sum, here * heads_dev, heads_dev, axis=1)
    attn_in_next, attn_out_next = muon(
        [rate_attn_in] * 3 + [rate_attn_out], summed, blocks_attn, attn_in, attn_out
    )
    gain_first_next, gain_second_next, gains_next = adam_update(gains, gain_grad, gain_first, gain_second)
    table_first_next, table_second_next, table_next = adam_update(table, table_grad, table_first, table_second)
    return (
        output.reshape(tokens.shape),
        tokens_grad.reshape(tokens.shape),
        attn_in_next,
        attn_out_next,
        ffn_in_next,
        ffn_out_next,
        mom_in,
        mom_out,
        mom_fin,
        mom_fout,
        gain_first_next,
        gain_second_next,
        gains_next,
        table_first_next,
        table_second_next,
        table_next,
    )


def solution(mesh):
    token = P(None, ("dp", "mp"), None)
    columns = P(None, "dp", "mp")
    flipped = P("mp", "dp")
    gain = P(None, "dp")
    head = P(None, "mp")
    return jax.shard_map(
        shards,
        mesh=mesh,
        in_specs=(
            token, P(None, "dp"), token, columns, flipped, columns, flipped, gain, head,
            columns, flipped, columns, flipped, gain, gain, head, head,
        ),
        out_specs=(
            token, token, columns, flipped, columns, flipped, columns, flipped, columns, flipped,
            gain, gain, gain, head, head, head,
        ),
        check_vma=False,
    )
```

```python
import functools

import jax
import jax.numpy as jnp
import numpy as np
from jax import lax
from jax.experimental import pallas as pl
from jax.experimental.pallas import tpu as pltpu
from jax.sharding import PartitionSpec as P

D = 768
H = 12
DH = 64
BUCKETS = 32
LEN = 512
STEP = 8
QB = 128
SKEW = 1024
PAIRS = H // 2
TILE = 128
HEAD_ORDER = (0, 1, 3, 4, 6, 7, 9, 10, 2, 5, 8, 11)

epsilon = 1e-06
negative_fill = -1e30
momentum_decay = 0.95
decay_rate = 0.01
linear_coefficient = 3.4445
coef_second = -4.775
coef_third = 2.0315
rate_attn_in = 0.25
rate_attn_out = 12.0
rate_ffn_in = 0.6
rate_ffn_out = 0.3
beta_one = 0.9
beta_two = 0.95
adam_epsilon = 1e-08
adam_rate = 0.3
bucket_marks = (12, 16, 23, 32, 46, 64, 91)

HIGHEST = lax.Precision.HIGHEST
HIGH = lax.Precision.HIGH
bf16 = jnp.bfloat16
f32 = jnp.float32
NN = (((1,), (0,)), ((), ()))
NT = (((1,), (1,)), ((), ()))
TN = (((0,), (0,)), ((), ()))


VMEM_GRANT = 60 << 20
ANY = pl.BlockSpec(memory_space=pltpu.HBM)
SMEM = pl.BlockSpec(memory_space=pltpu.SMEM)
VMEM = pl.BlockSpec(memory_space=pltpu.VMEM)


def dot(a, b, dims=NN):
    return lax.dot_general(a, b, dims, preferred_element_type=f32)


def skew_onehot():
    place = np.arange(SKEW)
    relative = np.where(place < SKEW - QB + 1, place, place - SKEW) - (LEN - QB)
    distance = np.abs(relative)
    far = 8 + sum((distance >= mark).astype(np.int32) for mark in bucket_marks)
    bucket = np.where(distance < 8, distance, far) + 16 * (relative > 0)
    return (bucket[:, None] == np.arange(BUCKETS)[None, :]).astype(np.float32)


def cost(micros):
    return pl.CostEstimate(flops=int(micros * 1e7), bytes_accessed=0, transcendentals=0)


def half_lanes(shape, half):
    lane = lax.broadcasted_iota(jnp.int32, shape, 1)
    return (lane < DH) if half == 0 else (lane >= DH)


def bias_kernel(line_ref, bias_ref):
    for half in range(2):
        line = jnp.broadcast_to(line_ref[0, half : half + 1, :], (QB, SKEW))
        bias_ref[0, half] = pltpu.roll(line, 0, 1, stride=1, stride_axis=0).T


def make_bias(line):
    return pl.pallas_call(
        bias_kernel,
        grid=(PAIRS,),
        compiler_params=pltpu.CompilerParams(vmem_limit_bytes=VMEM_GRANT),
        in_specs=[pl.BlockSpec((1, 2, SKEW), lambda p: (p, 0, 0))],
        out_specs=pl.BlockSpec((1, 2, SKEW, QB), lambda p: (p, 0, 0, 0)),
        out_shape=jax.ShapeDtypeStruct((PAIRS, 2, SKEW, QB), f32),
        cost_estimate=cost(8),
        name="make_bias",
    )(line)


def diag_kernel(acc_ref, diag_ref):
    row = lax.broadcasted_iota(jnp.int32, (QB, QB), 0)
    lane = lax.broadcasted_iota(jnp.int32, (QB, QB), 1)
    flip = (row + lane == QB - 1).astype(f32)
    for half in range(2):
        turned = lax.dot_general(flip, acc_ref[0, half], NT, precision=HIGHEST, preferred_element_type=f32)
        shifted = pltpu.roll(turned, SKEW - QB + 1, 1, stride=1, stride_axis=0)
        diag_ref[0, half : half + 1, :] = jnp.sum(shifted, axis=0, keepdims=True)


def diagonals(acc):
    return pl.pallas_call(
        diag_kernel,
        grid=(PAIRS,),
        compiler_params=pltpu.CompilerParams(vmem_limit_bytes=VMEM_GRANT),
        in_specs=[pl.BlockSpec((1, 2, SKEW, QB), lambda p: (p, 0, 0, 0))],
        out_specs=pl.BlockSpec((1, 2, SKEW), lambda p: (p, 0, 0)),
        out_shape=jax.ShapeDtypeStruct((PAIRS, 2, SKEW), f32),
        cost_estimate=cost(1),
        name="diagonals",
    )(acc)


def both_heads(block):
    zero = jnp.zeros_like(block)
    return jnp.concatenate(
        [
            jnp.where(half_lanes(block.shape, 0), block, zero),
            jnp.where(half_lanes(block.shape, 1), block, zero),
        ],
        axis=0,
    )


def block_scores(meta, block, mb, keys, queries_two, bias_ref):
    start = pl.multiple_of((LEN - QB) - QB * meta[3 + block], QB)
    length = meta[6 + 2 * mb + meta[block]]
    bias = jnp.concatenate([bias_ref[0, 0, pl.ds(start, LEN), :], bias_ref[0, 1, pl.ds(start, LEN), :]], axis=1)
    scores = dot(keys, queries_two, NT) + bias
    row = lax.broadcasted_iota(jnp.int32, scores.shape, 0)
    return jnp.where(row < length, scores, negative_fill)


def block_rows(meta, block):
    return pl.ds(pl.multiple_of(meta[block] * LEN, LEN), LEN)


def one_of_two(pair):
    top = lax.broadcasted_iota(jnp.int32, (QB, QB), 0) < DH
    return jnp.where(top, pair[:, :QB], pair[:, QB:]).T


def attend_kernel(meta, q_ref, k_ref, v_ref, bias_ref, o_ref, lse_ref):
    mb = pl.program_id(1)
    blocks = range(q_ref.shape[1] // QB)
    scores, values = [], []
    for block in blocks:
        rows = block_rows(meta, block)
        values.append(v_ref[0, rows, :].T)
        queries_two = both_heads(q_ref[0, block * QB : (block + 1) * QB, :])
        scores.append(block_scores(meta, block, mb, k_ref[0, rows, :], queries_two, bias_ref))
    for block in blocks:
        top = jnp.max(scores[block], axis=0, keepdims=True)
        weights = jnp.exp(scores[block] - top)
        total = jnp.sum(weights, axis=0, keepdims=True)
        lse_ref[0, 0, block : block + 1, :] = top + jnp.log(total)
        out = one_of_two(dot(values[block], weights.astype(bf16)) / total)
        o_ref[0, block * QB : (block + 1) * QB, :] = out.astype(bf16)


def attend_back_kernel(
    meta, q_ref, k_ref, v_ref, do_ref, o_ref, lse_ref, bias_ref, dq_ref, dk_ref, dv_ref, acc_ref, dk_acc, dv_acc
):
    mb = pl.program_id(1)

    @pl.when(mb == 0)
    def _():
        acc_ref[...] = jnp.zeros_like(acc_ref)

    dk_acc[...] = jnp.zeros_like(dk_acc)
    dv_acc[...] = jnp.zeros_like(dv_acc)
    parts = []
    for block in range(q_ref.shape[1] // QB):
        rows = block_rows(meta, block)
        own = slice(block * QB, (block + 1) * QB)
        keys = k_ref[0, rows, :]
        grad = do_ref[0, own, :]
        queries_two, grad_two = both_heads(q_ref[0, own, :]), both_heads(grad)
        scores = block_scores(meta, block, mb, keys, queries_two, bias_ref)
        grad_soft = dot(v_ref[0, rows, :], grad_two, NT)
        inner = (grad.astype(f32) * o_ref[0, own, :].astype(f32)).T
        inner = jnp.concatenate(
            [jnp.sum(inner[:DH], axis=0, keepdims=True), jnp.sum(inner[DH:], axis=0, keepdims=True)], axis=1
        )
        parts.append((rows, own, keys, queries_two, grad_two, scores, grad_soft, inner))
    lows = []
    for block, (_, _, _, _, _, scores, grad_soft, inner) in enumerate(parts):
        soft = jnp.exp(scores - lse_ref[0, 0, block : block + 1, :])
        grad_scores = soft * (grad_soft - inner)
        start = pl.multiple_of((LEN - QB) - QB * meta[3 + block], QB)
        acc_ref[0, 0, pl.ds(start, LEN), :] += grad_scores[:, :QB]
        acc_ref[0, 1, pl.ds(start, LEN), :] += grad_scores[:, QB:]
        lows.append((soft.astype(bf16), grad_scores.astype(bf16)))
    for (rows, own, keys, queries_two, grad_two, _, _, _), (soft, grad_low) in zip(parts, lows):
        both = dot(jnp.concatenate([grad_low, soft], axis=0), jnp.concatenate([queries_two, grad_two], axis=1))
        dk_acc[rows, :] += both[:LEN, :QB]
        dv_acc[rows, :] += both[LEN:, QB:]
        dq_ref[0, own, :] = one_of_two(dot(keys.T, grad_low)).astype(bf16)
    dk_ref[0] = dk_acc[...].astype(bf16)
    dv_ref[0] = dv_acc[...].astype(bf16)


def attention_specs(rows, window):
    own = pl.BlockSpec((1, rows, QB), lambda p, m, _: (m, 0, p))
    wide = pl.BlockSpec((1, window, QB), lambda p, m, _: (m, 0, p))
    lines = pl.BlockSpec((1, 2, SKEW, QB), lambda p, m, _: (p, 0, 0, 0))
    stats = pl.BlockSpec((1, 1, 8, 2 * QB), lambda p, m, _: (m, p, 0, 0))
    return own, wide, lines, stats


def attend(meta, q, k, v, bias):
    micro, rows, _ = q.shape
    own, wide, lines, stats = attention_specs(rows, k.shape[1])
    return pl.pallas_call(
        attend_kernel,
        grid_spec=pltpu.PrefetchScalarGridSpec(
            num_scalar_prefetch=1,
            grid=(PAIRS, micro),
            in_specs=[own, wide, wide, lines],
            out_specs=[own, stats],
        ),
        out_shape=[
            jax.ShapeDtypeStruct(q.shape, bf16),
            jax.ShapeDtypeStruct((micro, PAIRS, 8, 2 * QB), f32),
        ],
        compiler_params=pltpu.CompilerParams(vmem_limit_bytes=VMEM_GRANT),
        cost_estimate=cost(17),
        name="attend",
    )(meta, q, k, v, bias)


def attend_back(meta, q, k, v, grad, out, stats, bias, after=()):
    micro, rows, _ = q.shape
    window = k.shape[1]
    own, wide, lines, lse = attention_specs(rows, window)
    kernel = lambda *refs: attend_back_kernel(*refs[:8], *refs[8 + len(after) :])
    return pl.pallas_call(
        kernel,
        grid_spec=pltpu.PrefetchScalarGridSpec(
            num_scalar_prefetch=1,
            grid=(PAIRS, micro),
            in_specs=[own, wide, wide, own, own, lse, lines] + [ANY] * len(after),
            out_specs=[own, wide, wide, lines],
            scratch_shapes=[pltpu.VMEM((window, QB), f32), pltpu.VMEM((window, QB), f32)],
        ),
        out_shape=[
            jax.ShapeDtypeStruct(q.shape, bf16),
            jax.ShapeDtypeStruct(k.shape, bf16),
            jax.ShapeDtypeStruct(k.shape, bf16),
            jax.ShapeDtypeStruct(bias.shape, f32),
        ],
        compiler_params=pltpu.CompilerParams(vmem_limit_bytes=VMEM_GRANT),
        cost_estimate=cost(24),
        name="attend_back",
    )(meta, q, k, v, grad, out, stats, bias, *after)


PARTS = 8
PART = D // PARTS


def part_rows(place, k):
    return pl.ds(pl.multiple_of((place[0] ^ k) * PART, PART), PART)


def entry_of(place, group):
    return lax.rem(group - place[1] + 4, 4)


def wait_for(ref, sem):
    pltpu.make_async_copy(ref, ref, sem).wait()


def lower_lanes(shape):
    return lax.broadcasted_iota(jnp.int32, shape, 1) < DH


PROJECT_STEPS = 2


def project_kernel(place, above, own_all, below, own_ref, gain_ref, *refs):
    pieces = refs[:PARTS]
    q_ref, k_ref, v_ref, n_ref, n_own_ref = refs[PARTS : PARTS + 5]
    w_refs = refs[PARTS + 5 : PARTS + 9]
    x_ref, rest_ref, sems, w_sems = refs[PARTS + 9 :]
    mb, step = pl.program_id(0), pl.program_id(1)
    own_rows = own_all.shape[1]

    @pl.when((mb == 0) & (step == 0))
    def _():
        for group in range(4):
            entry = entry_of(place, group)
            lanes = pl.ds(group * TILE, TILE)
            for k, piece in enumerate(pieces):
                rows = part_rows(place, k)
                pltpu.make_async_copy(piece.at[entry, pl.ds(4, 2)], rest_ref.at[group, :, rows], w_sems.at[4]).start()
                for c in range(4):
                    pltpu.make_async_copy(piece.at[entry, c], w_refs[c].at[rows, lanes], w_sems.at[c]).start()
        for m in range(own_all.shape[0]):
            for block in range(2 * LEN // QB):
                row = block * QB - place[2]
                for source, first, here in (
                    (above, row + own_rows, row < 0),
                    (own_all, row, (row >= 0) & (row < own_rows)),
                    (below, jnp.minimum(row - own_rows, own_rows - QB), row >= own_rows),
                ):

                    @pl.when(here)
                    def _():
                        rows = pl.ds(pl.multiple_of(first, QB), QB)
                        into = x_ref.at[m, pl.ds(block * QB, QB)]
                        pltpu.make_async_copy(source.at[m, rows], into, sems.at[m]).start()

        wait_for(rest_ref, w_sems.at[4])
        lower = lower_lanes((D, TILE))
        for two in range(2):
            lanes = slice((4 + two) * TILE, (5 + two) * TILE)
            for both in range(2):
                even, odd = rest_ref[2 * two, both], rest_ref[2 * two + 1, both]
                w_refs[2 * both][:, lanes] = jnp.where(lower, even, odd)
                turned = pltpu.roll(jnp.where(lower, odd, even).astype(f32), DH, 1)
                w_refs[2 * both + 1][:, lanes] = turned.astype(bf16)
        for c in range(4):
            wait_for(w_refs[c].at[:, pl.ds(0, 4 * TILE)], w_sems.at[c])

    @pl.when(step == 0)
    def _():
        wait_for(x_ref.at[mb], sems.at[mb])

    def norm(rows):
        rows = rows.astype(f32)
        rho = lax.rsqrt(jnp.mean(rows * rows, axis=-1, keepdims=True) + epsilon)
        return (rows * rho * gain_ref[...]).astype(bf16)

    size = k_ref.shape[1]
    normed = norm(x_ref[mb, pl.ds(pl.multiple_of(step * size, size), size), :])
    n_ref[0] = normed
    k_ref[0] = dot(normed, w_refs[1][...]).astype(bf16)
    v_ref[0] = dot(normed, w_refs[2][...]).astype(bf16)
    normed = norm(own_ref[0])
    n_own_ref[0] = normed
    q_ref[0] = dot(normed, w_refs[0][...]).astype(bf16)


def project(place, sides, own, gain, pieces):
    micro, own_rows, _ = own.shape
    rows, few = 2 * LEN // PROJECT_STEPS, own_rows // PROJECT_STEPS
    wide = pl.BlockSpec((1, rows, D), lambda m, t: (m, t, 0))
    small = pl.BlockSpec((1, few, D), lambda m, t: (m, t, 0))
    whole = pl.BlockSpec((D, D), lambda m, t: (0, 0))
    many_shape = jax.ShapeDtypeStruct((micro, 2 * LEN, D), bf16)
    few_shape = jax.ShapeDtypeStruct(own.shape, bf16)
    results = pl.pallas_call(
        project_kernel,
        grid=(micro, PROJECT_STEPS),
        in_specs=[SMEM, ANY, ANY, ANY, small, pl.BlockSpec((1, D), lambda m, t: (0, 0))] + [ANY] * PARTS,
        out_specs=[small, wide, wide, wide, small] + [whole] * 4,
        out_shape=[few_shape, many_shape, many_shape, many_shape, few_shape]
        + [jax.ShapeDtypeStruct((D, D), bf16)] * 4,
        scratch_shapes=[
            pltpu.VMEM((micro, 2 * LEN, D), bf16),
            pltpu.VMEM((4, 2, D, TILE), bf16),
            pltpu.SemaphoreType.DMA((micro,)),
            pltpu.SemaphoreType.DMA((5,)),
        ],
        compiler_params=pltpu.CompilerParams(vmem_limit_bytes=VMEM_GRANT),
        cost_estimate=cost(14),
        name="project",
    )(place, sides[0], own, sides[1], own, gain, *pieces)
    return results[:5], results[5:]


GRAD_STEPS = 4


def attn_grads_kernel(place, n_ref, dk_ref, dv_ref, own_ref, dq_ref, dh_ref, o_ref, even_ref, odd_ref, *scratch):
    acc_ref, main_ref, rest_ref, sems = scratch
    step = pl.program_id(0)

    @pl.when(step == 0)
    def _():
        acc_ref[...] = jnp.zeros_like(acc_ref)

    turned = n_ref[...].T
    acc_ref[1] += dot(turned, dk_ref[...])
    acc_ref[2] += dot(turned, dv_ref[...])

    @pl.when(step % 2 == 1)
    def _():
        acc_ref[0] += dot(own_ref[...].T, dq_ref[...])
        acc_ref[3] += dot(dh_ref[...].T, o_ref[...])

    @pl.when(step == GRAD_STEPS - 1)
    def _():
        lower = lower_lanes((D, TILE))
        for c in range(4):
            main_ref[c] = acc_ref[c, :, : 4 * TILE].astype(bf16)
        for group in range(4):
            entry = entry_of(place, group)
            for k in range(PARTS):
                part = (odd_ref if k % 2 else even_ref).at[k // 2, entry, pl.ds(0, 4)]
                source = main_ref.at[:, part_rows(place, k), pl.ds(group * TILE, TILE)]
                pltpu.make_async_copy(source, part, sems.at[0]).start()
        for two in range(2):
            lanes = slice((4 + two) * TILE, (5 + two) * TILE)
            for both in range(2):
                one = acc_ref[2 * both, :, lanes]
                other = pltpu.roll(acc_ref[2 * both + 1, :, lanes], DH, 1)
                rest_ref[2 * two, both] = jnp.where(lower, one, other).astype(bf16)
                rest_ref[2 * two + 1, both] = jnp.where(lower, other, one).astype(bf16)
        for group in range(4):
            entry = entry_of(place, group)
            for k in range(PARTS):
                part = (odd_ref if k % 2 else even_ref).at[k // 2, entry, pl.ds(4, 2)]
                source = rest_ref.at[group, :, part_rows(place, k)]
                pltpu.make_async_copy(source, part, sems.at[0]).start()
        wait_for(even_ref, sems.at[0])
        wait_for(odd_ref, sems.at[0])


def attn_grads(place, normed_window, dk, dv, normed_own, dq, dh, o):
    rows, few = dk.shape[0] // GRAD_STEPS, dq.shape[0] // (GRAD_STEPS // 2)
    wide = pl.BlockSpec((rows, D), lambda t: (t, 0))
    small = pl.BlockSpec((few, D), lambda t: (t // 2, 0))
    parts = jax.ShapeDtypeStruct((PARTS // 2, 4, 6, PART, TILE), bf16)
    return pl.pallas_call(
        attn_grads_kernel,
        grid=(GRAD_STEPS,),
        in_specs=[SMEM, wide, wide, wide, small, small, small, small],
        out_specs=[ANY] * 2,
        out_shape=[parts] * 2,
        scratch_shapes=[
            pltpu.VMEM((4, D, D), f32),
            pltpu.VMEM((4, D, 4 * TILE), bf16),
            pltpu.VMEM((4, 2, D, TILE), bf16),
            pltpu.SemaphoreType.DMA((1,)),
        ],
        compiler_params=pltpu.CompilerParams(vmem_limit_bytes=VMEM_GRANT),
        cost_estimate=cost(10),
        name="attn_grads",
    )(place, normed_window, dk, dv, normed_own, dq, dh, o)


def norm_grads_kernel(place, dk_ref, dv_ref, dq_ref, wk_ref, wv_ref, wq_ref, back_ref, own_ref, forth_ref, held_ref):
    own_rows = dq_ref.shape[1]
    held_ref[...] = dot(dk_ref[0], wk_ref[...], NT) + dot(dv_ref[0], wv_ref[...], NT)
    own_ref[0] = dot(dq_ref[0], wq_ref[...], NT)
    back_ref[...] = jnp.zeros_like(back_ref)
    forth_ref[...] = jnp.zeros_like(forth_ref)
    for block in range(2 * LEN // QB):
        row = block * QB - place[2]
        part = slice(block * QB, (block + 1) * QB)

        @pl.when(row < 0)
        def _():
            back_ref[0, pl.ds(pl.multiple_of(row + own_rows, QB), QB), :] = held_ref[part, :].astype(bf16)

        @pl.when((row >= 0) & (row < own_rows))
        def _():
            own_ref[0, pl.ds(pl.multiple_of(row, QB), QB), :] += held_ref[part, :]

        @pl.when((row >= own_rows) & (row < 2 * own_rows))
        def _():
            forth_ref[0, pl.ds(pl.multiple_of(row - own_rows, QB), QB), :] = held_ref[part, :].astype(bf16)


def norm_grads(place, dk, dv, dq, w_k, w_v, w_q):
    micro, own_rows, _ = dq.shape
    wide = pl.BlockSpec((1, 2 * LEN, D), lambda m: (m, 0, 0))
    small = pl.BlockSpec((1, own_rows, D), lambda m: (m, 0, 0))
    whole = pl.BlockSpec((D, D), lambda m: (0, 0))
    return pl.pallas_call(
        norm_grads_kernel,
        grid=(micro,),
        in_specs=[SMEM, wide, wide, small, whole, whole, whole],
        out_specs=[small] * 3,
        out_shape=[
            jax.ShapeDtypeStruct(dq.shape, bf16),
            jax.ShapeDtypeStruct(dq.shape, f32),
            jax.ShapeDtypeStruct(dq.shape, bf16),
        ],
        scratch_shapes=[pltpu.VMEM((2 * LEN, D), f32)],
        compiler_params=pltpu.CompilerParams(vmem_limit_bytes=VMEM_GRANT),
        cost_estimate=cost(10),
        name="norm_grads",
    )(place, dk, dv, dq, w_k, w_v, w_q)


def gelu_and_slope(gate):
    root = 0.7978845608028654
    cube = 0.044715
    square = gate * gate
    bend = jnp.tanh(root * gate * (1.0 + cube * square))
    half = 0.5 * (1.0 + bend)
    slope = half + 0.5 * gate * (1.0 - bend * bend) * (root * (1.0 + 3.0 * cube * square))
    return gate * half, slope


def ffn_kernel(place, o_ref, x_ref, dy_ref, wo_ref, gain_ref, all_w, *refs):
    out_ref, dy1_ref, dh1_ref = refs[:3]
    parts = (refs[3:5], refs[5:7])
    (w_ref, g_ref, y_ref, n_ref, nt_ref, dyt_ref, acc_ref, dn_ref, hid_ref, dgate_ref, dup_ref,
     out_held, dy1_held, dh1_held, w_sems, g_sems, out_sems) = refs[7:]
    width = w_ref.shape[2] // 3
    gate_cols, up_cols, down_cols = (slice(c * width, (c + 1) * width) for c in range(3))

    def load(entry):
        group = lax.rem(entry + place[1], 4)
        for k in range(PARTS):
            rows = pl.ds(k * PART, PART)
            pltpu.make_async_copy(all_w.at[k, group], w_ref.at[entry, rows], w_sems.at[entry]).start()

    load(0)
    y = x_ref[...].astype(f32) + dot(o_ref[...], wo_ref[...], NT)
    y_ref[...] = y
    rho = lax.rsqrt(jnp.mean(y * y, axis=-1, keepdims=True) + epsilon)
    normed = (y * rho * gain_ref[...]).astype(bf16)
    n_ref[...] = normed
    nt_ref[...] = normed.T
    dyt_ref[...] = dy_ref[...].T
    acc_ref[...] = y
    dn_ref[...] = jnp.zeros_like(dn_ref)
    for entry in range(1, 4):
        load(entry)

    def through(entry):
        wait_for(w_ref.at[entry], w_sems.at[entry])
        w = w_ref.at[entry]
        normed = n_ref[...]
        gate = dot(normed, w[:, gate_cols])
        up = dot(normed, w[:, up_cols])
        grad_hid = dot(dy_ref[...], w[:, down_cols])
        act, slope = gelu_and_slope(gate)
        hid = (act * up).astype(bf16)
        dgate = (grad_hid * up * slope).astype(bf16)
        dup = (grad_hid * act).astype(bf16)
        hid_ref[...] = hid
        dgate_ref[...] = dgate
        dup_ref[...] = dup
        acc_ref[...] += dot(hid, w[:, down_cols], NT)
        dn_ref[...] += dot(dgate, w[:, gate_cols], NT) + dot(dup, w[:, up_cols], NT)

    def grads(entry, slot, pair):
        g_ref[slot, :, gate_cols] = dot(nt_ref[...], dgate_ref[...]).astype(bf16)
        g_ref[slot, :, up_cols] = dot(nt_ref[...], dup_ref[...]).astype(bf16)
        g_ref[slot, :, down_cols] = dot(dyt_ref[...], hid_ref[...]).astype(bf16)
        for k in range(PARTS):
            part = parts[pair][k % 2].at[k // 2, slot]
            pltpu.make_async_copy(g_ref.at[slot, part_rows(place, k)], part, g_sems.at[slot]).start()

    def one_group(entry, _):
        through(entry)
        grads(entry, entry, 0)
        return 0

    lax.fori_loop(0, 2, one_group, 0)
    through(2)
    wait_for(g_ref.at[0], g_sems.at[0])
    grads(2, 0, 1)
    through(3)
    outs = [(out_held, out_ref), (dy1_held, dy1_ref), (dh1_held, dh1_ref)]
    out_held[...] = acc_ref[...].astype(bf16)
    scaled_y = y_ref[...]
    rho = lax.rsqrt(jnp.mean(scaled_y * scaled_y, axis=-1, keepdims=True) + epsilon)
    scaled_y = scaled_y * rho
    u = dn_ref[...] * gain_ref[...]
    inner = jnp.mean(u * scaled_y, axis=-1, keepdims=True)
    dy1 = dy_ref[...].astype(f32) + rho * (u - scaled_y * inner)
    dy1_held[...] = dy1
    dh1_held[...] = dy1.astype(bf16)
    copies = [pltpu.make_async_copy(held, ref, out_sems.at[j]) for j, (held, ref) in enumerate(outs)]
    for copy in copies:
        copy.start()
    wait_for(g_ref.at[1], g_sems.at[1])
    grads(3, 1, 1)
    for copy in copies:
        copy.wait()
    for slot in range(2):
        wait_for(g_ref.at[slot], g_sems.at[slot])


def ffn(place, attended, x, dy, w_o, gain, weights):
    tokens = x.shape[0]
    columns = weights.shape[3]
    wide = lambda dtype: jax.ShapeDtypeStruct((tokens, D), dtype)
    parts = jax.ShapeDtypeStruct((PARTS // 2, 2, PART, columns), bf16)
    scratch = lambda rows, width, dtype: pltpu.VMEM((rows, width), dtype)
    return pl.pallas_call(
        ffn_kernel,
        in_specs=[SMEM] + [VMEM] * 5 + [ANY],
        out_specs=[ANY] * 7,
        out_shape=[wide(bf16), wide(f32), wide(bf16)] + [parts] * 4,
        scratch_shapes=[
            pltpu.VMEM((4, D, columns), bf16),
            pltpu.VMEM((2, D, columns), bf16),
            scratch(tokens, D, f32),
            scratch(tokens, D, bf16),
            scratch(D, tokens, bf16),
            scratch(D, tokens, bf16),
            scratch(tokens, D, f32),
            scratch(tokens, D, f32),
            scratch(tokens, columns // 3, bf16),
            scratch(tokens, columns // 3, bf16),
            scratch(tokens, columns // 3, bf16),
            scratch(tokens, D, bf16),
            scratch(tokens, D, f32),
            scratch(tokens, D, bf16),
            pltpu.SemaphoreType.DMA((4,)),
            pltpu.SemaphoreType.DMA((2,)),
            pltpu.SemaphoreType.DMA((3,)),
        ],
        compiler_params=pltpu.CompilerParams(vmem_limit_bytes=VMEM_GRANT),
        cost_estimate=cost(32),
        name="ffn",
    )(place, attended, x, dy, w_o, gain, weights)


def grams_of(blocks):
    return jnp.einsum("our,ouw->orw", blocks, blocks, precision=HIGHEST)


def dot_three(a, b):
    parts = []
    for v in (a, b):
        high = v.astype(bf16)
        parts.append((high, (v - high.astype(f32)).astype(bf16)))
    (a_high, a_low), (b_high, b_low) = parts
    return dot(a_high, b_high) + (dot(a_high, b_low) + dot(a_low, b_high))


def muon_kernel(rates, gram_ref, mom_ref, in_ref, out_ref, in_next, out_next):
    width = mom_ref.shape[2]
    for c, rate in enumerate(rates):
        gram = gram_ref[c, :width]
        row = lax.broadcasted_iota(jnp.int32, gram.shape, 0)
        eye = (row == lax.broadcasted_iota(jnp.int32, gram.shape, 1)).astype(f32)
        whole = jnp.sum(jnp.sum(gram * eye, axis=0, keepdims=True), axis=1, keepdims=True)
        first = gram / whole
        start = mom_ref[c] * lax.rsqrt(whole)
        step = linear_coefficient * eye + coef_second * first + coef_third * dot_three(first, first)
        second = dot_three(dot_three(first, step), step)
        once = dot_three(start, step)
        turn = dot_three(once, second)
        both = rate * (linear_coefficient * once + coef_second * turn + coef_third * dot_three(turn, second))
        if c < len(rates) - 1:
            in_next[c] = in_ref[c] * (1.0 - rate * decay_rate) - both
        else:
            both = both if out_ref.shape == both.shape else both.T
            out_next[...] = out_ref[...] * (1.0 - rate * decay_rate) - both


def muon(rates, gram, moms, in_param, out_param):
    return pl.pallas_call(
        functools.partial(muon_kernel, rates),
        in_specs=[VMEM] * 4,
        out_specs=[VMEM] * 2,
        out_shape=[jax.ShapeDtypeStruct(in_param.shape, f32), jax.ShapeDtypeStruct(out_param.shape, f32)],
        compiler_params=pltpu.CompilerParams(vmem_limit_bytes=VMEM_GRANT),
        cost_estimate=cost(8),
        name="muon",
    )(gram, moms, in_param, out_param)


def attn_momentum_kernel(place, *refs):
    count = len(refs) - 9
    terms, (in_mom, out_mom, in_ref, extra_ref) = refs[:count], refs[count : count + 4]
    mom_in_ref, mom_out_ref, gram_ref, gain_ref, flat_ref = refs[count + 4 :]
    tiles = [sum(term[c].astype(f32) for term in terms) for c in range(6)]
    gain = 0.0
    for c in range(4):
        tail = tiles[4 + c // 2]
        other = pltpu.roll(tail, DH, 1)
        swapped = (place[1] + c) % 2 == 1
        tail = jnp.where(swapped, other, tail)[:, :DH]
        grad = jnp.concatenate([tiles[c], tail], axis=1)
        if c < 3:
            gain += jnp.sum(in_ref[c].astype(bf16).astype(f32) * grad, axis=1, keepdims=True)
            mom = momentum_decay * in_mom[c] + grad
            mom_in_ref[c] = mom
        else:
            mom = momentum_decay * out_mom[...].T + grad
            mom_out_ref[...] = mom.T
        flat_ref[c] = mom
        gram_ref[c, : mom.shape[1]] = lax.dot_general(mom, mom, TN, precision=HIGHEST, preferred_element_type=f32)
        gram_ref[c, mom.shape[1] :] = extra_ref[c]
    gain_ref[...] = gain


def attn_momentum(place, terms, in_mom, out_mom, attn_in, extra):
    _, rows, width = in_mom.shape
    operands = [*terms, in_mom, out_mom, attn_in, extra]
    shape = lambda *dims: jax.ShapeDtypeStruct(dims, f32)
    return pl.pallas_call(
        attn_momentum_kernel,
        in_specs=[SMEM] + [VMEM] * len(operands),
        out_specs=[VMEM] * 5,
        out_shape=[
            shape(3, rows, width),
            shape(width, rows),
            shape(4, width + extra.shape[1], width),
            shape(rows, 1),
            shape(4, rows, width),
        ],
        compiler_params=pltpu.CompilerParams(vmem_limit_bytes=VMEM_GRANT),
        cost_estimate=cost(4),
        name="attn_momentum",
    )(place, *operands)


def ffn_momentum_kernel(*refs):
    count = len(refs) - 8
    terms, (in_mom, out_mom, in_ref) = refs[:count], refs[count : count + 3]
    mom_in_ref, mom_out_ref, gram_ref, gain_ref, flat_ref = refs[count + 3 :]
    width = in_mom.shape[2]
    gain = 0.0
    for c in range(3):
        grad = sum(term[:, c * width : (c + 1) * width].astype(f32) for term in terms)
        if c < 2:
            gain += jnp.sum(in_ref[c].astype(bf16).astype(f32) * grad, axis=1, keepdims=True)
            mom = momentum_decay * in_mom[c] + grad
            mom_in_ref[c] = mom
        else:
            mom = momentum_decay * out_mom[...] + grad
            mom_out_ref[...] = mom
        flat_ref[c] = mom
        gram_ref[c] = lax.dot_general(mom, mom, TN, precision=HIGHEST, preferred_element_type=f32)
    gain_ref[...] = gain


def ffn_momentum(terms, in_mom, out_mom, ffn_in):
    _, rows, width = in_mom.shape
    operands = [*terms, in_mom, out_mom, ffn_in]
    shape = lambda *dims: jax.ShapeDtypeStruct(dims, f32)
    return pl.pallas_call(
        ffn_momentum_kernel,
        in_specs=[VMEM] * len(operands),
        out_specs=[VMEM] * 5,
        out_shape=[
            shape(2, rows, width),
            shape(rows, width),
            shape(3, width, width),
            shape(rows, 1),
            shape(3, rows, width),
        ],
        compiler_params=pltpu.CompilerParams(vmem_limit_bytes=VMEM_GRANT),
        cost_estimate=cost(5),
        name="ffn_momentum",
    )(*operands)


def adam_update(param, grad, first, second):
    first_new = beta_one * first + (1.0 - beta_one) * grad
    second_new = beta_two * second + (1.0 - beta_two) * grad * grad
    corrected_first = first_new / (1.0 - beta_one**STEP)
    corrected_second = second_new / (1.0 - beta_two**STEP)
    return (
        first_new,
        second_new,
        param - adam_rate * corrected_first / (jnp.sqrt(corrected_second) + adam_epsilon),
    )


def direct():
    return lax.axis_size("dp") == PARTS and lax.axis_size("mp") == 4


def swap(x, bit):
    return lax.ppermute(x, "dp", [(j, j ^ bit) for j in range(lax.axis_size("dp"))])


def from_above(x, k):
    return lax.ppermute(x, "mp", [((j + k) % 4, j) for j in range(4)])


def to_above(x, k):
    return lax.ppermute(x, "mp", [(j, (j + k) % 4) for j in range(4)])


def behind(x, *others):
    return lax.optimization_barrier((x, others))[0]


def total(*terms):
    return sum(term.astype(f32) for term in terms)


def gather_all(shard):
    rows, columns = shard.shape
    whole = lax.all_gather(shard, ("dp", "mp"), axis=0, tiled=False)
    if rows == PART:
        return whole.reshape(PARTS, 4, PART, columns)
    whole = whole.reshape(-1, 4, rows, columns).transpose(1, 0, 2, 3).reshape(4, PARTS, PART, columns)
    return whole.transpose(1, 0, 2, 3)


def gather_pieces(shard):
    tiles, rows, _ = shard.shape
    if not direct():
        whole = lax.all_gather(shard, ("dp", "mp"), axis=0, tiled=False)
        whole = whole.reshape(PARTS, -1, 4, tiles, rows, TILE).transpose(0, 2, 3, 1, 4, 5)
        return list(whole.reshape(PARTS, 4, tiles, PART, TILE))
    own = jnp.stack([shard] + [from_above(shard, k) for k in (1, 2, 3)])
    return own


def spread_pieces(own, meanwhile):
    if not direct():
        return own
    others = behind([swap(own, bit) for bit in (2, 4, 6)], meanwhile)
    return [piece for here in (own, *others) for piece in (here, swap(here, 1))]


def scatter_core(even, odd):
    return total(even, swap(odd, 1)).astype(bf16)


def send_plane(mine):
    return [swap(mine[1], 2), swap(mine[2], 4), swap(mine[3], 6)]


def send_line(line):
    return [to_above(line[k], k) for k in (1, 2, 3)]


def plain_order(even, odd):
    return jnp.stack([even, odd], axis=1).reshape((PARTS,) + even.shape[1:])


def scatter_plain(parts, rows):
    groups, columns = parts.shape[2], parts.shape[-1]
    parts = parts.reshape(PARTS, 4, groups, PART // rows, rows, columns).transpose(0, 3, 1, 2, 4, 5)
    parts = parts.reshape((-1,) + parts.shape[3:])
    return lax.psum_scatter(parts, ("dp", "mp"), scatter_dimension=0, tiled=False)


def gather_small(x, axis_name, axis):
    if not direct():
        return lax.all_gather(x, axis_name, axis=axis, tiled=True)
    here = lax.axis_index(axis_name)
    size = lax.axis_size(axis_name)
    bit = 1
    while bit < size:
        other = lax.ppermute(x, axis_name, [(j, j ^ bit) for j in range(size)])
        upper = (here & bit) != 0
        x = jnp.concatenate([jnp.where(upper, other, x), jnp.where(upper, x, other)], axis=axis)
        bit *= 2
    return x


def sum_line(x):
    if not direct():
        return lax.psum(x, "mp")
    return x + from_above(x, 1) + from_above(x, 2) + from_above(x, 3)


def to_low(x):
    return x.astype(bf16)


def split_core(x):
    odd = (lax.axis_index("dp") & 1) != 0
    return jnp.where(odd, x[2:], x[:2]), to_low(jnp.where(odd, x[:2], x[2:]))


def sum_core(mine, other, meanwhile):
    return total(mine, behind(swap(other, 1), meanwhile))


def sum_first(pair, meanwhile):
    others = behind((swap(to_low(pair[0]), 2), swap(to_low(pair[1]), 4)), meanwhile)
    return total(pair[0], others[0]), total(pair[1], others[1])


def sum_second(pair, meanwhile):
    others = behind((swap(to_low(pair[0]), 4), swap(to_low(pair[1]), 2)), meanwhile)
    return total(pair[0], others[0]), total(pair[1], others[1])


def sum_last(pair, meanwhile):
    odd = (lax.axis_index("dp") & 1) != 0
    mine = to_low(jnp.stack(pair))
    other = behind(swap(mine, 1), meanwhile)
    return jnp.concatenate([jnp.where(odd, other, mine), jnp.where(odd, mine, other)]).astype(f32)


def shards(
    tokens, lengths, cotangent, attn_in, attn_out, ffn_in, ffn_out, gains, table,
    attn_in_mom, attn_out_mom, ffn_in_mom, ffn_out_mom,
    gain_first, gain_second, table_first, table_second,
):
    micro, own_rows, _ = tokens.shape
    here = lax.axis_index("mp")
    n_mp = lax.axis_size("mp")
    width = attn_in.shape[2]
    heads_dev = table.shape[1]

    rows_dev = attn_in.shape[1]
    width_ffn = ffn_in.shape[2]
    index = jnp.stack([lax.axis_index("dp"), here]).astype(jnp.int32)
    place = index if direct() else jnp.zeros_like(index)
    odd_group = (here & 1) != 0

    ffn_low = jnp.concatenate([ffn_in[0], ffn_in[1], ffn_out.T], axis=1).astype(bf16)
    attn_low = [part.astype(bf16) for part in (attn_in[0], attn_in[1], attn_in[2], attn_out.T)]
    tails = [part[:, TILE:] for part in attn_low]
    beside = lambda one, two: jnp.where(
        odd_group, jnp.concatenate([two, one], axis=1), jnp.concatenate([one, two], axis=1)
    )
    attn_tiles = jnp.stack([part[:, :TILE] for part in attn_low] + [beside(*tails[:2]), beside(*tails[2:])])
    gain_low = gather_small(gains.astype(bf16), "dp", 1).astype(f32)
    table_all = gather_small(table, "mp", 1)[:, np.array(HEAD_ORDER)]
    onehot = skew_onehot()
    line = lax.dot_general(
        table_all, onehot, (((0,), (1,)), ((), ())), precision=HIGHEST, preferred_element_type=f32
    ).reshape(PAIRS, 2, SKEW)
    ffn_all = gather_all(ffn_low)
    attn_own = gather_pieces(attn_tiles)
    halo = behind(tokens, attn_own)
    up, down = [(j, j + 1) for j in range(n_mp - 1)], [(j + 1, j) for j in range(n_mp - 1)]
    sides = (lax.ppermute(halo, "mp", up), lax.ppermute(halo, "mp", down))
    bias = make_bias(behind(line, attn_own))
    attn_pieces = spread_pieces(attn_own, (bias, gain_low, sides))

    first_row = own_rows * here
    first_doc = first_row // LEN
    inset = first_row - first_doc * LEN
    block_place = first_row // QB + jnp.arange(own_rows // QB, dtype=jnp.int32)
    slot = block_place // (LEN // QB) - first_doc
    lens_window = lax.dynamic_slice_in_dim(
        jnp.concatenate([lengths, jnp.ones((micro, 1), lengths.dtype)], axis=1), first_doc, 2, axis=1
    )
    meta = jnp.concatenate([slot, block_place % (LEN // QB), lens_window.reshape(-1)]).astype(jnp.int32)

    there = jnp.concatenate([place, inset[None].astype(jnp.int32)])
    projected, (w_q, w_k, w_v, w_o) = project(there, sides, tokens, gain_low[0:1], attn_pieces)
    q, k, v, normed_window, normed_own = projected
    attended, stats = attend(meta, q, k, v, bias)
    out_seq = attended
    attended = attended.reshape(micro * own_rows, D)
    normed_window = normed_window.reshape(micro * 2 * LEN, D)
    normed_own = normed_own.reshape(micro * own_rows, D)

    dy = cotangent.reshape(micro * own_rows, D)
    output, grad_middle, grad_mid_low, even_one, odd_one, even_two, odd_two = ffn(
        place, attended, tokens.reshape(micro * own_rows, D), dy, w_o, gain_low[1:2], ffn_all
    )
    grad_att = dot(grad_mid_low, w_o).astype(bf16).reshape(micro, own_rows, D)
    back_args = (meta, q, k, v, grad_att, out_seq, stats, bias)
    if direct():
        mine_one, mine_two = scatter_core(even_one, odd_one), scatter_core(even_two, odd_two)
        plane_one = send_plane(mine_one)
        grads = attend_back(*back_args, [mine_one, mine_two])
        line_one = total(mine_one[0], *behind(plane_one, grads)).astype(bf16)
        plane_two = send_plane(behind(mine_two, line_one))
        grads = behind(grads, line_one)
    else:
        even_ffn = jnp.concatenate([even_one, even_two], axis=1)
        odd_ffn = jnp.concatenate([odd_one, odd_two], axis=1)
        shard_ffn = scatter_plain(plain_order(even_ffn, odd_ffn)[:, :, None], rows_dev)[0].astype(f32)
        grads = attend_back(*back_args)
    grad_q, grad_k, grad_v, grad_bias = grads
    grad_q = grad_q.reshape(micro * own_rows, D)
    grad_k = grad_k.reshape(micro * 2 * LEN, D)
    grad_v = grad_v.reshape(micro * 2 * LEN, D)
    even, odd = attn_grads(
        place, normed_window, grad_k, grad_v, normed_own, grad_q, grad_mid_low, attended
    )
    if direct():
        diag = diagonals(behind(grad_bias, even))
        line_two = total(mine_two[0], *behind(plane_two, diag)).astype(bf16)
        mine_attn = scatter_core(even, behind(odd, line_two))
        plane_attn = send_plane(mine_attn)
        sent_ffn = [to_above(line_one[1], 1), to_above(line_two[0], 2), to_above(line_two[1], 3)]
        grad_q, grad_k, grad_v = behind((grad_q, grad_k, grad_v), mine_attn)
    else:
        diag = diagonals(grad_bias)
    back, own_part, forth = norm_grads(
        there,
        grad_k.reshape(micro, 2 * LEN, D),
        grad_v.reshape(micro, 2 * LEN, D),
        grad_q.reshape(micro, own_rows, D),
        w_k,
        w_v,
        w_q,
    )
    own_part = own_part.reshape(micro * own_rows, D)
    table_sum = lax.dot_general(
        onehot,
        diag.reshape(H, SKEW),
        (((0,), (1,)), ((), ())),
        precision=HIGHEST,
        preferred_element_type=f32,
    )
    low = lambda v: v.astype(bf16).astype(f32)
    extra = jnp.pad(table_sum.reshape(4, 1, -1), ((0, 0), (0, 15), (0, width - BUCKETS * H // 4)))
    if direct():
        line_attn = total(mine_attn[0], *behind(plane_attn, (extra, back, forth, own_part))).astype(bf16)
        sent_ffn = behind(sent_ffn, line_attn)
        line_attn = behind(line_attn, sent_ffn)
        terms = [line_one[0], *sent_ffn]
    else:
        terms = [shard_ffn]
    mom_fin, mom_fout, gram_ffn, gain_ffn, blocks_ffn = ffn_momentum(terms, ffn_in_mom, ffn_out_mom.T, ffn_in)
    flat_ffn = gram_ffn.reshape(4, -1, width_ffn)
    if direct():
        split_ffn = split_core(flat_ffn)
        core_ffn = sum_core(*split_ffn, ())
        terms = [line_attn[0], *behind(send_line(line_attn), gram_ffn)]
    else:
        terms = [scatter_plain(plain_order(even, odd), rows_dev)]
    mom_in, mom_out, gram_attn, gain_attn, blocks_attn = attn_momentum(
        index, terms, attn_in_mom, attn_out_mom, attn_in, extra
    )
    fin_blocks = lambda gram: muon(
        [rate_ffn_in] * 2 + [rate_ffn_out],
        gram.reshape(3, width_ffn, width_ffn),
        blocks_ffn,
        ffn_in,
        ffn_out.T,
    )
    if direct():
        mine, other = split_core(gram_attn)
        first_ffn = sum_first(core_ffn, mine)
        second_ffn = sum_second(first_ffn, ())
        core_attn = sum_core(mine, other, second_ffn)
        ffn_in_next, ffn_out_next = fin_blocks(sum_last(second_ffn, core_attn))
        back, forth = behind((back, forth), core_attn)
        back, forth = lax.ppermute(back, "mp", down), lax.ppermute(forth, "mp", up)
        first_attn = sum_first(core_attn, (ffn_in_next, back, forth))
        second_attn = sum_second(first_attn, ())
    else:
        second_attn = ()
        back, forth = lax.ppermute(back, "mp", down), lax.ppermute(forth, "mp", up)
        ffn_in_next, ffn_out_next = fin_blocks(lax.psum(flat_ffn, "dp"))
        summed = lax.psum(gram_attn, "dp")
    own_part, back, forth = behind((own_part, back, forth), second_attn)
    grad_normed = own_part + (back.astype(f32) + forth.astype(f32)).reshape(micro * own_rows, D)
    rows = tokens.reshape(micro * own_rows, D).astype(f32)
    rho = lax.rsqrt(jnp.mean(rows * rows, axis=-1, keepdims=True) + epsilon)
    u = grad_normed * gain_low[0]
    tokens_grad = grad_middle + rho * (u - rows * rho * rho * jnp.mean(u * rows, axis=-1, keepdims=True))
    if direct():
        summed = sum_last(second_attn, tokens_grad)
    table_sum = summed[:, width, : BUCKETS * H // 4]
    gain_terms = jnp.stack([gain_attn[:, 0], gain_ffn[:, 0]])
    small = jnp.concatenate([gain_terms.reshape(-1), table_sum.reshape(-1)])
    small = sum_line(jnp.pad(small, (0, -small.size % 1024)).reshape(-1, 128)).reshape(-1)
    gain_grad = small[: gain_terms.size].reshape(gain_terms.shape) / low(gains)
    table_sum = small[gain_terms.size : gain_terms.size + BUCKETS * H].reshape(BUCKETS, H)
    table_sum = table_sum[:, np.argsort(np.array(HEAD_ORDER))]
    table_grad = lax.dynamic_slice_in_dim(table_sum, here * heads_dev, heads_dev, axis=1)
    attn_in_next, attn_out_next = muon(
        [rate_attn_in] * 3 + [rate_attn_out], summed, blocks_attn, attn_in, attn_out
    )
    gain_first_next, gain_second_next, gains_next = adam_update(gains, gain_grad, gain_first, gain_second)
    table_first_next, table_second_next, table_next = adam_update(table, table_grad, table_first, table_second)
    return (
        output.reshape(tokens.shape),
        tokens_grad.reshape(tokens.shape),
        attn_in_next,
        attn_out_next,
        ffn_in_next,
        ffn_out_next.T,
        mom_in,
        mom_out,
        mom_fin,
        mom_fout.T,
        gain_first_next,
        gain_second_next,
        gains_next,
        table_first_next,
        table_second_next,
        table_next,
    )


def solution(mesh):
    token = P(None, ("dp", "mp"), None)
    columns = P(None, "dp", "mp")
    flipped = P("mp", "dp")
    gain = P(None, "dp")
    head = P(None, "mp")
    return jax.shard_map(
        shards,
        mesh=mesh,
        in_specs=(
            token, P(None, "dp"), token, columns, flipped, columns, flipped, gain, head,
            columns, flipped, columns, flipped, gain, gain, head, head,
        ),
        out_specs=(
            token, token, columns, flipped, columns, flipped, columns, flipped, columns, flipped,
            gain, gain, gain, head, head, head,
        ),
        check_vma=False,
    )
```

```python
import functools

import jax
import jax.numpy as jnp
import numpy as np
from jax import lax
from jax.experimental import pallas as pl
from jax.experimental.pallas import tpu as pltpu
from jax.sharding import PartitionSpec as P

D = 768
H = 12
DH = 64
BUCKETS = 32
LEN = 512
STEP = 8
QB = 128
SKEW = 1024
PAIRS = H // 2
TILE = 128
HEAD_ORDER = (0, 1, 3, 4, 6, 7, 9, 10, 2, 5, 8, 11)

epsilon = 1e-06
negative_fill = -1e30
momentum_decay = 0.95
decay_rate = 0.01
linear_coefficient = 3.4445
coef_second = -4.775
coef_third = 2.0315
rate_attn_in = 0.25
rate_attn_out = 12.0
rate_ffn_in = 0.6
rate_ffn_out = 0.3
beta_one = 0.9
beta_two = 0.95
adam_epsilon = 1e-08
adam_rate = 0.3
bucket_marks = (12, 16, 23, 32, 46, 64, 91)

HIGHEST = lax.Precision.HIGHEST
HIGH = lax.Precision.HIGH
bf16 = jnp.bfloat16
f32 = jnp.float32
NN = (((1,), (0,)), ((), ()))
NT = (((1,), (1,)), ((), ()))
TN = (((0,), (0,)), ((), ()))


VMEM_GRANT = 60 << 20
ANY = pl.BlockSpec(memory_space=pltpu.HBM)
SMEM = pl.BlockSpec(memory_space=pltpu.SMEM)
VMEM = pl.BlockSpec(memory_space=pltpu.VMEM)


def dot(a, b, dims=NN):
    return lax.dot_general(a, b, dims, preferred_element_type=f32)


def skew_onehot():
    place = np.arange(SKEW)
    relative = np.where(place < SKEW - QB + 1, place, place - SKEW) - (LEN - QB)
    distance = np.abs(relative)
    far = 8 + sum((distance >= mark).astype(np.int32) for mark in bucket_marks)
    bucket = np.where(distance < 8, distance, far) + 16 * (relative > 0)
    return (bucket[:, None] == np.arange(BUCKETS)[None, :]).astype(np.float32)


def cost(micros):
    return pl.CostEstimate(flops=int(micros * 1e7), bytes_accessed=0, transcendentals=0)


def half_lanes(shape, half):
    lane = lax.broadcasted_iota(jnp.int32, shape, 1)
    return (lane < DH) if half == 0 else (lane >= DH)


def bias_kernel(line_ref, bias_ref):
    for half in range(2):
        line = jnp.broadcast_to(line_ref[0, half : half + 1, :], (QB, SKEW))
        bias_ref[0, half] = pltpu.roll(line, 0, 1, stride=1, stride_axis=0).T


def make_bias(line):
    return pl.pallas_call(
        bias_kernel,
        grid=(PAIRS,),
        compiler_params=pltpu.CompilerParams(vmem_limit_bytes=VMEM_GRANT),
        in_specs=[pl.BlockSpec((1, 2, SKEW), lambda p: (p, 0, 0))],
        out_specs=pl.BlockSpec((1, 2, SKEW, QB), lambda p: (p, 0, 0, 0)),
        out_shape=jax.ShapeDtypeStruct((PAIRS, 2, SKEW, QB), f32),
        cost_estimate=cost(8),
        name="make_bias",
    )(line)


def diag_kernel(acc_ref, diag_ref):
    row = lax.broadcasted_iota(jnp.int32, (QB, QB), 0)
    lane = lax.broadcasted_iota(jnp.int32, (QB, QB), 1)
    flip = (row + lane == QB - 1).astype(f32)
    for half in range(2):
        turned = lax.dot_general(flip, acc_ref[0, half], NT, precision=HIGHEST, preferred_element_type=f32)
        shifted = pltpu.roll(turned, SKEW - QB + 1, 1, stride=1, stride_axis=0)
        diag_ref[0, half : half + 1, :] = jnp.sum(shifted, axis=0, keepdims=True)


def diagonals(acc):
    return pl.pallas_call(
        diag_kernel,
        grid=(PAIRS,),
        compiler_params=pltpu.CompilerParams(vmem_limit_bytes=VMEM_GRANT),
        in_specs=[pl.BlockSpec((1, 2, SKEW, QB), lambda p: (p, 0, 0, 0))],
        out_specs=pl.BlockSpec((1, 2, SKEW), lambda p: (p, 0, 0)),
        out_shape=jax.ShapeDtypeStruct((PAIRS, 2, SKEW), f32),
        cost_estimate=cost(1),
        name="diagonals",
    )(acc)


def both_heads(block):
    zero = jnp.zeros_like(block)
    return jnp.concatenate(
        [
            jnp.where(half_lanes(block.shape, 0), block, zero),
            jnp.where(half_lanes(block.shape, 1), block, zero),
        ],
        axis=0,
    )


def block_scores(meta, block, mb, keys, queries_two, bias_ref):
    start = pl.multiple_of((LEN - QB) - QB * meta[3 + block], QB)
    length = meta[6 + 2 * mb + meta[block]]
    bias = jnp.concatenate([bias_ref[0, 0, pl.ds(start, LEN), :], bias_ref[0, 1, pl.ds(start, LEN), :]], axis=1)
    scores = dot(keys, queries_two, NT) + bias
    row = lax.broadcasted_iota(jnp.int32, scores.shape, 0)
    return jnp.where(row < length, scores, negative_fill)


def block_rows(meta, block):
    return pl.ds(pl.multiple_of(meta[block] * LEN, LEN), LEN)


def one_of_two(pair):
    top = lax.broadcasted_iota(jnp.int32, (QB, QB), 0) < DH
    return jnp.where(top, pair[:, :QB], pair[:, QB:]).T


def attend_kernel(meta, q_ref, k_ref, v_ref, bias_ref, o_ref, lse_ref):
    mb = pl.program_id(1)
    blocks = range(q_ref.shape[1] // QB)
    scores, values = [], []
    for block in blocks:
        rows = block_rows(meta, block)
        values.append(v_ref[0, rows, :].T)
        queries_two = both_heads(q_ref[0, block * QB : (block + 1) * QB, :])
        scores.append(block_scores(meta, block, mb, k_ref[0, rows, :], queries_two, bias_ref))
    for block in blocks:
        top = jnp.max(scores[block], axis=0, keepdims=True)
        weights = jnp.exp(scores[block] - top)
        total = jnp.sum(weights, axis=0, keepdims=True)
        lse_ref[0, 0, block : block + 1, :] = top + jnp.log(total)
        out = one_of_two(dot(values[block], weights.astype(bf16)) / total)
        o_ref[0, block * QB : (block + 1) * QB, :] = out.astype(bf16)


def attend_back_kernel(
    meta, q_ref, k_ref, v_ref, do_ref, o_ref, lse_ref, bias_ref, dq_ref, dk_ref, dv_ref, acc_ref, dk_acc, dv_acc
):
    mb = pl.program_id(1)

    @pl.when(mb == 0)
    def _():
        acc_ref[...] = jnp.zeros_like(acc_ref)

    dk_acc[...] = jnp.zeros_like(dk_acc)
    dv_acc[...] = jnp.zeros_like(dv_acc)
    parts = []
    for block in range(q_ref.shape[1] // QB):
        rows = block_rows(meta, block)
        own = slice(block * QB, (block + 1) * QB)
        keys = k_ref[0, rows, :]
        grad = do_ref[0, own, :]
        queries_two, grad_two = both_heads(q_ref[0, own, :]), both_heads(grad)
        scores = block_scores(meta, block, mb, keys, queries_two, bias_ref)
        grad_soft = dot(v_ref[0, rows, :], grad_two, NT)
        inner = (grad.astype(f32) * o_ref[0, own, :].astype(f32)).T
        inner = jnp.concatenate(
            [jnp.sum(inner[:DH], axis=0, keepdims=True), jnp.sum(inner[DH:], axis=0, keepdims=True)], axis=1
        )
        parts.append((rows, own, keys, queries_two, grad_two, scores, grad_soft, inner))
    lows = []
    for block, (_, _, _, _, _, scores, grad_soft, inner) in enumerate(parts):
        soft = jnp.exp(scores - lse_ref[0, 0, block : block + 1, :])
        grad_scores = soft * (grad_soft - inner)
        start = pl.multiple_of((LEN - QB) - QB * meta[3 + block], QB)
        acc_ref[0, 0, pl.ds(start, LEN), :] += grad_scores[:, :QB]
        acc_ref[0, 1, pl.ds(start, LEN), :] += grad_scores[:, QB:]
        lows.append((soft.astype(bf16), grad_scores.astype(bf16)))
    for (rows, own, keys, queries_two, grad_two, _, _, _), (soft, grad_low) in zip(parts, lows):
        both = dot(jnp.concatenate([grad_low, soft], axis=0), jnp.concatenate([queries_two, grad_two], axis=1))
        dk_acc[rows, :] += both[:LEN, :QB]
        dv_acc[rows, :] += both[LEN:, QB:]
        dq_ref[0, own, :] = one_of_two(dot(keys.T, grad_low)).astype(bf16)
    dk_ref[0] = dk_acc[...].astype(bf16)
    dv_ref[0] = dv_acc[...].astype(bf16)


def attention_specs(rows, window):
    own = pl.BlockSpec((1, rows, QB), lambda p, m, _: (m, 0, p))
    wide = pl.BlockSpec((1, window, QB), lambda p, m, _: (m, 0, p))
    lines = pl.BlockSpec((1, 2, SKEW, QB), lambda p, m, _: (p, 0, 0, 0))
    stats = pl.BlockSpec((1, 1, 8, 2 * QB), lambda p, m, _: (m, p, 0, 0))
    return own, wide, lines, stats


def attend(meta, q, k, v, bias):
    micro, rows, _ = q.shape
    own, wide, lines, stats = attention_specs(rows, k.shape[1])
    return pl.pallas_call(
        attend_kernel,
        grid_spec=pltpu.PrefetchScalarGridSpec(
            num_scalar_prefetch=1,
            grid=(PAIRS, micro),
            in_specs=[own, wide, wide, lines],
            out_specs=[own, stats],
        ),
        out_shape=[
            jax.ShapeDtypeStruct(q.shape, bf16),
            jax.ShapeDtypeStruct((micro, PAIRS, 8, 2 * QB), f32),
        ],
        compiler_params=pltpu.CompilerParams(vmem_limit_bytes=VMEM_GRANT),
        cost_estimate=cost(17),
        name="attend",
    )(meta, q, k, v, bias)


def attend_back(meta, q, k, v, grad, out, stats, bias, after=()):
    micro, rows, _ = q.shape
    window = k.shape[1]
    own, wide, lines, lse = attention_specs(rows, window)
    kernel = lambda *refs: attend_back_kernel(*refs[:8], *refs[8 + len(after) :])
    return pl.pallas_call(
        kernel,
        grid_spec=pltpu.PrefetchScalarGridSpec(
            num_scalar_prefetch=1,
            grid=(PAIRS, micro),
            in_specs=[own, wide, wide, own, own, lse, lines] + [ANY] * len(after),
            out_specs=[own, wide, wide, lines],
            scratch_shapes=[pltpu.VMEM((window, QB), f32), pltpu.VMEM((window, QB), f32)],
        ),
        out_shape=[
            jax.ShapeDtypeStruct(q.shape, bf16),
            jax.ShapeDtypeStruct(k.shape, bf16),
            jax.ShapeDtypeStruct(k.shape, bf16),
            jax.ShapeDtypeStruct(bias.shape, f32),
        ],
        compiler_params=pltpu.CompilerParams(vmem_limit_bytes=VMEM_GRANT),
        cost_estimate=cost(24),
        name="attend_back",
    )(meta, q, k, v, grad, out, stats, bias, *after)


PARTS = 8
PART = D // PARTS


def part_rows(place, k):
    return pl.ds(pl.multiple_of((place[0] ^ k) * PART, PART), PART)


def entry_of(place, group):
    return lax.rem(group - place[1] + 4, 4)


def wait_for(ref, sem):
    pltpu.make_async_copy(ref, ref, sem).wait()


def lower_lanes(shape):
    return lax.broadcasted_iota(jnp.int32, shape, 1) < DH


PROJECT_STEPS = 2


def project_kernel(place, above, own_all, below, own_ref, gain_ref, *refs):
    pieces = refs[:PARTS]
    q_ref, k_ref, v_ref, n_ref, n_own_ref = refs[PARTS : PARTS + 5]
    w_refs = refs[PARTS + 5 : PARTS + 9]
    x_ref, rest_ref, sems, w_sems = refs[PARTS + 9 :]
    mb, step = pl.program_id(0), pl.program_id(1)
    own_rows = own_all.shape[1]

    @pl.when((mb == 0) & (step == 0))
    def _():
        for group in range(4):
            entry = entry_of(place, group)
            lanes = pl.ds(group * TILE, TILE)
            for k, piece in enumerate(pieces):
                rows = part_rows(place, k)
                pltpu.make_async_copy(piece.at[entry, pl.ds(4, 2)], rest_ref.at[group, :, rows], w_sems.at[4]).start()
                for c in range(4):
                    pltpu.make_async_copy(piece.at[entry, c], w_refs[c].at[rows, lanes], w_sems.at[c]).start()
        for m in range(own_all.shape[0]):
            for block in range(2 * LEN // QB):
                row = block * QB - place[2]
                for source, first, here in (
                    (above, row + own_rows, row < 0),
                    (own_all, row, (row >= 0) & (row < own_rows)),
                    (below, jnp.minimum(row - own_rows, own_rows - QB), row >= own_rows),
                ):

                    @pl.when(here)
                    def _():
                        rows = pl.ds(pl.multiple_of(first, QB), QB)
                        into = x_ref.at[m, pl.ds(block * QB, QB)]
                        pltpu.make_async_copy(source.at[m, rows], into, sems.at[m]).start()

        wait_for(rest_ref, w_sems.at[4])
        lower = lower_lanes((D, TILE))
        for two in range(2):
            lanes = slice((4 + two) * TILE, (5 + two) * TILE)
            for both in range(2):
                even, odd = rest_ref[2 * two, both], rest_ref[2 * two + 1, both]
                w_refs[2 * both][:, lanes] = jnp.where(lower, even, odd)
                turned = pltpu.roll(jnp.where(lower, odd, even).astype(f32), DH, 1)
                w_refs[2 * both + 1][:, lanes] = turned.astype(bf16)
        for c in range(4):
            wait_for(w_refs[c].at[:, pl.ds(0, 4 * TILE)], w_sems.at[c])

    @pl.when(step == 0)
    def _():
        wait_for(x_ref.at[mb], sems.at[mb])

    def norm(rows):
        rows = rows.astype(f32)
        rho = lax.rsqrt(jnp.mean(rows * rows, axis=-1, keepdims=True) + epsilon)
        return (rows * rho * gain_ref[...]).astype(bf16)

    size = k_ref.shape[1]
    normed = norm(x_ref[mb, pl.ds(pl.multiple_of(step * size, size), size), :])
    n_ref[0] = normed
    k_ref[0] = dot(normed, w_refs[1][...]).astype(bf16)
    v_ref[0] = dot(normed, w_refs[2][...]).astype(bf16)
    normed = norm(own_ref[0])
    n_own_ref[0] = normed
    q_ref[0] = dot(normed, w_refs[0][...]).astype(bf16)


def project(place, sides, own, gain, pieces):
    micro, own_rows, _ = own.shape
    rows, few = 2 * LEN // PROJECT_STEPS, own_rows // PROJECT_STEPS
    wide = pl.BlockSpec((1, rows, D), lambda m, t: (m, t, 0))
    small = pl.BlockSpec((1, few, D), lambda m, t: (m, t, 0))
    whole = pl.BlockSpec((D, D), lambda m, t: (0, 0))
    many_shape = jax.ShapeDtypeStruct((micro, 2 * LEN, D), bf16)
    few_shape = jax.ShapeDtypeStruct(own.shape, bf16)
    results = pl.pallas_call(
        project_kernel,
        grid=(micro, PROJECT_STEPS),
        in_specs=[SMEM, ANY, ANY, ANY, small, pl.BlockSpec((1, D), lambda m, t: (0, 0))] + [ANY] * PARTS,
        out_specs=[small, wide, wide, wide, small] + [whole] * 4,
        out_shape=[few_shape, many_shape, many_shape, many_shape, few_shape]
        + [jax.ShapeDtypeStruct((D, D), bf16)] * 4,
        scratch_shapes=[
            pltpu.VMEM((micro, 2 * LEN, D), bf16),
            pltpu.VMEM((4, 2, D, TILE), bf16),
            pltpu.SemaphoreType.DMA((micro,)),
            pltpu.SemaphoreType.DMA((5,)),
        ],
        compiler_params=pltpu.CompilerParams(vmem_limit_bytes=VMEM_GRANT),
        cost_estimate=cost(14),
        name="project",
    )(place, sides[0], own, sides[1], own, gain, *pieces)
    return results[:5], results[5:]


GRAD_STEPS = 4


def attn_grads_kernel(place, n_ref, dk_ref, dv_ref, own_ref, dq_ref, dh_ref, o_ref, even_ref, odd_ref, *scratch):
    acc_ref, main_ref, rest_ref, sems = scratch
    step = pl.program_id(0)

    @pl.when(step == 0)
    def _():
        acc_ref[...] = jnp.zeros_like(acc_ref)

    turned = n_ref[...].T
    acc_ref[1] += dot(turned, dk_ref[...])
    acc_ref[2] += dot(turned, dv_ref[...])

    @pl.when(step % 2 == 1)
    def _():
        acc_ref[0] += dot(own_ref[...].T, dq_ref[...])
        acc_ref[3] += dot(dh_ref[...].T, o_ref[...])

    @pl.when(step == GRAD_STEPS - 1)
    def _():
        lower = lower_lanes((D, TILE))
        for c in range(4):
            main_ref[c] = acc_ref[c, :, : 4 * TILE].astype(bf16)
        for group in range(4):
            entry = entry_of(place, group)
            for k in range(PARTS):
                part = (odd_ref if k % 2 else even_ref).at[k // 2, entry, pl.ds(0, 4)]
                source = main_ref.at[:, part_rows(place, k), pl.ds(group * TILE, TILE)]
                pltpu.make_async_copy(source, part, sems.at[0]).start()
        for two in range(2):
            lanes = slice((4 + two) * TILE, (5 + two) * TILE)
            for both in range(2):
                one = acc_ref[2 * both, :, lanes]
                other = pltpu.roll(acc_ref[2 * both + 1, :, lanes], DH, 1)
                rest_ref[2 * two, both] = jnp.where(lower, one, other).astype(bf16)
                rest_ref[2 * two + 1, both] = jnp.where(lower, other, one).astype(bf16)
        for group in range(4):
            entry = entry_of(place, group)
            for k in range(PARTS):
                part = (odd_ref if k % 2 else even_ref).at[k // 2, entry, pl.ds(4, 2)]
                source = rest_ref.at[group, :, part_rows(place, k)]
                pltpu.make_async_copy(source, part, sems.at[0]).start()
        wait_for(even_ref, sems.at[0])
        wait_for(odd_ref, sems.at[0])


def attn_grads(place, normed_window, dk, dv, normed_own, dq, dh, o):
    rows, few = dk.shape[0] // GRAD_STEPS, dq.shape[0] // (GRAD_STEPS // 2)
    wide = pl.BlockSpec((rows, D), lambda t: (t, 0))
    small = pl.BlockSpec((few, D), lambda t: (t // 2, 0))
    parts = jax.ShapeDtypeStruct((PARTS // 2, 4, 6, PART, TILE), bf16)
    return pl.pallas_call(
        attn_grads_kernel,
        grid=(GRAD_STEPS,),
        in_specs=[SMEM, wide, wide, wide, small, small, small, small],
        out_specs=[ANY] * 2,
        out_shape=[parts] * 2,
        scratch_shapes=[
            pltpu.VMEM((4, D, D), f32),
            pltpu.VMEM((4, D, 4 * TILE), bf16),
            pltpu.VMEM((4, 2, D, TILE), bf16),
            pltpu.SemaphoreType.DMA((1,)),
        ],
        compiler_params=pltpu.CompilerParams(vmem_limit_bytes=VMEM_GRANT),
        cost_estimate=cost(10),
        name="attn_grads",
    )(place, normed_window, dk, dv, normed_own, dq, dh, o)


def norm_grads_kernel(place, dk_ref, dv_ref, dq_ref, wk_ref, wv_ref, wq_ref, back_ref, own_ref, forth_ref, held_ref):
    own_rows = dq_ref.shape[1]
    held_ref[...] = dot(dk_ref[0], wk_ref[...], NT) + dot(dv_ref[0], wv_ref[...], NT)
    own_ref[0] = dot(dq_ref[0], wq_ref[...], NT)
    back_ref[...] = jnp.zeros_like(back_ref)
    forth_ref[...] = jnp.zeros_like(forth_ref)
    for block in range(2 * LEN // QB):
        row = block * QB - place[2]
        part = slice(block * QB, (block + 1) * QB)

        @pl.when(row < 0)
        def _():
            back_ref[0, pl.ds(pl.multiple_of(row + own_rows, QB), QB), :] = held_ref[part, :].astype(bf16)

        @pl.when((row >= 0) & (row < own_rows))
        def _():
            own_ref[0, pl.ds(pl.multiple_of(row, QB), QB), :] += held_ref[part, :]

        @pl.when((row >= own_rows) & (row < 2 * own_rows))
        def _():
            forth_ref[0, pl.ds(pl.multiple_of(row - own_rows, QB), QB), :] = held_ref[part, :].astype(bf16)


def norm_grads(place, dk, dv, dq, w_k, w_v, w_q):
    micro, own_rows, _ = dq.shape
    wide = pl.BlockSpec((1, 2 * LEN, D), lambda m: (m, 0, 0))
    small = pl.BlockSpec((1, own_rows, D), lambda m: (m, 0, 0))
    whole = pl.BlockSpec((D, D), lambda m: (0, 0))
    return pl.pallas_call(
        norm_grads_kernel,
        grid=(micro,),
        in_specs=[SMEM, wide, wide, small, whole, whole, whole],
        out_specs=[small] * 3,
        out_shape=[
            jax.ShapeDtypeStruct(dq.shape, bf16),
            jax.ShapeDtypeStruct(dq.shape, f32),
            jax.ShapeDtypeStruct(dq.shape, bf16),
        ],
        scratch_shapes=[pltpu.VMEM((2 * LEN, D), f32)],
        compiler_params=pltpu.CompilerParams(vmem_limit_bytes=VMEM_GRANT),
        cost_estimate=cost(10),
        name="norm_grads",
    )(place, dk, dv, dq, w_k, w_v, w_q)


def gelu_and_slope(gate):
    root = 0.7978845608028654
    cube = 0.044715
    square = gate * gate
    bend = jnp.tanh(root * gate * (1.0 + cube * square))
    half = 0.5 * (1.0 + bend)
    slope = half + 0.5 * gate * (1.0 - bend * bend) * (root * (1.0 + 3.0 * cube * square))
    return gate * half, slope


def ffn_kernel(place, o_ref, x_ref, dy_ref, wo_ref, gain_ref, all_w, *refs):
    out_ref, dy1_ref, dh1_ref = refs[:3]
    parts = (refs[3:5], refs[5:7])
    (w_ref, g_ref, y_ref, n_ref, nt_ref, dyt_ref, acc_ref, dn_ref, hid_ref, dgate_ref, dup_ref,
     out_held, dy1_held, dh1_held, w_sems, g_sems, out_sems) = refs[7:]
    width = w_ref.shape[2] // 3
    gate_cols, up_cols, down_cols = (slice(c * width, (c + 1) * width) for c in range(3))

    def load(entry):
        group = lax.rem(entry + place[1], 4)
        for k in range(PARTS):
            rows = pl.ds(k * PART, PART)
            pltpu.make_async_copy(all_w.at[k, group], w_ref.at[entry, rows], w_sems.at[entry]).start()

    load(0)
    y = x_ref[...].astype(f32) + dot(o_ref[...], wo_ref[...], NT)
    y_ref[...] = y
    rho = lax.rsqrt(jnp.mean(y * y, axis=-1, keepdims=True) + epsilon)
    normed = (y * rho * gain_ref[...]).astype(bf16)
    n_ref[...] = normed
    nt_ref[...] = normed.T
    dyt_ref[...] = dy_ref[...].T
    acc_ref[...] = y
    dn_ref[...] = jnp.zeros_like(dn_ref)
    for entry in range(1, 4):
        load(entry)

    def through(entry):
        wait_for(w_ref.at[entry], w_sems.at[entry])
        w = w_ref.at[entry]
        normed = n_ref[...]
        gate = dot(normed, w[:, gate_cols])
        up = dot(normed, w[:, up_cols])
        grad_hid = dot(dy_ref[...], w[:, down_cols])
        act, slope = gelu_and_slope(gate)
        hid = (act * up).astype(bf16)
        dgate = (grad_hid * up * slope).astype(bf16)
        dup = (grad_hid * act).astype(bf16)
        hid_ref[...] = hid
        dgate_ref[...] = dgate
        dup_ref[...] = dup
        acc_ref[...] += dot(hid, w[:, down_cols], NT)
        dn_ref[...] += dot(dgate, w[:, gate_cols], NT) + dot(dup, w[:, up_cols], NT)

    def grads(entry, slot, pair):
        g_ref[slot, :, gate_cols] = dot(nt_ref[...], dgate_ref[...]).astype(bf16)
        g_ref[slot, :, up_cols] = dot(nt_ref[...], dup_ref[...]).astype(bf16)
        g_ref[slot, :, down_cols] = dot(dyt_ref[...], hid_ref[...]).astype(bf16)
        for k in range(PARTS):
            part = parts[pair][k % 2].at[k // 2, slot]
            pltpu.make_async_copy(g_ref.at[slot, part_rows(place, k)], part, g_sems.at[slot]).start()

    def one_group(entry, _):
        through(entry)
        grads(entry, entry, 0)
        return 0

    lax.fori_loop(0, 2, one_group, 0)
    through(2)
    wait_for(g_ref.at[0], g_sems.at[0])
    grads(2, 0, 1)
    through(3)
    outs = [(out_held, out_ref), (dy1_held, dy1_ref), (dh1_held, dh1_ref)]
    out_held[...] = acc_ref[...].astype(bf16)
    scaled_y = y_ref[...]
    rho = lax.rsqrt(jnp.mean(scaled_y * scaled_y, axis=-1, keepdims=True) + epsilon)
    scaled_y = scaled_y * rho
    u = dn_ref[...] * gain_ref[...]
    inner = jnp.mean(u * scaled_y, axis=-1, keepdims=True)
    dy1 = dy_ref[...].astype(f32) + rho * (u - scaled_y * inner)
    dy1_held[...] = dy1
    dh1_held[...] = dy1.astype(bf16)
    copies = [pltpu.make_async_copy(held, ref, out_sems.at[j]) for j, (held, ref) in enumerate(outs)]
    for copy in copies:
        copy.start()
    wait_for(g_ref.at[1], g_sems.at[1])
    grads(3, 1, 1)
    for copy in copies:
        copy.wait()
    for slot in range(2):
        wait_for(g_ref.at[slot], g_sems.at[slot])


def ffn(place, attended, x, dy, w_o, gain, weights):
    tokens = x.shape[0]
    columns = weights.shape[3]
    wide = lambda dtype: jax.ShapeDtypeStruct((tokens, D), dtype)
    parts = jax.ShapeDtypeStruct((PARTS // 2, 2, PART, columns), bf16)
    scratch = lambda rows, width, dtype: pltpu.VMEM((rows, width), dtype)
    return pl.pallas_call(
        ffn_kernel,
        in_specs=[SMEM] + [VMEM] * 5 + [ANY],
        out_specs=[ANY] * 7,
        out_shape=[wide(bf16), wide(f32), wide(bf16)] + [parts] * 4,
        scratch_shapes=[
            pltpu.VMEM((4, D, columns), bf16),
            pltpu.VMEM((2, D, columns), bf16),
            scratch(tokens, D, f32),
            scratch(tokens, D, bf16),
            scratch(D, tokens, bf16),
            scratch(D, tokens, bf16),
            scratch(tokens, D, f32),
            scratch(tokens, D, f32),
            scratch(tokens, columns // 3, bf16),
            scratch(tokens, columns // 3, bf16),
            scratch(tokens, columns // 3, bf16),
            scratch(tokens, D, bf16),
            scratch(tokens, D, f32),
            scratch(tokens, D, bf16),
            pltpu.SemaphoreType.DMA((4,)),
            pltpu.SemaphoreType.DMA((2,)),
            pltpu.SemaphoreType.DMA((3,)),
        ],
        compiler_params=pltpu.CompilerParams(vmem_limit_bytes=VMEM_GRANT),
        cost_estimate=cost(32),
        name="ffn",
    )(place, attended, x, dy, w_o, gain, weights)


def grams_of(blocks):
    return jnp.einsum("our,ouw->orw", blocks, blocks, precision=HIGHEST)


def dot_three(a, b):
    parts = []
    for v in (a, b):
        high = v.astype(bf16)
        parts.append((high, (v - high.astype(f32)).astype(bf16)))
    (a_high, a_low), (b_high, b_low) = parts
    return dot(a_high, b_high) + (dot(a_high, b_low) + dot(a_low, b_high))


def muon_kernel(rates, gram_ref, mom_ref, in_ref, out_ref, in_next, out_next):
    width = mom_ref.shape[2]
    for c, rate in enumerate(rates):
        gram = gram_ref[c, :width]
        row = lax.broadcasted_iota(jnp.int32, gram.shape, 0)
        eye = (row == lax.broadcasted_iota(jnp.int32, gram.shape, 1)).astype(f32)
        whole = jnp.sum(jnp.sum(gram * eye, axis=0, keepdims=True), axis=1, keepdims=True)
        first = gram / whole
        start = mom_ref[c] * lax.rsqrt(whole)
        step = linear_coefficient * eye + coef_second * first + coef_third * dot_three(first, first)
        second = dot_three(dot_three(first, step), step)
        once = dot_three(start, step)
        turn = dot_three(once, second)
        both = rate * (linear_coefficient * once + coef_second * turn + coef_third * dot_three(turn, second))
        if c < len(rates) - 1:
            in_next[c] = in_ref[c] * (1.0 - rate * decay_rate) - both
        else:
            both = both if out_ref.shape == both.shape else both.T
            out_next[...] = out_ref[...] * (1.0 - rate * decay_rate) - both


def muon(rates, gram, moms, in_param, out_param):
    return pl.pallas_call(
        functools.partial(muon_kernel, rates),
        in_specs=[VMEM] * 4,
        out_specs=[VMEM] * 2,
        out_shape=[jax.ShapeDtypeStruct(in_param.shape, f32), jax.ShapeDtypeStruct(out_param.shape, f32)],
        compiler_params=pltpu.CompilerParams(vmem_limit_bytes=VMEM_GRANT),
        cost_estimate=cost(8),
        name="muon",
    )(gram, moms, in_param, out_param)


def attn_momentum_kernel(place, *refs):
    count = len(refs) - 9
    terms, (in_mom, out_mom, in_ref, extra_ref) = refs[:count], refs[count : count + 4]
    mom_in_ref, mom_out_ref, gram_ref, gain_ref, flat_ref = refs[count + 4 :]
    tiles = [sum(term[c].astype(f32) for term in terms) for c in range(6)]
    gain = 0.0
    for c in range(4):
        tail = tiles[4 + c // 2]
        other = pltpu.roll(tail, DH, 1)
        swapped = (place[1] + c) % 2 == 1
        tail = jnp.where(swapped, other, tail)[:, :DH]
        grad = jnp.concatenate([tiles[c], tail], axis=1)
        if c < 3:
            gain += jnp.sum(in_ref[c].astype(bf16).astype(f32) * grad, axis=1, keepdims=True)
            mom = momentum_decay * in_mom[c] + grad
            mom_in_ref[c] = mom
        else:
            mom = momentum_decay * out_mom[...].T + grad
            mom_out_ref[...] = mom.T
        flat_ref[c] = mom
        gram_ref[c, : mom.shape[1]] = lax.dot_general(mom, mom, TN, precision=HIGHEST, preferred_element_type=f32)
        gram_ref[c, mom.shape[1] :] = extra_ref[c]
    gain_ref[...] = gain


def attn_momentum(place, terms, in_mom, out_mom, attn_in, extra):
    _, rows, width = in_mom.shape
    operands = [*terms, in_mom, out_mom, attn_in, extra]
    shape = lambda *dims: jax.ShapeDtypeStruct(dims, f32)
    return pl.pallas_call(
        attn_momentum_kernel,
        in_specs=[SMEM] + [VMEM] * len(operands),
        out_specs=[VMEM] * 5,
        out_shape=[
            shape(3, rows, width),
            shape(width, rows),
            shape(4, width + extra.shape[1], width),
            shape(rows, 1),
            shape(4, rows, width),
        ],
        compiler_params=pltpu.CompilerParams(vmem_limit_bytes=VMEM_GRANT),
        cost_estimate=cost(4),
        name="attn_momentum",
    )(place, *operands)


def ffn_momentum_kernel(*refs):
    count = len(refs) - 8
    terms, (in_mom, out_mom, in_ref) = refs[:count], refs[count : count + 3]
    mom_in_ref, mom_out_ref, gram_ref, gain_ref, flat_ref = refs[count + 3 :]
    width = in_mom.shape[2]
    gain = 0.0
    for c in range(3):
        grad = sum(term[:, c * width : (c + 1) * width].astype(f32) for term in terms)
        if c < 2:
            gain += jnp.sum(in_ref[c].astype(bf16).astype(f32) * grad, axis=1, keepdims=True)
            mom = momentum_decay * in_mom[c] + grad
            mom_in_ref[c] = mom
        else:
            mom = momentum_decay * out_mom[...] + grad
            mom_out_ref[...] = mom
        flat_ref[c] = mom
        gram_ref[c] = lax.dot_general(mom, mom, TN, precision=HIGHEST, preferred_element_type=f32)
    gain_ref[...] = gain


def ffn_momentum(terms, in_mom, out_mom, ffn_in):
    _, rows, width = in_mom.shape
    operands = [*terms, in_mom, out_mom, ffn_in]
    shape = lambda *dims: jax.ShapeDtypeStruct(dims, f32)
    return pl.pallas_call(
        ffn_momentum_kernel,
        in_specs=[VMEM] * len(operands),
        out_specs=[VMEM] * 5,
        out_shape=[
            shape(2, rows, width),
            shape(rows, width),
            shape(3, width, width),
            shape(rows, 1),
            shape(3, rows, width),
        ],
        compiler_params=pltpu.CompilerParams(vmem_limit_bytes=VMEM_GRANT),
        cost_estimate=cost(5),
        name="ffn_momentum",
    )(*operands)


def adam_update(param, grad, first, second):
    first_new = beta_one * first + (1.0 - beta_one) * grad
    second_new = beta_two * second + (1.0 - beta_two) * grad * grad
    corrected_first = first_new / (1.0 - beta_one**STEP)
    corrected_second = second_new / (1.0 - beta_two**STEP)
    return (
        first_new,
        second_new,
        param - adam_rate * corrected_first / (jnp.sqrt(corrected_second) + adam_epsilon),
    )


def direct():
    return lax.axis_size("dp") == PARTS and lax.axis_size("mp") == 4


def swap(x, bit):
    return lax.ppermute(x, "dp", [(j, j ^ bit) for j in range(lax.axis_size("dp"))])


def from_above(x, k):
    return lax.ppermute(x, "mp", [((j + k) % 4, j) for j in range(4)])


def to_above(x, k):
    return lax.ppermute(x, "mp", [(j, (j + k) % 4) for j in range(4)])


def behind(x, *others):
    return lax.optimization_barrier((x, others))[0]


def total(*terms):
    return sum(term.astype(f32) for term in terms)


def gather_all(shard):
    rows, columns = shard.shape
    whole = lax.all_gather(shard, ("dp", "mp"), axis=0, tiled=False)
    if rows == PART:
        return whole.reshape(PARTS, 4, PART, columns)
    whole = whole.reshape(-1, 4, rows, columns).transpose(1, 0, 2, 3).reshape(4, PARTS, PART, columns)
    return whole.transpose(1, 0, 2, 3)


def gather_pieces(shard):
    tiles, rows, _ = shard.shape
    if not direct():
        whole = lax.all_gather(shard, ("dp", "mp"), axis=0, tiled=False)
        whole = whole.reshape(PARTS, -1, 4, tiles, rows, TILE).transpose(0, 2, 3, 1, 4, 5)
        return list(whole.reshape(PARTS, 4, tiles, PART, TILE))
    own = jnp.stack([shard] + [from_above(shard, k) for k in (1, 2, 3)])
    return own


def spread_pieces(own, meanwhile):
    if not direct():
        return own
    others = behind([swap(own, bit) for bit in (2, 4, 6)], meanwhile)
    return [piece for here in (own, *others) for piece in (here, swap(here, 1))]


def scatter_core(even, odd):
    return total(even, swap(odd, 1)).astype(bf16)


def send_plane(mine):
    return [swap(mine[1], 2), swap(mine[2], 4), swap(mine[3], 6)]


def send_line(line):
    return [to_above(line[k], k) for k in (1, 2, 3)]


def plain_order(even, odd):
    return jnp.stack([even, odd], axis=1).reshape((PARTS,) + even.shape[1:])


def scatter_plain(parts, rows):
    groups, columns = parts.shape[2], parts.shape[-1]
    parts = parts.reshape(PARTS, 4, groups, PART // rows, rows, columns).transpose(0, 3, 1, 2, 4, 5)
    parts = parts.reshape((-1,) + parts.shape[3:])
    return lax.psum_scatter(parts, ("dp", "mp"), scatter_dimension=0, tiled=False)


def gather_small(x, axis_name, axis):
    if not direct():
        return lax.all_gather(x, axis_name, axis=axis, tiled=True)
    here = lax.axis_index(axis_name)
    size = lax.axis_size(axis_name)
    bit = 1
    while bit < size:
        other = lax.ppermute(x, axis_name, [(j, j ^ bit) for j in range(size)])
        upper = (here & bit) != 0
        x = jnp.concatenate([jnp.where(upper, other, x), jnp.where(upper, x, other)], axis=axis)
        bit *= 2
    return x


def sum_line(x):
    if not direct():
        return lax.psum(x, "mp")
    return x + from_above(x, 1) + from_above(x, 2) + from_above(x, 3)


def to_low(x):
    return x.astype(bf16)


def split_core(x):
    odd = (lax.axis_index("dp") & 1) != 0
    return jnp.where(odd, x[2:], x[:2]), to_low(jnp.where(odd, x[:2], x[2:]))


def sum_core(mine, other, meanwhile):
    return total(mine, behind(swap(other, 1), meanwhile))


def sum_first(pair, meanwhile):
    others = behind((swap(to_low(pair[0]), 2), swap(to_low(pair[1]), 4)), meanwhile)
    return total(pair[0], others[0]), total(pair[1], others[1])


def sum_second(pair, meanwhile):
    others = behind((swap(to_low(pair[0]), 4), swap(to_low(pair[1]), 2)), meanwhile)
    return total(pair[0], others[0]), total(pair[1], others[1])


def sum_last(pair, meanwhile):
    odd = (lax.axis_index("dp") & 1) != 0
    mine = to_low(jnp.stack(pair))
    other = behind(swap(mine, 1), meanwhile)
    return jnp.concatenate([jnp.where(odd, other, mine), jnp.where(odd, mine, other)]).astype(f32)


def shards(
    tokens, lengths, cotangent, attn_in, attn_out, ffn_in, ffn_out, gains, table,
    attn_in_mom, attn_out_mom, ffn_in_mom, ffn_out_mom,
    gain_first, gain_second, table_first, table_second,
):
    micro, own_rows, _ = tokens.shape
    here = lax.axis_index("mp")
    n_mp = lax.axis_size("mp")
    width = attn_in.shape[2]
    heads_dev = table.shape[1]

    rows_dev = attn_in.shape[1]
    width_ffn = ffn_in.shape[2]
    index = jnp.stack([lax.axis_index("dp"), here]).astype(jnp.int32)
    place = index if direct() else jnp.zeros_like(index)
    odd_group = (here & 1) != 0

    ffn_low = jnp.concatenate([ffn_in[0], ffn_in[1], ffn_out.T], axis=1).astype(bf16)
    attn_low = [part.astype(bf16) for part in (attn_in[0], attn_in[1], attn_in[2], attn_out.T)]
    tails = [part[:, TILE:] for part in attn_low]
    beside = lambda one, two: jnp.where(
        odd_group, jnp.concatenate([two, one], axis=1), jnp.concatenate([one, two], axis=1)
    )
    attn_tiles = jnp.stack([part[:, :TILE] for part in attn_low] + [beside(*tails[:2]), beside(*tails[2:])])
    gain_low = gather_small(gains.astype(bf16), "dp", 1).astype(f32)
    table_all = gather_small(table, "mp", 1)[:, np.array(HEAD_ORDER)]
    onehot = skew_onehot()
    line = lax.dot_general(
        table_all, onehot, (((0,), (1,)), ((), ())), precision=HIGHEST, preferred_element_type=f32
    ).reshape(PAIRS, 2, SKEW)
    ffn_all = gather_all(ffn_low)
    attn_own = gather_pieces(attn_tiles)
    halo = behind(tokens, attn_own)
    up, down = [(j, j + 1) for j in range(n_mp - 1)], [(j + 1, j) for j in range(n_mp - 1)]
    sides = (lax.ppermute(halo, "mp", up), lax.ppermute(halo, "mp", down))
    bias = make_bias(behind(line, attn_own))
    attn_pieces = spread_pieces(attn_own, (bias, gain_low, sides))

    first_row = own_rows * here
    first_doc = first_row // LEN
    inset = first_row - first_doc * LEN
    block_place = first_row // QB + jnp.arange(own_rows // QB, dtype=jnp.int32)
    slot = block_place // (LEN // QB) - first_doc
    lens_window = lax.dynamic_slice_in_dim(
        jnp.concatenate([lengths, jnp.ones((micro, 1), lengths.dtype)], axis=1), first_doc, 2, axis=1
    )
    meta = jnp.concatenate([slot, block_place % (LEN // QB), lens_window.reshape(-1)]).astype(jnp.int32)

    there = jnp.concatenate([place, inset[None].astype(jnp.int32)])
    projected, (w_q, w_k, w_v, w_o) = project(there, sides, tokens, gain_low[0:1], attn_pieces)
    q, k, v, normed_window, normed_own = projected
    attended, stats = attend(meta, q, k, v, bias)
    out_seq = attended
    attended = attended.reshape(micro * own_rows, D)
    normed_window = normed_window.reshape(micro * 2 * LEN, D)
    normed_own = normed_own.reshape(micro * own_rows, D)

    dy = cotangent.reshape(micro * own_rows, D)
    output, grad_middle, grad_mid_low, even_one, odd_one, even_two, odd_two = ffn(
        place, attended, tokens.reshape(micro * own_rows, D), dy, w_o, gain_low[1:2], ffn_all
    )
    grad_att = dot(grad_mid_low, w_o).astype(bf16).reshape(micro, own_rows, D)
    back_args = (meta, q, k, v, grad_att, out_seq, stats, bias)
    if direct():
        mine_one, core_two = scatter_core(even_one, odd_one), swap(odd_two, 1)
        plane_one = send_plane(mine_one)
        grads = attend_back(*back_args, [mine_one])
        mine_two = total(even_two, behind(core_two, grads)).astype(bf16)
        line_one = total(mine_one[0], *behind(plane_one, grads)).astype(bf16)
        plane_two = send_plane(behind(mine_two, line_one))
        grads = behind(grads, line_one)
    else:
        even_ffn = jnp.concatenate([even_one, even_two], axis=1)
        odd_ffn = jnp.concatenate([odd_one, odd_two], axis=1)
        shard_ffn = scatter_plain(plain_order(even_ffn, odd_ffn)[:, :, None], rows_dev)[0].astype(f32)
        grads = attend_back(*back_args)
    grad_q, grad_k, grad_v, grad_bias = grads
    grad_q = grad_q.reshape(micro * own_rows, D)
    grad_k = grad_k.reshape(micro * 2 * LEN, D)
    grad_v = grad_v.reshape(micro * 2 * LEN, D)
    even, odd = attn_grads(
        place, normed_window, grad_k, grad_v, normed_own, grad_q, grad_mid_low, attended
    )
    if direct():
        diag = diagonals(behind(grad_bias, even))
        line_two = total(mine_two[0], *behind(plane_two, diag)).astype(bf16)
        mine_attn = scatter_core(even, behind(odd, line_two))
        plane_attn = send_plane(mine_attn)
        sent_ffn = [to_above(line_one[1], 1), to_above(line_two[0], 2), to_above(line_two[1], 3)]
        grad_q, grad_k, grad_v = behind((grad_q, grad_k, grad_v), mine_attn)
    else:
        diag = diagonals(grad_bias)
    back, own_part, forth = norm_grads(
        there,
        grad_k.reshape(micro, 2 * LEN, D),
        grad_v.reshape(micro, 2 * LEN, D),
        grad_q.reshape(micro, own_rows, D),
        w_k,
        w_v,
        w_q,
    )
    own_part = own_part.reshape(micro * own_rows, D)
    table_sum = lax.dot_general(
        onehot,
        diag.reshape(H, SKEW),
        (((0,), (1,)), ((), ())),
        precision=HIGHEST,
        preferred_element_type=f32,
    )
    low = lambda v: v.astype(bf16).astype(f32)
    extra = jnp.pad(table_sum.reshape(4, 1, -1), ((0, 0), (0, 15), (0, width - BUCKETS * H // 4)))
    if direct():
        line_attn = total(mine_attn[0], *behind(plane_attn, (extra, back, forth, own_part))).astype(bf16)
        sent_ffn = behind(sent_ffn, line_attn)
        line_attn = behind(line_attn, sent_ffn)
        terms = [line_one[0], *sent_ffn]
    else:
        terms = [shard_ffn]
    mom_fin, mom_fout, gram_ffn, gain_ffn, blocks_ffn = ffn_momentum(terms, ffn_in_mom, ffn_out_mom.T, ffn_in)
    flat_ffn = gram_ffn.reshape(4, -1, width_ffn)
    if direct():
        split_ffn = split_core(flat_ffn)
        core_ffn = sum_core(*split_ffn, ())
        terms = [line_attn[0], *behind(send_line(line_attn), gram_ffn)]
    else:
        terms = [scatter_plain(plain_order(even, odd), rows_dev)]
    mom_in, mom_out, gram_attn, gain_attn, blocks_attn = attn_momentum(
        index, terms, attn_in_mom, attn_out_mom, attn_in, extra
    )
    fin_blocks = lambda gram: muon(
        [rate_ffn_in] * 2 + [rate_ffn_out],
        gram.reshape(3, width_ffn, width_ffn),
        blocks_ffn,
        ffn_in,
        ffn_out.T,
    )
    if direct():
        mine, other = split_core(gram_attn)
        first_ffn = sum_first(core_ffn, mine)
        second_ffn = sum_second(first_ffn, ())
        core_attn = sum_core(mine, other, second_ffn)
        ffn_in_next, ffn_out_next = fin_blocks(sum_last(second_ffn, core_attn))
        back, forth = behind((back, forth), core_attn)
        back, forth = lax.ppermute(back, "mp", down), lax.ppermute(forth, "mp", up)
        first_attn = sum_first(core_attn, (ffn_in_next, back, forth))
        second_attn = sum_second(first_attn, ())
    else:
        second_attn = ()
        back, forth = lax.ppermute(back, "mp", down), lax.ppermute(forth, "mp", up)
        ffn_in_next, ffn_out_next = fin_blocks(lax.psum(flat_ffn, "dp"))
        summed = lax.psum(gram_attn, "dp")
    own_part, back, forth = behind((own_part, back, forth), second_attn)
    grad_normed = own_part + (back.astype(f32) + forth.astype(f32)).reshape(micro * own_rows, D)
    rows = tokens.reshape(micro * own_rows, D).astype(f32)
    rho = lax.rsqrt(jnp.mean(rows * rows, axis=-1, keepdims=True) + epsilon)
    u = grad_normed * gain_low[0]
    tokens_grad = grad_middle + rho * (u - rows * rho * rho * jnp.mean(u * rows, axis=-1, keepdims=True))
    if direct():
        summed = sum_last(second_attn, tokens_grad)
    table_sum = summed[:, width, : BUCKETS * H // 4]
    gain_terms = jnp.stack([gain_attn[:, 0], gain_ffn[:, 0]])
    small = jnp.concatenate([gain_terms.reshape(-1), table_sum.reshape(-1)])
    small = sum_line(jnp.pad(small, (0, -small.size % 1024)).reshape(-1, 128)).reshape(-1)
    gain_grad = small[: gain_terms.size].reshape(gain_terms.shape) / low(gains)
    table_sum = small[gain_terms.size : gain_terms.size + BUCKETS * H].reshape(BUCKETS, H)
    table_sum = table_sum[:, np.argsort(np.array(HEAD_ORDER))]
    table_grad = lax.dynamic_slice_in_dim(table_sum, here * heads_dev, heads_dev, axis=1)
    attn_in_next, attn_out_next = muon(
        [rate_attn_in] * 3 + [rate_attn_out], summed, blocks_attn, attn_in, attn_out
    )
    gain_first_next, gain_second_next, gains_next = adam_update(gains, gain_grad, gain_first, gain_second)
    table_first_next, table_second_next, table_next = adam_update(table, table_grad, table_first, table_second)
    return (
        output.reshape(tokens.shape),
        tokens_grad.reshape(tokens.shape),
        attn_in_next,
        attn_out_next,
        ffn_in_next,
        ffn_out_next.T,
        mom_in,
        mom_out,
        mom_fin,
        mom_fout.T,
        gain_first_next,
        gain_second_next,
        gains_next,
        table_first_next,
        table_second_next,
        table_next,
    )


def solution(mesh):
    token = P(None, ("dp", "mp"), None)
    columns = P(None, "dp", "mp")
    flipped = P("mp", "dp")
    gain = P(None, "dp")
    head = P(None, "mp")
    return jax.shard_map(
        shards,
        mesh=mesh,
        in_specs=(
            token, P(None, "dp"), token, columns, flipped, columns, flipped, gain, head,
            columns, flipped, columns, flipped, gain, gain, head, head,
        ),
        out_specs=(
            token, token, columns, flipped, columns, flipped, columns, flipped, columns, flipped,
            gain, gain, gain, head, head, head,
        ),
        check_vma=False,
    )
```
